32 devices in a mesh: dp: 8 (over z, x), fsdp: 4 (over y, core).
Axes of the slice: x: 2, y: 2, z: 4, core: 2. Of those that a mesh axis runs over, the one named last changes fastest.
Arguments:
- features: bfloat16 [64, 4, 256, 128], P(('dp', 'fsdp')), may hold values from -6 to 6
- view_count: int32 [64], P(('dp', 'fsdp')), may hold values from 2 to 4
- plane_offsets: int32 [64, 4, 128], P(('dp', 'fsdp')), may hold values from 0 to 15
- depth_grad: float32 [64, 4, 256], P(('dp', 'fsdp')), may hold values from -6 to 6
- gain_self: bfloat16 [128], P('fsdp'), may hold values from 0.5 to 1.5
- self_qkv: bfloat16 [128, 384], P('fsdp'), may hold values from -0.5 to 0.5
- self_out: bfloat16 [128, 128], P('fsdp'), may hold values from -1.5 to 1.5
- gain_cross: bfloat16 [128], P('fsdp'), may hold values from 0.5 to 1.5
- cross_qkv: bfloat16 [128, 384], P('fsdp'), may hold values from -0.5 to 0.5
- cross_out: bfloat16 [128, 128], P('fsdp'), may hold values from -1.5 to 1.5
- gain_ff: bfloat16 [128], P('fsdp'), may hold values from 0.5 to 1.5
- ff_in: bfloat16 [128, 512], P('fsdp'), may hold values from -0.5 to 0.5
- ff_out: bfloat16 [512, 128], P('fsdp'), may hold values from -0.25 to 0.25
- refine: bfloat16 [128, 1152], P('fsdp'), may hold values from -0.1875 to 0.1875
Outputs:
- depth: float32 [64, 4, 256], P(('dp', 'fsdp'))
- features_grad: float32 [64, 4, 256, 128], P(('dp', 'fsdp'))
- gain_self_grad: float32 [128], P('fsdp')
- self_qkv_grad: float32 [128, 384], P('fsdp')
- self_out_grad: float32 [128, 128], P('fsdp')
- gain_cross_grad: float32 [128], P('fsdp')
- cross_qkv_grad: float32 [128, 384], P('fsdp')
- cross_out_grad: float32 [128, 128], P('fsdp')
- gain_ff_grad: float32 [128], P('fsdp')
- ff_in_grad: float32 [128, 512], P('fsdp')
- ff_out_grad: float32 [512, 128], P('fsdp')
- refine_grad: float32 [128, 1152], P('fsdp')
The draws below stay inside these ranges and needn't reach their ends.
Inputs may be any that keep to these rules, and one draw needn't show every extreme that they name: Views of a scene from view_count on are padding.
All inputs are finite; a program needn't handle non-finite values.
Results may differ from the reference program's by a relative error of at most 0.03.
The reference program's roundings to bfloat16 on the way count: a program that leaves them out, or rounds other values in their place, can miss the bound.
Values may be sent and summed in bfloat16 or wider, within the bound.
No kernel may reach another device: no remote copies, remote signals or barrier semaphores. Data moves between devices by JAX's collectives and lax.ppermute only.
A program may use at most 128 MiB of HBM per device.

```python
import jax
import jax.numpy as jnp
from jax import lax

C = 128
FFH = 512
PLANES = 128
WIN = 8
VIEWS = 4
HV = 16
SCENES = 64


def plant(result, rng, low, top_value):
    index_at = [jax.random.randint(jax.random.fold_in(rng, axis), (), 0, length) for axis, length in enumerate(result.shape)]
    longest = result.shape.index(max(result.shape))
    beside = index_at[:longest] + [(index_at[longest] + 1) % result.shape[longest]] + index_at[longest + 1:]
    return result.at[tuple(index_at)].set(low).at[tuple(beside)].set(top_value)


def level_of(own_key, dims, shards, smallest, largest):
    def one(axis_at, shards_of):
        heights = jax.random.uniform(jax.random.fold_in(jax.random.fold_in(own_key, 6), axis_at), (shards_of,), jnp.float32, smallest / len(shards), largest / len(shards))
        return jnp.repeat(jnp.exp(heights), dims[axis_at] // shards_of).reshape((-1,) + (1,) * (len(dims) - axis_at - 1))

    factor_of = one(*shards[0])
    for cut in shards[1:]:
        factor_of = factor_of * one(*cut)
    return factor_of


def bell_draw(rng, shape, scale, bound, split=(), kind=jnp.bfloat16):
    loudness = level_of(rng, shape, split, -0.22, 0.18) if split else 1.0
    array = jax.random.normal(rng, shape, jnp.float32) * scale * loudness
    return jnp.minimum(jnp.maximum(array, -bound), bound).astype(kind)


def setup_inputs(seed: int = 0) -> dict:
    seeds = jax.random.split(jax.random.key(seed), 15)
    return {
        "features": bell_draw(seeds[0], (SCENES, VIEWS, HV * HV, C), 1.0, 6.0, ((0, 32),)),
        "view_count": plant(jax.random.randint(seeds[1], (SCENES,), 2, VIEWS + 1), jax.random.fold_in(seeds[1], 1), 2, VIEWS).astype(jnp.int32),
        "plane_offsets": plant(jax.random.randint(seeds[2], (SCENES, VIEWS, PLANES), 0, HV), jax.random.fold_in(seeds[2], 1), 0, HV - 1).astype(jnp.int32),
        "depth_grad": bell_draw(seeds[3], (SCENES, VIEWS, HV * HV), 1.0, 6.0, ((0, 32),), jnp.float32),
        "gain_self": jnp.clip(1.0 + 0.1 * jax.random.normal(seeds[4], (C,), jnp.float32), 0.5, 1.5).astype(jnp.bfloat16),
        "self_qkv": bell_draw(seeds[5], (C, 3 * C), C ** -0.5, 0.5, ((0, 4),)),
        "self_out": bell_draw(seeds[6], (C, C), (C // 8) ** -0.5, 1.5, ((0, 4),)),
        "gain_cross": jnp.clip(1.0 + 0.1 * jax.random.normal(seeds[7], (C,), jnp.float32), 0.5, 1.5).astype(jnp.bfloat16),
        "cross_qkv": bell_draw(seeds[8], (C, 3 * C), C ** -0.5, 0.5, ((0, 4),)),
        "cross_out": bell_draw(seeds[9], (C, C), (C // 8) ** -0.5, 1.5, ((0, 4),)),
        "gain_ff": jnp.clip(1.0 + 0.1 * jax.random.normal(seeds[10], (C,), jnp.float32), 0.5, 1.5).astype(jnp.bfloat16),
        "ff_in": bell_draw(seeds[11], (C, FFH), C ** -0.5, 0.5, ((0, 4),)),
        "ff_out": bell_draw(seeds[12], (FFH, C), FFH ** -0.5, 0.25, ((0, 4),)),
        "refine": bell_draw(seeds[13], (PLANES, 9 * PLANES), (9 * PLANES) ** -0.5, 0.1875, ((0, 4),)),
    }


@jax.custom_vjp
def low(v):
    return lax.optimization_barrier(v.astype(jnp.bfloat16)).astype(jnp.float32)

@jax.custom_vjp
def low_back(v):
    return v

def low_keep(v):
    return (low(v), None)

def low_pass(kept, grad):
    return (grad,)

def back_keep(v):
    return (v, None)

def back_low(kept, grad):
    return (low(grad),)
low.defvjp(low_keep, low_pass)
low_back.defvjp(back_keep, back_low)
HIGH = lax.Precision.HIGHEST
MASKED = -1e+30
SELF_FORMS = ('vwqc,vwkc->vwqk', 'vwqk,vwkc->vwqc')
CROSS_FORMS = ('vwqc,uwkc->wvquk', 'wvquk,uwkc->vwqc')

def product(form, left, right):
    return jnp.einsum(form, left, right, precision=HIGH)

def layer_norm(value, gain):
    centred = value - lax.optimization_barrier(jnp.mean(value, -1, keepdims=True))
    spread = lax.optimization_barrier(jnp.mean(centred * centred, -1, keepdims=True))
    return centred * lax.rsqrt(spread + 1e-05) * gain

def to_windows(rows):
    views, width = (rows.shape[0], rows.shape[-1])
    side = HV // WIN
    grid = rows.reshape(views, side, WIN, side, WIN, width).transpose(0, 1, 3, 2, 4, 5)
    return grid.reshape(views, side * side, WIN * WIN, width)

def to_rows(tiles):
    views, width = (tiles.shape[0], tiles.shape[-1])
    side = HV // WIN
    grid = tiles.reshape(views, side, side, WIN, WIN, width).transpose(0, 1, 3, 2, 4, 5)
    return grid.reshape(views, HV, HV, width)

def attend(hidden, gain, w_qkv, w_out, forms, axes, allowed):
    width = hidden.shape[-1]
    normed = low(layer_norm(hidden, gain))
    packed = low(low_back(product('vwtc,cd->vwtd', normed, w_qkv)))
    query = packed[..., :width]
    keys = packed[..., width:2 * width]
    values = packed[..., 2 * width:]
    scores = low_back(product(forms[0], query, keys)) * width ** (-0.5)
    scores = jnp.where(allowed, scores, MASKED)
    probs = low(jax.nn.softmax(scores, axis=axes))
    mixed = low(low_back(product(forms[1], probs, values)))
    return hidden + low_back(product('vwtc,cd->vwtd', mixed, w_out))

def feed(hidden, gain, w_in, w_out):
    normed = low(layer_norm(hidden, gain))
    inner = low_back(product('vwtc,cd->vwtd', normed, w_in))
    active = low(jax.nn.gelu(inner, approximate=False))
    return hidden + low_back(product('vwtc,cd->vwtd', active, w_out))

def convolve(w_refine, cost_low):
    planes = cost_low.shape[1]
    kernel = w_refine.reshape(planes, 9, planes)
    padded = jnp.pad(cost_low, ((0, 0), (0, 0), (1, 1), (1, 1)))
    total = jnp.zeros(cost_low.shape, jnp.float32)
    for tap in range(9):
        row_step, col_step = (tap // 3, tap % 3)
        window = padded[:, :, row_step:row_step + HV, col_step:col_step + HV]
        total = total + product('de,veyx->vdyx', kernel[:, tap], window)
    return total

def depth_head(tiles, count, offsets, w_refine):
    views, width = (tiles.shape[0], tiles.shape[-1])
    planes = offsets.shape[1]
    rows = low(to_rows(tiles))
    order = jnp.arange(views, dtype=jnp.int32)
    partner = jnp.where(order < count, (order + 1) % count, 0).astype(jnp.int32)
    across = jnp.take(rows, partner, axis=0)
    corr = low_back(product('vyxc,vykc->vyxk', rows, across))
    place = jnp.arange(HV, dtype=jnp.int32)
    select = (place[None, None, None, :] == place[None, None, :, None] - offsets[:, :, None, None]).astype(jnp.float32)
    cost = product('vyxk,vdxk->vdyx', corr, select) * (0.5 * width ** (-0.5))
    refined = cost + low_back(convolve(w_refine, low(cost)))
    refined = refined.reshape(views, planes, HV * HV)
    probs = jax.nn.softmax(refined, axis=1)
    depth_values = 1.0 + 3.0 * jnp.arange(planes, dtype=jnp.float32) / (planes - 1)
    valid = (order < count).astype(jnp.float32)
    return lax.optimization_barrier(jnp.sum(probs * depth_values[None, :, None], axis=1)) * valid[:, None]

def scene(tiles, count, offsets, weights):
    gain_a, w_sq, w_so, gain_b, w_cq, w_co, gain_c, w_fi, w_fo, w_ref = weights
    order = jnp.arange(tiles.shape[0], dtype=jnp.int32)
    allowed = ((order[None, :] < count) & (order[None, :] != order[:, None]))[None, :, None, :, None]
    first = attend(tiles, gain_a, w_sq, w_so, SELF_FORMS, 3, True)
    second = attend(first, gain_b, w_cq, w_co, CROSS_FORMS, (3, 4), allowed)
    third = feed(second, gain_c, w_fi, w_fo)
    return depth_head(third, count, offsets, w_ref)

def reference(features, view_count, plane_offsets, depth_grad, gain_self, self_qkv, self_out, gain_cross, cross_qkv, cross_out, gain_ff, ff_in, ff_out, refine):
    weights = tuple((piece.astype(jnp.float32) for piece in (gain_self, self_qkv, self_out, gain_cross, cross_qkv, cross_out, gain_ff, ff_in, ff_out, refine)))

    def visit(totals, item):
        rows, count, offsets, cotangent = item
        tiles = to_windows(rows.astype(jnp.float32))
        depth, pull = jax.vjp(lambda held, params: scene(held, count, offsets, params), tiles, weights)
        d_tiles, d_weights = pull(cotangent)
        totals = jax.tree.map(lambda left, right: left + right, totals, d_weights)
        grad_rows = to_rows(d_tiles).reshape(rows.shape)
        return (totals, (depth, grad_rows))
    start = tuple((jnp.zeros_like(piece) for piece in weights))
    totals, (depth, grad_features) = lax.scan(visit, start, (features, view_count, plane_offsets, depth_grad))
    return (depth, grad_features, totals[0], totals[1], totals[2], totals[3], totals[4], totals[5], totals[6], totals[7], totals[8], totals[9])
```

```python
import functools

import jax
import jax.numpy as jnp
from jax import lax
from jax.experimental import pallas as pl
from jax.experimental.pallas import tpu as pltpu
from jax.sharding import PartitionSpec as P

C = 128
FFH = 512
PLANES = 128
WIN = 8
VIEWS = 4
HV = 16
PIX = HV * HV
TOK = VIEWS * WIN * WIN
HALF = PIX // 2
PAD_ROWS = 16
MASKED = -1e30
SCALE = C**-0.5
LOG2E = 1.4426950408889634
F32 = jnp.float32
BF16 = jnp.bfloat16
BLOCKS = (3, 1, 3, 1, 4, 4, 9)
VMEM_LIMIT = 60 * 1024 * 1024

ERF_P = 0.39
ERF_C = (0.23532522, 0.09138841, 0.6495594, -0.63540028, 0.88666437, -0.22753713)


def mm(left, right):
    return lax.dot_general(left, right, (((1,), (0,)), ((), ())), preferred_element_type=F32)


def mm_nt(left, right):
    return lax.dot_general(left, right, (((1,), (1,)), ((), ())), preferred_element_type=F32)


def mm_tn(left, right):
    return lax.dot_general(left, right, (((0,), (0,)), ((), ())), preferred_element_type=F32)


def norm_forward(value, gain):
    centred = value - jnp.mean(value, -1, keepdims=True)
    spread = jnp.mean(centred * centred, -1, keepdims=True)
    rstd = lax.rsqrt(spread + 1e-05)
    xhat = centred * rstd
    return xhat, jnp.broadcast_to(rstd, value.shape), (xhat * gain).astype(BF16)


def norm_backward(d_normed, xhat, rstd, gain):
    d_xhat = d_normed * gain
    mean_d = jnp.mean(d_xhat, -1, keepdims=True)
    mean_dx = jnp.mean(d_xhat * xhat, -1, keepdims=True)
    d_gain = jnp.sum((d_normed * xhat).reshape(-1, 8, C), 0)
    return rstd * (d_xhat - mean_d - xhat * mean_dx), d_gain


def split_two(value):
    high = value.astype(BF16)
    return jnp.concatenate([high, (value - high.astype(F32)).astype(BF16)], -1)


def iota(shape, axis):
    return lax.broadcasted_iota(jnp.int32, shape, axis)


def fsdp_bits(parts):
    return parts.bit_length() - 1


def pack_kernel(parts, index_ref, *refs):
    out = refs[-1]
    rows = C // parts
    at = 0
    for ref, blocks in zip(refs[3:10], BLOCKS):
        if ref.shape[0] == blocks * rows and ref.shape[1] == C:
            out[at : at + blocks * rows, :] = ref[...]
        else:
            for block in range(blocks):
                out[at + block * rows : at + (block + 1) * rows, :] = ref[:, block * C : (block + 1) * C]
        at += blocks * rows
    lane = iota((rows, C), 1)
    place = (lane == iota((rows, C), 0) + index_ref[0] * rows).astype(BF16)
    line = iota((PAD_ROWS, C), 0)
    gains = jnp.zeros((PAD_ROWS, C), F32)
    for which in range(3):
        row = mm(jnp.broadcast_to(refs[which][...], (8, rows)), place)[:1]
        gains = jnp.where(line == which, row, gains)
    out[at : at + PAD_ROWS, :] = gains.astype(BF16)


def unpack_kernel(parts, index_ref, left, right, *outs):
    rows = C // parts
    at = 0
    for out, blocks in zip(outs[3:10], BLOCKS):
        total = left[at : at + blocks * rows, :].astype(F32) + right[at : at + blocks * rows, :].astype(F32)
        if out.shape[0] == blocks * rows and out.shape[1] == C:
            out[...] = total
        else:
            for block in range(blocks):
                out[:, block * C : (block + 1) * C] = total[block * rows : (block + 1) * rows]
        at += blocks * rows
    gains = left[at : at + PAD_ROWS, :].astype(F32) + right[at : at + PAD_ROWS, :].astype(F32)
    lane = iota((C, rows), 0)
    place = (lane == iota((C, rows), 1) + index_ref[0] * rows).astype(F32)
    picked = lax.dot_general(
        gains, place, (((1,), (0,)), ((), ())), precision=lax.Precision.HIGHEST, preferred_element_type=F32
    )
    for which in range(3):
        outs[which][...] = picked[which : which + 1]


def main_kernel(
    scenes,
    parts,
    count_ref,
    index_ref,
    features,
    offsets,
    depth_grad,
    packed,
    depth_out,
    grad_out,
    grads_out,
    w_sq, w_so, w_cq, w_co, w_fi, w_fo, w_rf,
    t_sq, t_so, t_cq, t_co, t_fi, t_fo, t_rf,
    gains,
    bias,
    x0s,
    xh_a, xh_b, xh_c, rs_a, rs_b, rs_c,
    no_a, no_b, no_c,
    qkv_a, qkv_b, p_a, p_b, o_a, o_b,
    gd, act,
    x3s, d3s,
    low, rev,
    pads, taps, back_taps,
    g_sq, g_so, g_cq, g_co, g_fi, g_fo, g_rf, g_gain,
):
    rows = C // parts
    halves = HV // WIN

    at = 0
    for ref, blocks in zip((w_sq, w_so, w_cq, w_co, w_fi, w_fo, w_rf), BLOCKS):
        for shard in range(parts):
            if ref is w_fo:
                ref[shard * blocks * rows : (shard + 1) * blocks * rows, :] = packed[shard, at : at + blocks * rows, :]
            else:
                for block in range(blocks):
                    ref[shard * rows : (shard + 1) * rows, block * C : (block + 1) * C] = packed[
                        shard, at + block * rows : at + (block + 1) * rows, :
                    ]
        at += blocks * rows
    total = packed[0, at : at + PAD_ROWS, :].astype(F32)
    for shard in range(1, parts):
        total = total + packed[shard, at : at + PAD_ROWS, :].astype(F32)
    gains[...] = total[:8]
    for source, target in ((w_sq, t_sq), (w_so, t_so), (w_cq, t_cq), (w_co, t_co), (w_fi, t_fi), (w_rf, t_rf)):
        for block in range(source.shape[1] // C):
            target[block * C : (block + 1) * C, :] = source[:, block * C : (block + 1) * C].T
    for block in range(FFH // C):
        t_fo[:, block * C : (block + 1) * C] = w_fo[block * C : (block + 1) * C, :].T

    for ref in (g_sq, g_so, g_cq, g_co, g_fi, g_fo, g_rf, g_gain, pads):
        ref[...] = jnp.zeros_like(ref)
    for ref in (taps, back_taps):
        ref[:, :HV, :] = jnp.zeros((VIEWS, HV, 3 * C), BF16)
        ref[:, HV + PIX :, :] = jnp.zeros((VIEWS, HV, 3 * C), BF16)

    gain_a = gains[0:1, :]
    gain_b = gains[1:2, :]
    gain_c = gains[2:3, :]

    def forward(step, carry):
        scene = step // halves
        half = step % halves

        @pl.when(half == 0)
        def _():
            live = count_ref[scene]
            of_key = iota((TOK, TOK), 1) // (WIN * WIN)
            of_query = iota((TOK, TOK), 0) // (WIN * WIN)
            bias[...] = jnp.where((of_key < live) & (of_key != of_query), 0.0, MASKED)

        piece = features[scene, :, pl.ds(pl.multiple_of(half * HALF, HALF), HALF), :]
        x0s[...] = piece.astype(F32).reshape(VIEWS, WIN, 2, WIN, C)
        for side in range(2):
            spot = pl.ds(side * TOK, TOK)
            x0 = x0s[:, :, side].reshape(TOK, C)
            xhat, rstd, normed = norm_forward(x0, gain_a)
            xh_a[step, spot, :] = xhat
            rs_a[step, spot, :] = rstd
            no_a[step, spot, :] = normed
            qkv = mm(normed, w_sq[...]).astype(BF16)
            qkv_a[step, spot, :] = qkv
            mixed = []
            for view in range(VIEWS):
                lines = slice(view * WIN * WIN, (view + 1) * WIN * WIN)
                scores = mm_nt(qkv[lines, :C], qkv[lines, C : 2 * C]) * (SCALE * LOG2E)
                expo = jnp.exp2(scores - jnp.max(scores, -1, keepdims=True))
                probs = (expo * (1.0 / jnp.sum(expo, -1, keepdims=True))).astype(BF16)
                p_a[step, pl.ds(side * TOK + view * WIN * WIN, WIN * WIN), :] = probs
                mixed.append(mm(probs, qkv[lines, 2 * C :]))
            mixed = jnp.concatenate(mixed, 0).astype(BF16)
            o_a[step, spot, :] = mixed
            x1 = x0 + mm(mixed, w_so[...])
            xhat, rstd, normed = norm_forward(x1, gain_b)
            xh_b[step, spot, :] = xhat
            rs_b[step, spot, :] = rstd
            no_b[step, spot, :] = normed
            qkv = mm(normed, w_cq[...]).astype(BF16)
            qkv_b[step, spot, :] = qkv
            scores = mm_nt(qkv[:, :C], qkv[:, C : 2 * C]) * (SCALE * LOG2E) + bias[...]
            expo = jnp.exp2(scores - jnp.max(scores, -1, keepdims=True))
            probs = (expo * (1.0 / jnp.sum(expo, -1, keepdims=True))).astype(BF16)
            p_b[step, spot, :] = probs
            mixed = mm(probs, qkv[:, 2 * C :]).astype(BF16)
            o_b[step, spot, :] = mixed
            x2 = x1 + mm(mixed, w_co[...])
            xhat, rstd, normed = norm_forward(x2, gain_c)
            xh_c[step, spot, :] = xhat
            rs_c[step, spot, :] = rstd
            no_c[step, spot, :] = normed
            x3 = x2
            for block in range(FFH // C):
                cols = slice(block * C, (block + 1) * C)
                inner = mm(normed, w_fi[:, cols])
                t = 1.0 / (1.0 + (ERF_P * 0.5**0.5) * jnp.abs(inner))
                bell = jnp.exp2(inner * inner * (-0.5 * LOG2E))
                poly = 0.5 * ERF_C[5] * t + 0.5 * ERF_C[4]
                for coef in ERF_C[3::-1]:
                    poly = poly * t + 0.5 * coef
                tail = poly * t * bell
                cdf = jnp.where(inner >= 0.0, 1.0 - tail, tail)
                active = (inner * cdf).astype(BF16)
                gd[step, spot, cols] = cdf + inner * bell * 0.3989422804014327
                act[step, spot, cols] = active
                x3 = x3 + mm(active, w_fo[cols, :])
            x3s[scene, :, half, :, side] = x3.reshape(VIEWS, WIN, WIN, C)
        return carry

    lax.fori_loop(0, scenes * halves, forward, 0)

    row = iota((HALF, HALF), 0)
    lane = iota((HALF, HALF), 1)
    flip = (row + lane == HALF - 1).astype(BF16)
    eye = row == lane
    skew_keep = jnp.where((lane < HV) & (lane <= row % HV), 0.5 * SCALE, 0.0)
    back_keep = jnp.where((lane < HV) & (HV - 1 - lane <= row % HV), 0.5 * SCALE, 0.0)
    column = iota((PIX, C), 0) % HV
    not_first = column > 0
    not_last = column < HV - 1
    depth_values = 1.0 + 3.0 * iota((1, PLANES), 1).astype(F32) / (PLANES - 1)

    def im2col(value, pad, dest):
        pad[8 : 8 + PIX, :] = value
        dest[HV : HV + PIX, C : 2 * C] = value.astype(BF16)
        before = jnp.where(not_first, pad[7 : 7 + PIX, :], 0.0).astype(BF16)
        after = jnp.where(not_last, pad[9 : 9 + PIX, :], 0.0).astype(BF16)
        return before, after

    def head(scene, carry):
        live = count_ref[scene]
        for view in range(VIEWS):
            piece = x3s[scene, view].reshape(PIX, C).astype(BF16)
            low[view] = piece
            for part in range(2):
                lines = slice(part * HALF, (part + 1) * HALF)
                rev[view, lines, :] = mm(flip, piece[lines]).astype(BF16)
        d3s[scene] = jnp.zeros(d3s.shape[1:], F32)
        for view in range(VIEWS):
            partner = jnp.where(view + 1 < live, view + 1, 0)
            shift = offsets[scene, view : view + 1, :]
            hot = (shift == row).astype(BF16)
            hot_back = (shift == HV - 1 - row).astype(BF16)
            skewed = []
            for part in range(2):
                lines = slice(part * HALF, (part + 1) * HALF)
                corr = mm_nt(low[view, lines, :], rev[partner, lines, :])
                skewed.append(pltpu.roll(corr, 1, 1, stride=1, stride_axis=0) * skew_keep)
            cost = mm(split_two(jnp.concatenate(skewed, 0)), jnp.concatenate([hot, hot], 0))
            before, after = im2col(cost, pads.at[0, view], taps.at[view])
            taps[view, HV : HV + PIX, :C] = before
            taps[view, HV : HV + PIX, 2 * C :] = after
            columns = jnp.concatenate([taps[view, HV * a : HV * a + PIX, :] for a in range(3)], -1)
            refined = cost + mm(columns, t_rf[...])
            expo = jnp.exp2((refined - jnp.max(refined, -1, keepdims=True)) * LOG2E)
            inverse = 1.0 / jnp.sum(expo, -1, keepdims=True)
            depth = jnp.sum(expo * depth_values, -1, keepdims=True) * inverse
            valid = jnp.where(view < live, 1.0, 0.0)
            incoming = []
            for part in range(2):
                lines = slice(part * HALF, (part + 1) * HALF)
                depth_out[scene, view : view + 1, lines] = (
                    jnp.sum(jnp.where(eye, depth[lines], 0.0), 0, keepdims=True) * valid
                )
                incoming.append(
                    jnp.sum(jnp.where(eye, depth_grad[scene, view : view + 1, lines], 0.0), 1, keepdims=True)
                )
            weight = jnp.concatenate(incoming, 0) * (inverse * valid)
            d_refined = expo * (weight * depth_values - weight * depth)
            before, after = im2col(d_refined, pads.at[1, view], back_taps.at[view])
            back_taps[view, HV : HV + PIX, :C] = after
            back_taps[view, HV : HV + PIX, 2 * C :] = before
            g_rf[...] += mm_tn(back_taps[view, HV : HV + PIX, C : 2 * C], columns)
            d_cost = d_refined
            for a in range(3):
                shifted = back_taps[view, HV * (2 - a) : HV * (2 - a) + PIX, :]
                for b in range(3):
                    tap = 3 * a + b
                    d_cost = d_cost + mm(shifted[:, b * C : (b + 1) * C], w_rf[:, tap * C : (tap + 1) * C])
            d_skewed = mm_nt(split_two(d_cost), jnp.concatenate([hot_back, hot_back], -1))
            for part in range(2):
                lines = slice(part * HALF, (part + 1) * HALF)
                d_corr = pltpu.roll(
                    d_skewed[lines] * back_keep, HALF - HV + 1, 1, stride=1, stride_axis=0
                ).astype(BF16)
                shape = (WIN, 2, WIN, C)
                d3s[scene, view, part] += mm(d_corr, low[partner, lines, :]).reshape(shape)
                d3s[scene, partner, part] += mm_tn(d_corr, low[view, lines, :]).reshape(shape)
        return carry

    lax.fori_loop(0, scenes, head, 0)

    def backward(step, carry):
        scene = step // halves
        half = step % halves
        for side in range(2):
            spot = pl.ds(side * TOK, TOK)
            d3 = d3s[scene, :, half, :, side].reshape(TOK, C)
            d_low = d3.astype(BF16)
            normed = no_c[step, spot, :]
            g_fo[...] += mm_tn(d_low, act[step, spot, :])
            d_normed = jnp.zeros((TOK, C), F32)
            d_inners = []
            for block in range(FFH // C):
                cols = slice(block * C, (block + 1) * C)
                d_inner = (mm(d_low, t_fo[:, cols]) * gd[step, spot, cols]).astype(BF16)
                d_inners.append(d_inner)
            d_inner = jnp.concatenate(d_inners, -1)
            g_fi[...] += mm_tn(normed, d_inner)
            d_normed = mm(d_inner, t_fi[...])
            d_hidden, d_gain = norm_backward(d_normed, xh_c[step, spot, :], rs_c[step, spot, :], gain_c)
            g_gain[2] += d_gain
            d2 = d3 + d_hidden
            d_low = d2.astype(BF16)
            qkv = qkv_b[step, spot, :]
            g_co[...] += mm_tn(o_b[step, spot, :], d_low)
            d_mixed = mm(d_low, t_co[...]).astype(BF16)
            probs = p_b[step, spot, :]
            d_values = mm_tn(probs, d_mixed)
            d_probs = mm_nt(d_mixed, qkv[:, 2 * C :])
            probs = probs.astype(F32)
            delta = jnp.sum(d_probs * probs, -1, keepdims=True)
            d_raw = (probs * ((d_probs - delta) * SCALE)).astype(BF16)
            d_query = mm(d_raw, qkv[:, C : 2 * C])
            d_keys = mm_tn(d_raw, qkv[:, :C])
            d_packed = jnp.concatenate([d_query, d_keys, d_values], -1).astype(BF16)
            g_cq[...] += mm_tn(no_b[step, spot, :], d_packed)
            d_normed = mm(d_packed, t_cq[...])
            d_hidden, d_gain = norm_backward(d_normed, xh_b[step, spot, :], rs_b[step, spot, :], gain_b)
            g_gain[1] += d_gain
            d1 = d2 + d_hidden
            d_low = d1.astype(BF16)
            qkv = qkv_a[step, spot, :]
            g_so[...] += mm_tn(o_a[step, spot, :], d_low)
            d_mixed = mm(d_low, t_so[...]).astype(BF16)
            pieces = []
            for view in range(VIEWS):
                lines = slice(view * WIN * WIN, (view + 1) * WIN * WIN)
                probs = p_a[step, pl.ds(side * TOK + view * WIN * WIN, WIN * WIN), :]
                d_values = mm_tn(probs, d_mixed[lines])
                d_probs = mm_nt(d_mixed[lines], qkv[lines, 2 * C :])
                probs = probs.astype(F32)
                delta = jnp.sum(d_probs * probs, -1, keepdims=True)
                d_raw = (probs * ((d_probs - delta) * SCALE)).astype(BF16)
                d_query = mm(d_raw, qkv[lines, C : 2 * C])
                d_keys = mm_tn(d_raw, qkv[lines, :C])
                pieces.append(jnp.concatenate([d_query, d_keys, d_values], -1))
            d_packed = jnp.concatenate(pieces, 0).astype(BF16)
            g_sq[...] += mm_tn(no_a[step, spot, :], d_packed)
            d_normed = mm(d_packed, t_sq[...])
            d_hidden, d_gain = norm_backward(d_normed, xh_a[step, spot, :], rs_a[step, spot, :], gain_a)
            g_gain[0] += d_gain
            grad_out[scene, :, half, :, side] = (d1 + d_hidden).reshape(VIEWS, WIN, WIN, C)
        return carry

    lax.fori_loop(0, scenes * halves, backward, 0)

    bits = fsdp_bits(parts)
    line = iota((PAD_ROWS, C), 0)
    gain_rows = jnp.zeros((PAD_ROWS, C), F32)
    for which in range(3):
        gain_rows = jnp.where(line == which, jnp.sum(g_gain[which], 0, keepdims=True), gain_rows)
    gain_rows = gain_rows.astype(BF16)
    for block in range(FFH // C):
        w_fo[block * C : (block + 1) * C, :] = g_fo[:, block * C : (block + 1) * C].T.astype(BF16)
    for shard in range(parts):
        apart = shard ^ index_ref[0]
        slot = jnp.int32(0)
        for bit in range(bits):
            slot = slot + ((apart >> bit) & 1) * (1 << (bits - 1 - bit))
        at = 0
        for ref, blocks in zip((g_sq, g_so, g_cq, g_co, g_fi, w_fo, g_rf), BLOCKS):
            if ref is w_fo:
                grads_out[slot, at : at + blocks * rows, :] = ref[shard * blocks * rows : (shard + 1) * blocks * rows, :]
            else:
                for block in range(blocks):
                    grads_out[slot, at + block * rows : at + (block + 1) * rows, :] = ref[
                        shard * rows : (shard + 1) * rows, block * C : (block + 1) * C
                    ].astype(BF16)
            at += blocks * rows
        grads_out[slot, at : at + PAD_ROWS, :] = gain_rows


VMEM = pl.BlockSpec(memory_space=pltpu.VMEM)
SMEM = pl.BlockSpec(memory_space=pltpu.SMEM)


def exchange(value, axis, bit):
    size = lax.axis_size(axis)
    return lax.ppermute(value, axis, [(i, i ^ (1 << bit)) for i in range(size)])


def local(
    features,
    view_count,
    plane_offsets,
    depth_grad,
    gain_self,
    self_qkv,
    self_out,
    gain_cross,
    cross_qkv,
    cross_out,
    gain_ff,
    ff_in,
    ff_out,
    refine,
):
    parts = lax.axis_size("fsdp")
    copies = lax.axis_size("dp")
    scenes = features.shape[0]
    rows = C // parts
    shard_rows = sum(BLOCKS) * rows + PAD_ROWS
    index = lax.axis_index("fsdp").astype(jnp.int32).reshape(1)
    params = pltpu.CompilerParams(vmem_limit_bytes=VMEM_LIMIT)

    pack = pl.pallas_call(
        functools.partial(pack_kernel, parts),
        out_shape=jax.ShapeDtypeStruct((shard_rows, C), BF16),
        in_specs=[SMEM] + [VMEM] * 10,
        out_specs=VMEM,
        compiler_params=params,
        name="pack",
    )
    shard = pack(
        index,
        gain_self.reshape(1, rows),
        gain_cross.reshape(1, rows),
        gain_ff.reshape(1, rows),
        self_qkv,
        self_out,
        cross_qkv,
        cross_out,
        ff_in,
        ff_out,
        refine,
    )
    packed = lax.all_gather(shard, "fsdp", axis=0)

    steps = scenes * (HV // WIN)
    span = 2 * TOK
    scratch = [
        ((C, 3 * C), BF16), ((C, C), BF16), ((C, 3 * C), BF16), ((C, C), BF16),
        ((C, FFH), BF16), ((FFH, C), BF16), ((C, 9 * PLANES), BF16),
        ((3 * C, C), BF16), ((C, C), BF16), ((3 * C, C), BF16), ((C, C), BF16),
        ((FFH, C), BF16), ((C, FFH), BF16), ((9 * PLANES, C), BF16),
        ((8, C), F32),
        ((TOK, TOK), F32),
        ((VIEWS, WIN, 2, WIN, C), F32),
    ]
    scratch += [((steps, span, C), F32)] * 6
    scratch += [((steps, span, C), BF16)] * 3
    scratch += [
        ((steps, span, 3 * C), BF16), ((steps, span, 3 * C), BF16),
        ((steps, span, WIN * WIN), BF16), ((steps, span, TOK), BF16),
        ((steps, span, C), BF16), ((steps, span, C), BF16),
        ((steps, span, FFH), F32), ((steps, span, FFH), BF16),
        ((scenes, VIEWS, 2, WIN, 2, WIN, C), F32), ((scenes, VIEWS, 2, WIN, 2, WIN, C), F32),
        ((VIEWS, PIX, C), BF16), ((VIEWS, PIX, C), BF16),
        ((2, VIEWS, PIX + 16, C), F32),
        ((VIEWS, PIX + 2 * HV, 3 * C), BF16), ((VIEWS, PIX + 2 * HV, 3 * C), BF16),
        ((C, 3 * C), F32), ((C, C), F32), ((C, 3 * C), F32), ((C, C), F32),
        ((C, FFH), F32), ((C, FFH), F32), ((C, 9 * PLANES), F32), ((3, 8, C), F32),
    ]
    main = pl.pallas_call(
        functools.partial(main_kernel, scenes, parts),
        out_shape=(
            jax.ShapeDtypeStruct((scenes, VIEWS, PIX), F32),
            jax.ShapeDtypeStruct((scenes, VIEWS, 2, WIN, 2, WIN, C), F32),
            jax.ShapeDtypeStruct((parts, shard_rows, C), BF16),
        ),
        in_specs=[SMEM, SMEM] + [VMEM] * 4,
        out_specs=(VMEM, VMEM, VMEM),
        scratch_shapes=[pltpu.VMEM(shape, kind) for shape, kind in scratch],
        compiler_params=params,
        name="layer",
    )
    depth, grad_features, grads = main(view_count, index, features, plane_offsets, depth_grad, packed)

    for bit in range(fsdp_bits(parts)):
        half = grads.shape[0] // 2
        grads = grads[:half] + exchange(grads[half:], "fsdp", bit)
    grads = grads[0]
    bits = fsdp_bits(copies)
    for bit in range(bits - 1):
        grads = grads + exchange(grads, "dp", bit)
    other = exchange(grads, "dp", bits - 1)

    unpack = pl.pallas_call(
        functools.partial(unpack_kernel, parts),
        out_shape=tuple(jax.ShapeDtypeStruct((1, rows), F32) for _ in range(3))
        + tuple(
            jax.ShapeDtypeStruct(piece.shape, F32)
            for piece in (self_qkv, self_out, cross_qkv, cross_out, ff_in, ff_out, refine)
        ),
        in_specs=[SMEM, VMEM, VMEM],
        out_specs=(VMEM,) * 10,
        compiler_params=params,
        name="unpack",
    )
    ga, gb, gc, d_sq, d_so, d_cq, d_co, d_fi, d_fo, d_rf = unpack(index, grads, other)
    return (
        depth,
        grad_features.reshape(features.shape),
        ga.reshape(rows),
        d_sq,
        d_so,
        gb.reshape(rows),
        d_cq,
        d_co,
        gc.reshape(rows),
        d_fi,
        d_fo,
        d_rf,
    )


def solution(mesh):
    placed = (
        P(("dp", "fsdp"), None, None, None),
        P(("dp", "fsdp")),
        P(("dp", "fsdp"), None, None),
        P(("dp", "fsdp"), None, None),
        P("fsdp"),
        P("fsdp", None),
        P("fsdp", None),
        P("fsdp"),
        P("fsdp", None),
        P("fsdp", None),
        P("fsdp"),
        P("fsdp", None),
        P("fsdp", None),
        P("fsdp", None),
    )
    return jax.shard_map(
        local,
        mesh=mesh,
        in_specs=placed,
        out_specs=(
            P(("dp", "fsdp"), None, None),
            P(("dp", "fsdp"), None, None, None),
            P("fsdp"),
            P("fsdp", None),
            P("fsdp", None),
            P("fsdp"),
            P("fsdp", None),
            P("fsdp", None),
            P("fsdp"),
            P("fsdp", None),
            P("fsdp", None),
            P("fsdp", None),
        ),
        check_vma=False,
    )
```

```python
import functools

import jax
import jax.numpy as jnp
from jax import lax
from jax.experimental import pallas as pl
from jax.experimental.pallas import tpu as pltpu
from jax.sharding import PartitionSpec as P

C = 128
FFH = 512
PLANES = 128
WIN = 8
VIEWS = 4
HV = 16
PIX = HV * HV
TOK = VIEWS * WIN * WIN
HALF = PIX // 2
PAD_ROWS = 16
MASKED = -1e30
SCALE = C**-0.5
LOG2E = 1.4426950408889634
F32 = jnp.float32
BF16 = jnp.bfloat16
BLOCKS = (3, 1, 3, 1, 4, 4, 9)
VMEM_LIMIT = 60 * 1024 * 1024

ERF_P = 0.39
ERF_C = (0.23532522, 0.09138841, 0.6495594, -0.63540028, 0.88666437, -0.22753713)


def mm(left, right):
    return lax.dot_general(left, right, (((1,), (0,)), ((), ())), preferred_element_type=F32)


def mm_nt(left, right):
    return lax.dot_general(left, right, (((1,), (1,)), ((), ())), preferred_element_type=F32)


def mm_tn(left, right):
    return lax.dot_general(left, right, (((0,), (0,)), ((), ())), preferred_element_type=F32)


def norm_forward(value, gain):
    centred = value - jnp.mean(value, -1, keepdims=True)
    spread = jnp.mean(centred * centred, -1, keepdims=True)
    rstd = lax.rsqrt(spread + 1e-05)
    xhat = centred * rstd
    return xhat, jnp.broadcast_to(rstd, value.shape), (xhat * gain).astype(BF16)


def norm_backward(d_normed, xhat, rstd, gain):
    d_xhat = d_normed * gain
    mean_d = jnp.mean(d_xhat, -1, keepdims=True)
    mean_dx = jnp.mean(d_xhat * xhat, -1, keepdims=True)
    d_gain = jnp.sum((d_normed * xhat).reshape(-1, 8, C), 0)
    return rstd * (d_xhat - mean_d - xhat * mean_dx), d_gain


def split_two(value):
    high = value.astype(BF16)
    return jnp.concatenate([high, (value - high.astype(F32)).astype(BF16)], -1)


def iota(shape, axis):
    return lax.broadcasted_iota(jnp.int32, shape, axis)


def fsdp_bits(parts):
    return parts.bit_length() - 1


def pack_kernel(parts, index_ref, *refs):
    out = refs[-1]
    rows = C // parts
    at = 0
    for ref, blocks in zip(refs[3:10], BLOCKS):
        if ref.shape[0] == blocks * rows and ref.shape[1] == C:
            out[at : at + blocks * rows, :] = ref[...]
        else:
            for block in range(blocks):
                out[at + block * rows : at + (block + 1) * rows, :] = ref[:, block * C : (block + 1) * C]
        at += blocks * rows
    lane = iota((rows, C), 1)
    place = (lane == iota((rows, C), 0) + index_ref[0] * rows).astype(BF16)
    line = iota((PAD_ROWS, C), 0)
    gains = jnp.zeros((PAD_ROWS, C), F32)
    for which in range(3):
        row = mm(jnp.broadcast_to(refs[which][...], (8, rows)), place)[:1]
        gains = jnp.where(line == which, row, gains)
    out[at : at + PAD_ROWS, :] = gains.astype(BF16)


def unpack_kernel(parts, index_ref, left, right, *outs):
    rows = C // parts
    at = 0
    for out, blocks in zip(outs[3:10], BLOCKS):
        total = left[at : at + blocks * rows, :].astype(F32) + right[at : at + blocks * rows, :].astype(F32)
        if out.shape[0] == blocks * rows and out.shape[1] == C:
            out[...] = total
        else:
            for block in range(blocks):
                out[:, block * C : (block + 1) * C] = total[block * rows : (block + 1) * rows]
        at += blocks * rows
    gains = left[at : at + PAD_ROWS, :].astype(F32) + right[at : at + PAD_ROWS, :].astype(F32)
    lane = iota((C, rows), 0)
    place = (lane == iota((C, rows), 1) + index_ref[0] * rows).astype(F32)
    picked = lax.dot_general(
        gains, place, (((1,), (0,)), ((), ())), precision=lax.Precision.HIGHEST, preferred_element_type=F32
    )
    for which in range(3):
        outs[which][...] = picked[which : which + 1]


def main_kernel(
    scenes,
    parts,
    count_ref,
    index_ref,
    features,
    offsets,
    depth_grad,
    packed,
    depth_out,
    grad_out,
    grads_out,
    w_sq, w_so, w_cq, w_co, w_fi, w_fo, w_rf,
    t_sq, t_so, t_cq, t_co, t_fi, t_fo, t_rf, b_rf,
    gains,
    bias,
    x0s,
    xh_a, xh_b, xh_c, rs_a, rs_b, rs_c,
    no_a, no_b, no_c,
    qkv_a, qkv_b, p_a, p_b, o_a, o_b,
    gd, act,
    x3s, d3s,
    low, rev,
    pads, taps, back_taps,
    tables, eye, flip, hots,
    g_sq, g_so, g_cq, g_co, g_fi, g_fo, g_rf, g_gain,
):
    rows = C // parts
    halves = HV // WIN

    at = 0
    for ref, blocks in zip((w_sq, w_so, w_cq, w_co, w_fi, w_fo, w_rf), BLOCKS):
        for shard in range(parts):
            if ref is w_fo:
                ref[shard * blocks * rows : (shard + 1) * blocks * rows, :] = packed[shard, at : at + blocks * rows, :]
            else:
                for block in range(blocks):
                    ref[shard * rows : (shard + 1) * rows, block * C : (block + 1) * C] = packed[
                        shard, at + block * rows : at + (block + 1) * rows, :
                    ]
        at += blocks * rows
    total = packed[0, at : at + PAD_ROWS, :].astype(F32)
    for shard in range(1, parts):
        total = total + packed[shard, at : at + PAD_ROWS, :].astype(F32)
    gains[...] = total[:8]
    for source, target in ((w_sq, t_sq), (w_so, t_so), (w_cq, t_cq), (w_co, t_co), (w_fi, t_fi), (w_rf, t_rf)):
        for block in range(source.shape[1] // C):
            target[block * C : (block + 1) * C, :] = source[:, block * C : (block + 1) * C].T
    for block in range(9):
        b_rf[block * C : (block + 1) * C, :] = w_rf[:, block * C : (block + 1) * C]
    for block in range(FFH // C):
        t_fo[:, block * C : (block + 1) * C] = w_fo[block * C : (block + 1) * C, :].T

    for ref in (g_sq, g_so, g_cq, g_co, g_fi, g_fo, g_rf, g_gain, pads):
        ref[...] = jnp.zeros_like(ref)
    for ref in (taps, back_taps):
        ref[:, :HV, :] = jnp.zeros((VIEWS, HV, 3 * C), BF16)
        ref[:, HV + PIX :, :] = jnp.zeros((VIEWS, HV, 3 * C), BF16)

    gain_a = gains[0:1, :]
    gain_b = gains[1:2, :]
    gain_c = gains[2:3, :]

    places = [slice(side * TOK, (side + 1) * TOK) for side in range(2)]
    windows = [slice(at * WIN * WIN, (at + 1) * WIN * WIN) for at in range(2 * VIEWS)]

    def soft(scores):
        expo = jnp.exp2(scores - jnp.max(scores, -1, keepdims=True))
        return (expo * (1.0 / jnp.sum(expo, -1, keepdims=True))).astype(BF16)

    def forward(step, carry):
        scene = step // halves
        half = step % halves

        @pl.when(half == 0)
        def _():
            live = count_ref[scene]
            of_key = iota((TOK, TOK), 1) // (WIN * WIN)
            of_query = iota((TOK, TOK), 0) // (WIN * WIN)
            bias[...] = jnp.where((of_key < live) & (of_key != of_query), 0.0, MASKED)

        piece = features[scene, :, pl.ds(pl.multiple_of(half * HALF, HALF), HALF), :]
        x0s[...] = piece.astype(F32).reshape(VIEWS, WIN, 2, WIN, C)
        x0 = jnp.concatenate([x0s[:, :, side].reshape(TOK, C) for side in range(2)], 0)
        xhat, rstd, normed = norm_forward(x0, gain_a)
        xh_a[step] = xhat
        rs_a[step] = rstd
        no_a[step] = normed
        qkv = mm(normed, w_sq[...]).astype(BF16)
        qkv_a[step] = qkv
        scores = jnp.concatenate([mm_nt(qkv[at, :C], qkv[at, C : 2 * C]) for at in windows], 0)
        probs = soft(scores * (SCALE * LOG2E))
        p_a[step] = probs
        mixed = jnp.concatenate([mm(probs[at], qkv[at, 2 * C :]) for at in windows], 0).astype(BF16)
        o_a[step] = mixed
        x1 = x0 + mm(mixed, w_so[...])
        xhat, rstd, normed = norm_forward(x1, gain_b)
        xh_b[step] = xhat
        rs_b[step] = rstd
        no_b[step] = normed
        qkv = mm(normed, w_cq[...]).astype(BF16)
        qkv_b[step] = qkv
        scores = [mm_nt(qkv[at, :C], qkv[at, C : 2 * C]) * (SCALE * LOG2E) + bias[...] for at in places]
        probs = soft(jnp.concatenate(scores, 0))
        p_b[step] = probs
        mixed = jnp.concatenate([mm(probs[at], qkv[at, 2 * C :]) for at in places], 0).astype(BF16)
        o_b[step] = mixed
        x2 = x1 + mm(mixed, w_co[...])
        xhat, rstd, normed = norm_forward(x2, gain_c)
        xh_c[step] = xhat
        rs_c[step] = rstd
        no_c[step] = normed
        x3 = x2
        for block in range(FFH // C):
            cols = slice(block * C, (block + 1) * C)
            inner = mm(normed, w_fi[:, cols])
            t = 1.0 / (1.0 + (ERF_P * 0.5**0.5) * jnp.abs(inner))
            bell = jnp.exp2(inner * inner * (-0.5 * LOG2E))
            poly = 0.5 * ERF_C[5] * t + 0.5 * ERF_C[4]
            for coef in ERF_C[3::-1]:
                poly = poly * t + 0.5 * coef
            tail = poly * t * bell
            cdf = jnp.where(inner >= 0.0, 1.0 - tail, tail)
            gd[step, :, cols] = cdf + inner * bell * 0.3989422804014327
            act[step, :, cols] = (inner * cdf).astype(BF16)
        x3 = x2 + mm(act[step], w_fo[...])
        for side in range(2):
            x3s[scene, :, half, :, side] = x3[places[side]].reshape(VIEWS, WIN, WIN, C)
        return carry

    lax.fori_loop(0, scenes * halves, forward, 0)

    row = iota((HV, C), 0)
    lane = iota((HV, C), 1)
    tables[0:HV, :] = jnp.where((lane < HV) & (lane <= row), 0.5 * SCALE, 0.0)
    tables[HV : 2 * HV, :] = jnp.where((lane < HV) & (HV - 1 - lane <= row), 0.5 * SCALE, 0.0)
    tables[2 * HV : 3 * HV, :] = jnp.where(row > 0, 1.0, 0.0)
    tables[3 * HV : 4 * HV, :] = jnp.where(row < HV - 1, 1.0, 0.0)
    eye[...] = jnp.where(iota((HALF, HALF), 0) == iota((HALF, HALF), 1), 1.0, 0.0)
    flip[...] = (iota((HALF, HALF), 0) + iota((HALF, HALF), 1) == HALF - 1).astype(BF16)
    hots[...] = jnp.zeros_like(hots)
    depth_values = 1.0 + 3.0 * iota((1, PLANES), 1).astype(F32) / (PLANES - 1)
    upper = [slice(part * HALF, (part + 1) * HALF) for part in range(2)]
    views = range(VIEWS)

    def by_row(value, table):
        return (value.reshape(-1, HV, C) * table).reshape(value.shape)

    def im2col(value, pad, dest, first, last):
        pad[8 : 8 + PIX, :] = value
        dest[HV : HV + PIX, C : 2 * C] = value.astype(BF16)
        before = by_row(pad[7 : 7 + PIX, :], tables[2 * HV : 3 * HV, :])
        after = by_row(pad[9 : 9 + PIX, :], tables[3 * HV : 4 * HV, :])
        dest[HV : HV + PIX, first * C : (first + 1) * C] = before.astype(BF16)
        dest[HV : HV + PIX, last * C : (last + 1) * C] = after.astype(BF16)

    def head(scene, carry):
        live = count_ref[scene]
        goes_on = {1: live > 2, 2: live > 3}

        def partner_of(ref, view, at):
            if view in goes_on:
                return jnp.where(goes_on[view], ref[view + 1, at, :], ref[0, at, :])
            return ref[(view + 1) % VIEWS, at, :]

        for view in views:
            low[view] = x3s[scene, view].reshape(PIX, C).astype(BF16)
            shift = offsets[scene, view : view + 1, :]
            hots[0, view, 0:HV, :] = (shift == row).astype(BF16)
            hots[0, view, C : C + HV, :] = (shift == row).astype(BF16)
            hots[1, view, 0:HV, :] = (shift == HV - 1 - row).astype(BF16)
        for view in views:
            for at in upper:
                rev[view, at, :] = mm(flip[...], low[view, at, :]).astype(BF16)
        corrs = [[mm_nt(low[view, at, :], partner_of(rev, view, at)) for at in upper] for view in views]
        skewed = [
            [by_row(pltpu.roll(corr, 1, 1, stride=1, stride_axis=0), tables[0:HV, :]) for corr in corrs[view]]
            for view in views
        ]
        cost = [mm(split_two(jnp.concatenate(skewed[view], 0)), hots[0, view]) for view in views]
        for view in views:
            im2col(cost[view], pads.at[0, view], taps.at[view], 0, 2)
        refined = [
            cost[view]
            + mm(
                jnp.concatenate([taps[view, HV * a : HV * a + PIX, :] for a in range(3)], -1),
                t_rf[...],
            )
            for view in views
        ]
        d_refined = []
        for view in views:
            expo = jnp.exp2((refined[view] - jnp.max(refined[view], -1, keepdims=True)) * LOG2E)
            inverse = 1.0 / jnp.sum(expo, -1, keepdims=True)
            depth = jnp.sum(expo * depth_values, -1, keepdims=True) * inverse
            valid = jnp.where(view < live, 1.0, 0.0)
            incoming = []
            for at in upper:
                depth_out[scene, view : view + 1, at] = jnp.sum(eye[...] * depth[at], 0, keepdims=True) * valid
                incoming.append(jnp.sum(eye[...] * depth_grad[scene, view : view + 1, at], 1, keepdims=True))
            weight = jnp.concatenate(incoming, 0) * (inverse * valid)
            d_refined.append(expo * (weight * depth_values - weight * depth))
        for view in views:
            im2col(d_refined[view], pads.at[1, view], back_taps.at[view], 2, 0)
        d_cost = [
            d_refined[view]
            + mm(
                jnp.concatenate([back_taps[view, HV * (2 - a) : HV * (2 - a) + PIX, :] for a in range(3)], -1),
                b_rf[...],
            )
            for view in views
        ]
        for view in views:
            columns = jnp.concatenate([taps[view, HV * a : HV * a + PIX, :] for a in range(3)], -1)
            g_rf[...] += mm_tn(back_taps[view, HV : HV + PIX, C : 2 * C], columns)
        d_skewed = [
            mm_nt(split_two(d_cost[view]), jnp.concatenate([hots[1, view, :C, :]] * 2, -1)) for view in views
        ]
        d_corr = [
            [
                pltpu.roll(
                    by_row(d_skewed[view][at], tables[HV : 2 * HV, :]), HALF - HV + 1, 1, stride=1, stride_axis=0
                ).astype(BF16)
                for at in upper
            ]
            for view in views
        ]
        for part in range(2):
            at = upper[part]
            total = [mm(d_corr[view][part], partner_of(low, view, at)) for view in views]
            for view in views:
                there = mm_tn(d_corr[view][part], low[view, at, :])
                if view in goes_on:
                    total[view + 1] = total[view + 1] + jnp.where(goes_on[view], there, 0.0)
                    total[0] = total[0] + jnp.where(goes_on[view], 0.0, there)
                else:
                    total[(view + 1) % VIEWS] = total[(view + 1) % VIEWS] + there
            for view in views:
                d3s[scene, view, part] = total[view].reshape(WIN, 2, WIN, C)
        return carry

    lax.fori_loop(0, scenes, head, 0)

    def soft_back(probs, d_probs):
        probs = probs.astype(F32)
        delta = jnp.sum(d_probs * probs, -1, keepdims=True)
        return (probs * ((d_probs - delta) * SCALE)).astype(BF16)

    def backward(step, carry):
        scene = step // halves
        half = step % halves
        d3 = jnp.concatenate([d3s[scene, :, half, :, side].reshape(TOK, C) for side in range(2)], 0)
        d_low = d3.astype(BF16)
        d_inners = []
        for block in range(FFH // C):
            cols = slice(block * C, (block + 1) * C)
            d_inners.append((mm(d_low, t_fo[:, cols]) * gd[step, :, cols]).astype(BF16))
        d_inner = jnp.concatenate(d_inners, -1)
        d_normed = mm(d_inner, t_fi[...])
        g_fo[...] += mm_tn(d_low, act[step])
        g_fi[...] += mm_tn(no_c[step], d_inner)
        d_hidden, d_gain = norm_backward(d_normed, xh_c[step], rs_c[step], gain_c)
        g_gain[2] += d_gain
        d2 = d3 + d_hidden
        d_low = d2.astype(BF16)
        qkv = qkv_b[step]
        d_mixed = mm(d_low, t_co[...]).astype(BF16)
        g_co[...] += mm_tn(o_b[step], d_low)
        probs = p_b[step]
        d_values = jnp.concatenate([mm_tn(probs[at], d_mixed[at]) for at in places], 0)
        d_probs = jnp.concatenate([mm_nt(d_mixed[at], qkv[at, 2 * C :]) for at in places], 0)
        d_raw = soft_back(probs, d_probs)
        d_query = jnp.concatenate([mm(d_raw[at], qkv[at, C : 2 * C]) for at in places], 0)
        d_keys = jnp.concatenate([mm_tn(d_raw[at], qkv[at, :C]) for at in places], 0)
        d_packed = jnp.concatenate([d_query, d_keys, d_values], -1).astype(BF16)
        d_normed = mm(d_packed, t_cq[...])
        g_cq[...] += mm_tn(no_b[step], d_packed)
        d_hidden, d_gain = norm_backward(d_normed, xh_b[step], rs_b[step], gain_b)
        g_gain[1] += d_gain
        d1 = d2 + d_hidden
        d_low = d1.astype(BF16)
        qkv = qkv_a[step]
        d_mixed = mm(d_low, t_so[...]).astype(BF16)
        g_so[...] += mm_tn(o_a[step], d_low)
        probs = p_a[step]
        d_values = jnp.concatenate([mm_tn(probs[at], d_mixed[at]) for at in windows], 0)
        d_probs = jnp.concatenate([mm_nt(d_mixed[at], qkv[at, 2 * C :]) for at in windows], 0)
        d_raw = soft_back(probs, d_probs)
        d_query = jnp.concatenate([mm(d_raw[at], qkv[at, C : 2 * C]) for at in windows], 0)
        d_keys = jnp.concatenate([mm_tn(d_raw[at], qkv[at, :C]) for at in windows], 0)
        d_packed = jnp.concatenate([d_query, d_keys, d_values], -1).astype(BF16)
        d_normed = mm(d_packed, t_sq[...])
        g_sq[...] += mm_tn(no_a[step], d_packed)
        d_hidden, d_gain = norm_backward(d_normed, xh_a[step], rs_a[step], gain_a)
        g_gain[0] += d_gain
        d0 = d1 + d_hidden
        for side in range(2):
            grad_out[scene, :, half, :, side] = d0[places[side]].reshape(VIEWS, WIN, WIN, C)
        return carry

    lax.fori_loop(0, scenes * halves, backward, 0)

    bits = fsdp_bits(parts)
    line = iota((PAD_ROWS, C), 0)
    gain_rows = jnp.zeros((PAD_ROWS, C), F32)
    for which in range(3):
        gain_rows = jnp.where(line == which, jnp.sum(g_gain[which], 0, keepdims=True), gain_rows)
    gain_rows = gain_rows.astype(BF16)
    for block in range(FFH // C):
        w_fo[block * C : (block + 1) * C, :] = g_fo[:, block * C : (block + 1) * C].T.astype(BF16)
    for shard in range(parts):
        apart = shard ^ index_ref[0]
        slot = jnp.int32(0)
        for bit in range(bits):
            slot = slot + ((apart >> bit) & 1) * (1 << (bits - 1 - bit))
        at = 0
        for ref, blocks in zip((g_sq, g_so, g_cq, g_co, g_fi, w_fo, g_rf), BLOCKS):
            if ref is w_fo:
                grads_out[slot, at : at + blocks * rows, :] = ref[shard * blocks * rows : (shard + 1) * blocks * rows, :]
            else:
                for block in range(blocks):
                    grads_out[slot, at + block * rows : at + (block + 1) * rows, :] = ref[
                        shard * rows : (shard + 1) * rows, block * C : (block + 1) * C
                    ].astype(BF16)
            at += blocks * rows
        grads_out[slot, at : at + PAD_ROWS, :] = gain_rows


VMEM = pl.BlockSpec(memory_space=pltpu.VMEM)
SMEM = pl.BlockSpec(memory_space=pltpu.SMEM)


def exchange(value, axis, bit):
    size = lax.axis_size(axis)
    return lax.ppermute(value, axis, [(i, i ^ (1 << bit)) for i in range(size)])


def local(
    features,
    view_count,
    plane_offsets,
    depth_grad,
    gain_self,
    self_qkv,
    self_out,
    gain_cross,
    cross_qkv,
    cross_out,
    gain_ff,
    ff_in,
    ff_out,
    refine,
):
    parts = lax.axis_size("fsdp")
    copies = lax.axis_size("dp")
    scenes = features.shape[0]
    rows = C // parts
    shard_rows = sum(BLOCKS) * rows + PAD_ROWS
    index = lax.axis_index("fsdp").astype(jnp.int32).reshape(1)
    params = pltpu.CompilerParams(vmem_limit_bytes=VMEM_LIMIT)

    pack = pl.pallas_call(
        functools.partial(pack_kernel, parts),
        out_shape=jax.ShapeDtypeStruct((shard_rows, C), BF16),
        in_specs=[SMEM] + [VMEM] * 10,
        out_specs=VMEM,
        compiler_params=params,
        name="pack",
    )
    shard = pack(
        index,
        gain_self.reshape(1, rows),
        gain_cross.reshape(1, rows),
        gain_ff.reshape(1, rows),
        self_qkv,
        self_out,
        cross_qkv,
        cross_out,
        ff_in,
        ff_out,
        refine,
    )
    packed = lax.all_gather(shard, "fsdp", axis=0)

    steps = scenes * (HV // WIN)
    span = 2 * TOK
    scratch = [
        ((C, 3 * C), BF16), ((C, C), BF16), ((C, 3 * C), BF16), ((C, C), BF16),
        ((C, FFH), BF16), ((FFH, C), BF16), ((C, 9 * PLANES), BF16),
        ((3 * C, C), BF16), ((C, C), BF16), ((3 * C, C), BF16), ((C, C), BF16),
        ((FFH, C), BF16), ((C, FFH), BF16), ((9 * PLANES, C), BF16), ((9 * PLANES, C), BF16),
        ((8, C), F32),
        ((TOK, TOK), F32),
        ((VIEWS, WIN, 2, WIN, C), F32),
    ]
    scratch += [((steps, span, C), F32)] * 6
    scratch += [((steps, span, C), BF16)] * 3
    scratch += [
        ((steps, span, 3 * C), BF16), ((steps, span, 3 * C), BF16),
        ((steps, span, WIN * WIN), BF16), ((steps, span, TOK), BF16),
        ((steps, span, C), BF16), ((steps, span, C), BF16),
        ((steps, span, FFH), F32), ((steps, span, FFH), BF16),
        ((scenes, VIEWS, 2, WIN, 2, WIN, C), F32), ((scenes, VIEWS, 2, WIN, 2, WIN, C), F32),
        ((VIEWS, PIX, C), BF16), ((VIEWS, PIX, C), BF16),
        ((2, VIEWS, PIX + 16, C), F32),
        ((VIEWS, PIX + 2 * HV, 3 * C), BF16), ((VIEWS, PIX + 2 * HV, 3 * C), BF16),
        ((4 * HV, C), F32), ((HALF, HALF), F32), ((HALF, HALF), BF16), ((2, VIEWS, 2 * C, C), BF16),
        ((C, 3 * C), F32), ((C, C), F32), ((C, 3 * C), F32), ((C, C), F32),
        ((C, FFH), F32), ((C, FFH), F32), ((C, 9 * PLANES), F32), ((3, 8, C), F32),
    ]
    main = pl.pallas_call(
        functools.partial(main_kernel, scenes, parts),
        out_shape=(
            jax.ShapeDtypeStruct((scenes, VIEWS, PIX), F32),
            jax.ShapeDtypeStruct((scenes, VIEWS, 2, WIN, 2, WIN, C), F32),
            jax.ShapeDtypeStruct((parts, shard_rows, C), BF16),
        ),
        in_specs=[SMEM, SMEM] + [VMEM] * 4,
        out_specs=(VMEM, VMEM, VMEM),
        scratch_shapes=[pltpu.VMEM(shape, kind) for shape, kind in scratch],
        compiler_params=params,
        name="layer",
    )
    depth, grad_features, grads = main(view_count, index, features, plane_offsets, depth_grad, packed)

    for bit in range(fsdp_bits(parts)):
        half = grads.shape[0] // 2
        grads = grads[:half] + exchange(grads[half:], "fsdp", bit)
    grads = grads[0]
    bits = fsdp_bits(copies)
    for bit in range(bits - 1):
        grads = grads + exchange(grads, "dp", bit)
    other = exchange(grads, "dp", bits - 1)

    unpack = pl.pallas_call(
        functools.partial(unpack_kernel, parts),
        out_shape=tuple(jax.ShapeDtypeStruct((1, rows), F32) for _ in range(3))
        + tuple(
            jax.ShapeDtypeStruct(piece.shape, F32)
            for piece in (self_qkv, self_out, cross_qkv, cross_out, ff_in, ff_out, refine)
        ),
        in_specs=[SMEM, VMEM, VMEM],
        out_specs=(VMEM,) * 10,
        compiler_params=params,
        name="unpack",
    )
    ga, gb, gc, d_sq, d_so, d_cq, d_co, d_fi, d_fo, d_rf = unpack(index, grads, other)
    return (
        depth,
        grad_features.reshape(features.shape),
        ga.reshape(rows),
        d_sq,
        d_so,
        gb.reshape(rows),
        d_cq,
        d_co,
        gc.reshape(rows),
        d_fi,
        d_fo,
        d_rf,
    )


def solution(mesh):
    placed = (
        P(("dp", "fsdp"), None, None, None),
        P(("dp", "fsdp")),
        P(("dp", "fsdp"), None, None),
        P(("dp", "fsdp"), None, None),
        P("fsdp"),
        P("fsdp", None),
        P("fsdp", None),
        P("fsdp"),
        P("fsdp", None),
        P("fsdp", None),
        P("fsdp"),
        P("fsdp", None),
        P("fsdp", None),
        P("fsdp", None),
    )
    return jax.shard_map(
        local,
        mesh=mesh,
        in_specs=placed,
        out_specs=(
            P(("dp", "fsdp"), None, None),
            P(("dp", "fsdp"), None, None, None),
            P("fsdp"),
            P("fsdp", None),
            P("fsdp", None),
            P("fsdp"),
            P("fsdp", None),
            P("fsdp", None),
            P("fsdp"),
            P("fsdp", None),
            P("fsdp", None),
            P("fsdp", None),
        ),
        check_vma=False,
    )
```

```python
import functools

import jax
import jax.numpy as jnp
from jax import lax
from jax.experimental import pallas as pl
from jax.experimental.pallas import tpu as pltpu
from jax.sharding import PartitionSpec as P

C = 128
FFH = 512
PLANES = 128
WIN = 8
VIEWS = 4
HV = 16
PIX = HV * HV
TOK = VIEWS * WIN * WIN
HALF = PIX // 2
GAIN_ROWS = 16
MASKED = -1e30
SCALE = C**-0.5
LOG2E = 1.4426950408889634
F32 = jnp.float32
BF16 = jnp.bfloat16
BLOCKS = (3, 1, 3, 1, 4, 4, 9)
MIB = 1024 * 1024

ERF_P = 0.39
ERF_C = (0.23532522, 0.09138841, 0.6495594, -0.63540028, 0.88666437, -0.22753713)


def mm(left, right):
    return lax.dot_general(left, right, (((1,), (0,)), ((), ())), preferred_element_type=F32)


def mm_nt(left, right):
    return lax.dot_general(left, right, (((1,), (1,)), ((), ())), preferred_element_type=F32)


def mm_tn(left, right):
    return lax.dot_general(left, right, (((0,), (0,)), ((), ())), preferred_element_type=F32)


def norm_forward(value, gain):
    centred = value - jnp.mean(value, -1, keepdims=True)
    spread = jnp.mean(centred * centred, -1, keepdims=True)
    rstd = lax.rsqrt(spread + 1e-05)
    xhat = centred * rstd
    return xhat, jnp.broadcast_to(rstd, value.shape), (xhat * gain).astype(BF16)


def norm_backward(d_normed, xhat, rstd, gain):
    d_xhat = d_normed * gain
    mean_d = jnp.mean(d_xhat, -1, keepdims=True)
    mean_dx = jnp.mean(d_xhat * xhat, -1, keepdims=True)
    d_gain = jnp.sum((d_normed * xhat).reshape(-1, 8, C), 0)
    return rstd * (d_xhat - mean_d - xhat * mean_dx), d_gain


def split_two(value):
    high = value.astype(BF16)
    return jnp.concatenate([high, (value - high.astype(F32)).astype(BF16)], -1)


def iota(shape, axis):
    return lax.broadcasted_iota(jnp.int32, shape, axis)


def bits_of(size):
    return size.bit_length() - 1


def rows_of(parts):
    return -(-(sum(BLOCKS) * (C // parts) + GAIN_ROWS) // 32) * 32


def place_of(parts):
    return lax.axis_index("fsdp").astype(jnp.int32), (lax.axis_index("dp") & 1).astype(jnp.int32)


def pack_kernel(parts, *refs):
    gains, weights, out, scratch, sems = refs[:3], refs[3:10], refs[10], refs[11], refs[12]
    rows = C // parts
    copies = []

    def copy(source, target):
        copies.append(pltpu.make_async_copy(source, target, sems.at[len(copies)]))
        copies[-1].start()

    for which in range(3):
        copy(gains[which], scratch.at[which])
    at = 0
    for ref, blocks in zip(weights, BLOCKS):
        if ref.shape[0] == blocks * rows and ref.shape[1] == C:
            copy(ref, out.at[at : at + blocks * rows, :])
        else:
            for block in range(blocks):
                copy(ref.at[:, block * C : (block + 1) * C], out.at[at + block * rows : at + (block + 1) * rows, :])
        at += blocks * rows
    for one in copies[:3]:
        one.wait()
    place = (iota((rows, C), 1) == iota((rows, C), 0) + place_of(parts)[0] * rows).astype(BF16)
    line = iota((GAIN_ROWS, C), 0)
    total = jnp.zeros((GAIN_ROWS, C), F32)
    for which in range(3):
        row = mm(jnp.broadcast_to(scratch[which], (8, rows)), place)[:1]
        total = jnp.where(line == which, row, total)
    out[at : at + GAIN_ROWS, :] = total.astype(BF16)
    if at + GAIN_ROWS < out.shape[0]:
        out[at + GAIN_ROWS :, :] = jnp.zeros((out.shape[0] - at - GAIN_ROWS, C), BF16)
    for one in copies[3:]:
        one.wait()


def unpack_kernel(parts, *refs):
    terms = (len(refs) - 11) // 2
    own, other, outs = refs[:terms], refs[terms : 2 * terms], refs[2 * terms :]
    rows = C // parts
    me, side = place_of(parts)
    whole = outs[-1]
    half = own[0].shape[0]
    for first, pieces in ((side, own), (1 - side, other)):
        whole[pl.ds(pl.multiple_of(first * half, 16), half), :] = sum(piece[...].astype(F32) for piece in pieces)
    at = 0
    for out, blocks in zip(outs[3:10], BLOCKS):
        if out.shape[0] == blocks * rows and out.shape[1] == C:
            out[...] = whole[at : at + blocks * rows, :]
        else:
            for block in range(blocks):
                out[:, block * C : (block + 1) * C] = whole[at + block * rows : at + (block + 1) * rows, :]
        at += blocks * rows
    lane = iota((C, rows), 0)
    place = (lane == iota((C, rows), 1) + me * rows).astype(F32)
    picked = lax.dot_general(
        whole[at : at + GAIN_ROWS, :],
        place,
        (((1,), (0,)), ((), ())),
        precision=lax.Precision.HIGHEST,
        preferred_element_type=F32,
    )
    for which in range(3):
        outs[which][...] = picked[which : which + 1]


def merge(*threads):
    spent = [0.0] * len(threads)
    left = set(range(len(threads)))
    while left:
        which = min(left, key=lambda i: (spent[i], i))
        try:
            spent[which] += next(threads[which])
        except StopIteration:
            left.remove(which)


def paced(thread, rate):
    for share in thread:
        yield share * rate


def soft(scores):
    expo = jnp.exp2(scores - jnp.max(scores, -1, keepdims=True))
    return (expo * (1.0 / jnp.sum(expo, -1, keepdims=True))).astype(BF16)


def soft_back(probs, d_probs):
    probs = probs.astype(F32)
    delta = jnp.sum(d_probs * probs, -1, keepdims=True)
    return (probs * ((d_probs - delta) * SCALE)).astype(BF16)


def joined(pieces):
    return jnp.concatenate(pieces, 0)


def main_kernel(
    scenes,
    parts,
    count_ref,
    features_hbm,
    offsets,
    depth_grad,
    *refs,
):
    packed = refs[:parts]
    (
    depth_out,
    grad_hbm,
    keep_out,
    send_out,
    w_sq, w_so, w_cq, w_co, w_fi, w_fo, w_rf,
    t_sq, t_so, t_cq, t_co, t_fi, t_fo, t_rf, b_rf,
    gains,
    bias,
    x0s, x2s,
    xh_a, xh_b, xh_c, rs_a, rs_b, rs_c,
    no_a, no_b, no_c,
    qkv_a, qkv_b, p_a, p_b, o_a, o_b,
    gd, act,
    x3s, d3s,
    low, rev,
    pads, taps, back_taps,
    tables, eye, flip, hots,
    g_sq, g_so, g_cq, g_co, g_fi, g_fo, g_rf, g_gain,
    features, grad_out, sems,
    ) = refs[parts:]
    rows = C // parts
    me, side_of_rows = place_of(parts)
    bring = pltpu.make_async_copy(features_hbm, features, sems.at[0])
    bring.start()
    sent = []

    total = jnp.zeros((GAIN_ROWS, C), F32)
    for apart, piece in enumerate(packed):
        shard = me ^ apart
        at = 0
        for ref, blocks in zip((w_sq, w_so, w_cq, w_co, w_fi, w_fo, w_rf), BLOCKS):
            if ref is w_fo:
                spot = pl.ds(pl.multiple_of(shard * (blocks * rows), 16), blocks * rows)
                ref[spot, :] = piece[at : at + blocks * rows, :]
            else:
                spot = pl.ds(pl.multiple_of(shard * rows, 16), rows)
                for block in range(blocks):
                    ref[spot, block * C : (block + 1) * C] = piece[at + block * rows : at + (block + 1) * rows, :]
            at += blocks * rows
        total = total + piece[at : at + GAIN_ROWS, :].astype(F32)
    gains[...] = total[:8]
    for source, target in ((w_sq, t_sq), (w_so, t_so), (w_cq, t_cq), (w_co, t_co), (w_fi, t_fi), (w_rf, t_rf)):
        for block in range(source.shape[1] // C):
            target[block * C : (block + 1) * C, :] = source[:, block * C : (block + 1) * C].T
    for block in range(9):
        b_rf[block * C : (block + 1) * C, :] = w_rf[:, block * C : (block + 1) * C]
    for block in range(FFH // C):
        t_fo[:, block * C : (block + 1) * C] = w_fo[block * C : (block + 1) * C, :].T

    for ref in (g_sq, g_so, g_cq, g_co, g_fi, g_fo, g_rf, g_gain, pads, hots):
        ref[...] = jnp.zeros_like(ref)
    for ref in (taps, back_taps):
        for scene in range(scenes):
            ref[scene, :, :HV, :] = jnp.zeros((VIEWS, HV, 3 * C), BF16)
            ref[scene, :, HV + PIX :, :] = jnp.zeros((VIEWS, HV, 3 * C), BF16)

    row = iota((HV, C), 0)
    lane = iota((HV, C), 1)
    tables[0:HV, :] = jnp.where((lane < HV) & (lane <= row), 0.5 * SCALE, 0.0)
    tables[HV : 2 * HV, :] = jnp.where((lane < HV) & (HV - 1 - lane <= row), 0.5 * SCALE, 0.0)
    tables[2 * HV : 3 * HV, :] = jnp.where(row > 0, 1.0, 0.0)
    tables[3 * HV : 4 * HV, :] = jnp.where(row < HV - 1, 1.0, 0.0)
    eye[...] = jnp.where(iota((HALF, HALF), 0) == iota((HALF, HALF), 1), 1.0, 0.0)
    flip[...] = (iota((HALF, HALF), 0) + iota((HALF, HALF), 1) == HALF - 1).astype(BF16)
    of_key = iota((TOK, TOK), 1) // (WIN * WIN)
    of_query = iota((TOK, TOK), 0) // (WIN * WIN)
    for scene in range(scenes):
        live = count_ref[scene]
        bias[scene] = jnp.where((of_key < live) & (of_key != of_query), 0.0, MASKED)

    gain_a = gains[0:1, :]
    gain_b = gains[1:2, :]
    gain_c = gains[2:3, :]
    depth_values = 1.0 + 3.0 * iota((1, PLANES), 1).astype(F32) / (PLANES - 1)
    upper = [slice(part * HALF, (part + 1) * HALF) for part in range(2)]
    views = range(VIEWS)
    places = [slice(side * TOK, (side + 1) * TOK) for side in range(2)]
    windows = [slice(at * WIN * WIN, (at + 1) * WIN * WIN) for at in range(2 * VIEWS)]

    def attend(scene, half):
        step = 2 * scene + half
        piece = features[scene, :, half * HALF : (half + 1) * HALF, :]
        x0s[step] = piece.astype(F32).reshape(VIEWS, WIN, 2, WIN, C)
        x0 = joined([x0s[step, :, :, side].reshape(TOK, C) for side in range(2)])
        xhat, rstd, normed = norm_forward(x0, gain_a)
        xh_a[step] = xhat
        rs_a[step] = rstd
        no_a[step] = normed
        yield 400
        qkv = mm(normed, w_sq[...]).astype(BF16)
        qkv_a[step] = qkv
        yield 300
        scores = joined([mm_nt(qkv[at, :C], qkv[at, C : 2 * C]) for at in windows])
        yield 200
        probs = soft(scores * (SCALE * LOG2E))
        p_a[step] = probs
        yield 400
        mixed = joined([mm(probs[at], qkv[at, 2 * C :]) for at in windows]).astype(BF16)
        o_a[step] = mixed
        yield 300
        x1 = x0 + mm(mixed, w_so[...])
        yield 200
        xhat, rstd, normed = norm_forward(x1, gain_b)
        xh_b[step] = xhat
        rs_b[step] = rstd
        no_b[step] = normed
        yield 400
        qkv = mm(normed, w_cq[...]).astype(BF16)
        qkv_b[step] = qkv
        yield 300
        scores = [mm_nt(qkv[at, :C], qkv[at, C : 2 * C]) * (SCALE * LOG2E) + bias[scene] for at in places]
        yield 300
        probs = soft(joined(scores))
        p_b[step] = probs
        yield 500
        mixed = joined([mm(probs[at], qkv[at, 2 * C :]) for at in places]).astype(BF16)
        o_b[step] = mixed
        yield 300
        x2 = x1 + mm(mixed, w_co[...])
        x2s[step] = x2
        yield 200
        xhat, rstd, normed = norm_forward(x2, gain_c)
        xh_c[step] = xhat
        rs_c[step] = rstd
        no_c[step] = normed
        yield 400

    def feed(scene, half):
        step = 2 * scene + half
        for block in range(FFH // C):
            cols = slice(block * C, (block + 1) * C)
            for at in places:
                inner = mm(no_c[step, at, :], w_fi[:, cols])
                t = 1.0 / (1.0 + (ERF_P * 0.5**0.5) * jnp.abs(inner))
                bell = jnp.exp2(inner * inner * (-0.5 * LOG2E))
                poly = 0.5 * ERF_C[5] * t + 0.5 * ERF_C[4]
                for coef in ERF_C[3::-1]:
                    poly = poly * t + 0.5 * coef
                tail = poly * t * bell
                cdf = jnp.where(inner >= 0.0, 1.0 - tail, tail)
                gd[step, at, cols] = cdf + inner * bell * 0.3989422804014327
                act[step, at, cols] = (inner * cdf).astype(BF16)
                yield 260
        x3 = x2s[step] + mm(act[step], w_fo[...])
        for side in range(2):
            x3s[scene, :, half, :, side] = x3[places[side]].reshape(VIEWS, WIN, WIN, C)
        yield 300

    def by_row(value, table):
        return (value.reshape(-1, HV, C) * table).reshape(value.shape)

    def im2col(value, pad, dest, first, last):
        pad[8 : 8 + PIX, :] = value
        dest[HV : HV + PIX, C : 2 * C] = value.astype(BF16)
        before = by_row(pad[7 : 7 + PIX, :], tables[2 * HV : 3 * HV, :])
        after = by_row(pad[9 : 9 + PIX, :], tables[3 * HV : 4 * HV, :])
        dest[HV : HV + PIX, first * C : (first + 1) * C] = before.astype(BF16)
        dest[HV : HV + PIX, last * C : (last + 1) * C] = after.astype(BF16)

    def head(scene):
        live = count_ref[scene]
        goes_on = {1: live > 2, 2: live > 3}

        def partner_of(ref, view, at):
            if view in goes_on:
                return jnp.where(goes_on[view], ref[scene, view + 1, at, :], ref[scene, 0, at, :])
            return ref[scene, (view + 1) % VIEWS, at, :]

        for view in views:
            low[scene, view] = x3s[scene, view].reshape(PIX, C).astype(BF16)
            shift = offsets[scene, view : view + 1, :]
            hots[scene, 0, view, 0:HV, :] = (shift == row).astype(BF16)
            hots[scene, 0, view, C : C + HV, :] = (shift == row).astype(BF16)
            hots[scene, 1, view, 0:HV, :] = (shift == HV - 1 - row).astype(BF16)
        yield 150
        for view in views:
            for at in upper:
                rev[scene, view, at, :] = mm(flip[...], low[scene, view, at, :]).astype(BF16)
        yield 250
        corrs = [[mm_nt(low[scene, view, at, :], partner_of(rev, view, at)) for at in upper] for view in views]
        yield 250
        skewed = [
            [by_row(pltpu.roll(corr, 1, 1, stride=1, stride_axis=0), tables[0:HV, :]) for corr in corrs[view]]
            for view in views
        ]
        yield 300
        cost = [mm(split_two(joined(skewed[view])), hots[scene, 0, view]) for view in views]
        yield 300
        for view in views:
            im2col(cost[view], pads.at[scene, 0, view], taps.at[scene, view], 0, 2)
            yield 80
        refined = []
        for view in views:
            columns = jnp.concatenate([taps[scene, view, HV * a : HV * a + PIX, :] for a in range(3)], -1)
            refined.append(cost[view] + mm(columns, t_rf[...]))
            yield 320
        d_refined = []
        for view in views:
            expo = jnp.exp2((refined[view] - jnp.max(refined[view], -1, keepdims=True)) * LOG2E)
            inverse = 1.0 / jnp.sum(expo, -1, keepdims=True)
            depth = jnp.sum(expo * depth_values, -1, keepdims=True) * inverse
            valid = jnp.where(view < live, 1.0, 0.0)
            incoming = []
            for at in upper:
                depth_out[scene, view : view + 1, at] = jnp.sum(eye[...] * depth[at], 0, keepdims=True) * valid
                incoming.append(jnp.sum(eye[...] * depth_grad[scene, view : view + 1, at], 1, keepdims=True))
            weight = joined(incoming) * (inverse * valid)
            d_refined.append(expo * (weight * depth_values - weight * depth))
            yield 250
        for view in views:
            im2col(d_refined[view], pads.at[scene, 1, view], back_taps.at[scene, view], 2, 0)
            yield 80
        d_cost = []
        for view in views:
            columns = jnp.concatenate(
                [back_taps[scene, view, HV * (2 - a) : HV * (2 - a) + PIX, :] for a in range(3)], -1
            )
            d_cost.append(d_refined[view] + mm(columns, b_rf[...]))
            yield 320
        for view in views:
            columns = jnp.concatenate([taps[scene, view, HV * a : HV * a + PIX, :] for a in range(3)], -1)
            g_rf[...] += mm_tn(back_taps[scene, view, HV : HV + PIX, C : 2 * C], columns)
            yield 250
        d_skewed = [
            mm_nt(split_two(d_cost[view]), jnp.concatenate([hots[scene, 1, view, :C, :]] * 2, -1)) for view in views
        ]
        yield 300
        d_corr = [
            [
                pltpu.roll(
                    by_row(d_skewed[view][at], tables[HV : 2 * HV, :]), HALF - HV + 1, 1, stride=1, stride_axis=0
                ).astype(BF16)
                for at in upper
            ]
            for view in views
        ]
        yield 250
        for part in range(2):
            at = upper[part]
            total = [mm(d_corr[view][part], partner_of(low, view, at)) for view in views]
            for view in views:
                there = mm_tn(d_corr[view][part], low[scene, view, at, :])
                if view in goes_on:
                    total[view + 1] = total[view + 1] + jnp.where(goes_on[view], there, 0.0)
                    total[0] = total[0] + jnp.where(goes_on[view], 0.0, there)
                else:
                    total[(view + 1) % VIEWS] = total[(view + 1) % VIEWS] + there
            for view in views:
                d3s[scene, view, part] = total[view].reshape(WIN, 2, WIN, C)
            yield 250

    def back(scene, half):
        step = 2 * scene + half
        d3 = joined([d3s[scene, :, half, :, side].reshape(TOK, C) for side in range(2)])
        d_low = d3.astype(BF16)
        d_inners = []
        for block in range(FFH // C):
            cols = slice(block * C, (block + 1) * C)
            d_inners.append((mm(d_low, t_fo[:, cols]) * gd[step, :, cols]).astype(BF16))
            yield 100
        d_inner = jnp.concatenate(d_inners, -1)
        d_normed = mm(d_inner, t_fi[...])
        yield 300
        g_fo[...] += mm_tn(d_low, act[step])
        yield 250
        g_fi[...] += mm_tn(no_c[step], d_inner)
        yield 250
        d_hidden, d_gain = norm_backward(d_normed, xh_c[step], rs_c[step], gain_c)
        g_gain[2] += d_gain
        d2 = d3 + d_hidden
        yield 300
        d_low = d2.astype(BF16)
        qkv = qkv_b[step]
        d_mixed = mm(d_low, t_co[...]).astype(BF16)
        yield 200
        g_co[...] += mm_tn(o_b[step], d_low)
        probs = p_b[step]
        d_values = joined([mm_tn(probs[at], d_mixed[at]) for at in places])
        d_probs = joined([mm_nt(d_mixed[at], qkv[at, 2 * C :]) for at in places])
        yield 400
        d_raw = soft_back(probs, d_probs)
        yield 300
        d_query = joined([mm(d_raw[at], qkv[at, C : 2 * C]) for at in places])
        d_keys = joined([mm_tn(d_raw[at], qkv[at, :C]) for at in places])
        d_packed = jnp.concatenate([d_query, d_keys, d_values], -1).astype(BF16)
        yield 400
        d_normed = mm(d_packed, t_cq[...])
        yield 200
        g_cq[...] += mm_tn(no_b[step], d_packed)
        yield 200
        d_hidden, d_gain = norm_backward(d_normed, xh_b[step], rs_b[step], gain_b)
        g_gain[1] += d_gain
        d1 = d2 + d_hidden
        yield 300
        d_low = d1.astype(BF16)
        qkv = qkv_a[step]
        d_mixed = mm(d_low, t_so[...]).astype(BF16)
        yield 200
        g_so[...] += mm_tn(o_a[step], d_low)
        probs = p_a[step]
        d_values = joined([mm_tn(probs[at], d_mixed[at]) for at in windows])
        d_probs = joined([mm_nt(d_mixed[at], qkv[at, 2 * C :]) for at in windows])
        yield 400
        d_raw = soft_back(probs, d_probs)
        yield 200
        d_query = joined([mm(d_raw[at], qkv[at, C : 2 * C]) for at in windows])
        d_keys = joined([mm_tn(d_raw[at], qkv[at, :C]) for at in windows])
        d_packed = jnp.concatenate([d_query, d_keys, d_values], -1).astype(BF16)
        yield 300
        d_normed = mm(d_packed, t_sq[...])
        yield 200
        g_sq[...] += mm_tn(no_a[step], d_packed)
        yield 200
        d_hidden, d_gain = norm_backward(d_normed, xh_a[step], rs_a[step], gain_a)
        g_gain[0] += d_gain
        d0 = d1 + d_hidden
        for side in range(2):
            grad_out[scene, :, half, :, side] = d0[places[side]].reshape(VIEWS, WIN, WIN, C)
        sent.append(
            pltpu.make_async_copy(grad_out.at[scene, :, half], grad_hbm.at[scene, :, half], sems.at[1 + step])
        )
        sent[-1].start()
        yield 300

    def chain(*threads):
        for thread in threads:
            yield from thread

    def feeds(scene):
        return chain(feed(scene, 0), feed(scene, 1))

    bring.wait()
    merge(attend(0, 0))
    merge(attend(0, 1), feed(0, 0))
    for scene in range(1, scenes):
        merge(attend(scene, 0), feed(scene - 1, 1))
        merge(chain(attend(scene, 1), feed(scene, 1)), feed(scene, 0), paced(head(scene - 1), 1.0))
        merge(head(scene), paced(chain(back(scene - 1, 0), back(scene - 1, 1)), 0.6))
    merge(back(scenes - 1, 0), back(scenes - 1, 1))

    bits = bits_of(parts)
    line = iota((GAIN_ROWS, C), 0)
    gain_rows = jnp.zeros((GAIN_ROWS, C), F32)
    for which in range(3):
        gain_rows = jnp.where(line == which, jnp.sum(g_gain[which], 0, keepdims=True), gain_rows)
    gain_rows = gain_rows.astype(BF16)
    for block in range(FFH // C):
        w_fo[block * C : (block + 1) * C, :] = g_fo[:, block * C : (block + 1) * C].T.astype(BF16)
    half_rows = rows_of(parts) // 2
    first = side_of_rows
    for apart in range(parts):
        shard = me ^ apart
        slot = sum(((apart >> bit) & 1) << (bits - 1 - bit) for bit in range(bits))
        dest = (keep_out, send_out)[slot // (parts // 2)].at[slot % (parts // 2)]

        def put(at, value):
            height = value.shape[0]
            which, offset = divmod(at, half_rows)
            assert offset + height <= half_rows
            dest[pl.ds(pl.multiple_of((first ^ which) * half_rows + offset, 16), height), :] = value

        at = 0
        for ref, blocks in zip((g_sq, g_so, g_cq, g_co, g_fi, w_fo, g_rf), BLOCKS):
            for block in range(blocks):
                if ref is w_fo:
                    spot = pl.ds(pl.multiple_of(shard * (blocks * rows) + block * rows, 16), rows)
                    put(at, ref[spot, :])
                else:
                    spot = pl.ds(pl.multiple_of(shard * rows, 16), rows)
                    put(at, ref[spot, block * C : (block + 1) * C].astype(BF16))
                at += rows
        put(at, gain_rows)
        if at + GAIN_ROWS < rows_of(parts):
            put(at + GAIN_ROWS, jnp.zeros((rows_of(parts) - at - GAIN_ROWS, C), BF16))
    for one in sent:
        one.wait()


VMEM = pl.BlockSpec(memory_space=pltpu.VMEM)
HBM = pl.BlockSpec(memory_space=pltpu.HBM)
SMEM = pl.BlockSpec(memory_space=pltpu.SMEM)


def exchange(value, fsdp_mask, dp_mask):
    parts = lax.axis_size("fsdp")
    count = parts * lax.axis_size("dp")
    mask = dp_mask * parts + fsdp_mask
    return lax.ppermute(value, ("dp", "fsdp"), [(i, i ^ mask) for i in range(count)])


def local(
    features,
    view_count,
    plane_offsets,
    depth_grad,
    gain_self,
    self_qkv,
    self_out,
    gain_cross,
    cross_qkv,
    cross_out,
    gain_ff,
    ff_in,
    ff_out,
    refine,
):
    parts = lax.axis_size("fsdp")
    copies = lax.axis_size("dp")
    scenes = features.shape[0]
    rows = C // parts
    shard_rows = rows_of(parts)
    small = pltpu.CompilerParams(vmem_limit_bytes=8 * MIB)

    pack = pl.pallas_call(
        functools.partial(pack_kernel, parts),
        out_shape=jax.ShapeDtypeStruct((shard_rows, C), BF16),
        in_specs=[HBM] * 10,
        out_specs=VMEM,
        scratch_shapes=[pltpu.VMEM((3, 1, rows), BF16), pltpu.SemaphoreType.DMA((3 + sum(BLOCKS),))],
        compiler_params=pltpu.CompilerParams(vmem_limit_bytes=60 * MIB),
        name="pack",
    )
    shard = pack(
        gain_self.reshape(1, rows),
        gain_cross.reshape(1, rows),
        gain_ff.reshape(1, rows),
        self_qkv,
        self_out,
        cross_qkv,
        cross_out,
        ff_in,
        ff_out,
        refine,
    )
    packed = {0: shard}
    for bit in reversed(range(bits_of(parts))):
        packed |= {apart | (1 << bit): exchange(piece, 1 << bit, 0) for apart, piece in packed.items()}
    packed = [packed[apart] for apart in range(parts)]

    steps = scenes * (HV // WIN)
    span = 2 * TOK
    scratch = [
        ((C, 3 * C), BF16), ((C, C), BF16), ((C, 3 * C), BF16), ((C, C), BF16),
        ((C, FFH), BF16), ((FFH, C), BF16), ((C, 9 * PLANES), BF16),
        ((3 * C, C), BF16), ((C, C), BF16), ((3 * C, C), BF16), ((C, C), BF16),
        ((FFH, C), BF16), ((C, FFH), BF16), ((9 * PLANES, C), BF16), ((9 * PLANES, C), BF16),
        ((8, C), F32),
        ((scenes, TOK, TOK), F32),
        ((steps, VIEWS, WIN, 2, WIN, C), F32),
        ((steps, span, C), F32),
    ]
    scratch += [((steps, span, C), F32)] * 6
    scratch += [((steps, span, C), BF16)] * 3
    scratch += [
        ((steps, span, 3 * C), BF16), ((steps, span, 3 * C), BF16),
        ((steps, span, WIN * WIN), BF16), ((steps, span, TOK), BF16),
        ((steps, span, C), BF16), ((steps, span, C), BF16),
        ((steps, span, FFH), F32), ((steps, span, FFH), BF16),
        ((scenes, VIEWS, 2, WIN, 2, WIN, C), F32), ((scenes, VIEWS, 2, WIN, 2, WIN, C), F32),
        ((scenes, VIEWS, PIX, C), BF16), ((scenes, VIEWS, PIX, C), BF16),
        ((scenes, 2, VIEWS, PIX + 16, C), F32),
        ((scenes, VIEWS, PIX + 2 * HV, 3 * C), BF16), ((scenes, VIEWS, PIX + 2 * HV, 3 * C), BF16),
        ((4 * HV, C), F32), ((HALF, HALF), F32), ((HALF, HALF), BF16), ((scenes, 2, VIEWS, 2 * C, C), BF16),
        ((C, 3 * C), F32), ((C, C), F32), ((C, 3 * C), F32), ((C, C), F32),
        ((C, FFH), F32), ((C, FFH), F32), ((C, 9 * PLANES), F32), ((3, 8, C), F32),
    ]
    main = pl.pallas_call(
        functools.partial(main_kernel, scenes, parts),
        out_shape=(
            jax.ShapeDtypeStruct((scenes, VIEWS, PIX), F32),
            jax.ShapeDtypeStruct((scenes, VIEWS, 2, WIN, 2, WIN, C), F32),
            jax.ShapeDtypeStruct((parts // 2, shard_rows, C), BF16),
            jax.ShapeDtypeStruct((parts // 2, shard_rows, C), BF16),
        ),
        in_specs=[SMEM, HBM] + [VMEM] * (2 + parts),
        out_specs=(VMEM, HBM, VMEM, VMEM),
        scratch_shapes=[pltpu.VMEM(shape, kind) for shape, kind in scratch]
        + [
            pltpu.VMEM(features.shape, BF16),
            pltpu.VMEM((scenes, VIEWS, 2, WIN, 2, WIN, C), F32),
            pltpu.SemaphoreType.DMA((1 + steps,)),
        ],
        compiler_params=pltpu.CompilerParams(vmem_limit_bytes=52 * MIB),
        name="layer",
    )
    depth, grad_features, keep, send = main(view_count, features, plane_offsets, depth_grad, *packed)

    for bit in range(bits_of(parts)):
        if bit > 0:
            keep, send = keep[: keep.shape[0] // 2], keep[keep.shape[0] // 2 :]
        if bit < bits_of(parts) - 1:
            keep = keep + exchange(send, 1 << bit, 0)
    last = parts // 2
    half = shard_rows // 2
    beside = exchange(send[0, :half], last, 0)
    across = exchange(keep[0, half:], 0, 1)
    corner = exchange(send[0, half:], last, 1)
    grads = (keep[0, :half].astype(F32) + beside) + (across.astype(F32) + corner)
    grads = grads.astype(BF16)
    for bit in reversed(range(2, bits_of(copies))):
        grads = grads + exchange(grads, 0, 1 << bit)
    if bits_of(copies) > 1:
        along = exchange(grads, 0, 2)
        swapped = exchange(grads, 0, 1)
        corner = exchange(grads, 0, 3)
        own, other = (grads, along), (swapped, corner)
    else:
        own, other = (grads,), (exchange(grads, 0, 1),)

    unpack = pl.pallas_call(
        functools.partial(unpack_kernel, parts),
        out_shape=tuple(jax.ShapeDtypeStruct((1, rows), F32) for _ in range(3))
        + tuple(
            jax.ShapeDtypeStruct(piece.shape, F32)
            for piece in (self_qkv, self_out, cross_qkv, cross_out, ff_in, ff_out, refine)
        ),
        in_specs=[VMEM] * (2 * len(own)),
        out_specs=(VMEM,) * 10,
        scratch_shapes=[pltpu.VMEM((shard_rows, C), F32)],
        compiler_params=small,
        name="unpack",
    )
    ga, gb, gc, d_sq, d_so, d_cq, d_co, d_fi, d_fo, d_rf = unpack(*own, *other)
    return (
        depth,
        grad_features.reshape(features.shape),
        ga.reshape(rows),
        d_sq,
        d_so,
        gb.reshape(rows),
        d_cq,
        d_co,
        gc.reshape(rows),
        d_fi,
        d_fo,
        d_rf,
    )


def solution(mesh):
    placed = (
        P(("dp", "fsdp"), None, None, None),
        P(("dp", "fsdp")),
        P(("dp", "fsdp"), None, None),
        P(("dp", "fsdp"), None, None),
        P("fsdp"),
        P("fsdp", None),
        P("fsdp", None),
        P("fsdp"),
        P("fsdp", None),
        P("fsdp", None),
        P("fsdp"),
        P("fsdp", None),
        P("fsdp", None),
        P("fsdp", None),
    )
    return jax.shard_map(
        local,
        mesh=mesh,
        in_specs=placed,
        out_specs=(
            P(("dp", "fsdp"), None, None),
            P(("dp", "fsdp"), None, None, None),
            P("fsdp"),
            P("fsdp", None),
            P("fsdp", None),
            P("fsdp"),
            P("fsdp", None),
            P("fsdp", None),
            P("fsdp"),
            P("fsdp", None),
            P("fsdp", None),
            P("fsdp", None),
        ),
        check_vma=False,
    )
```

```python
import functools

import jax
import jax.numpy as jnp
from jax import lax
from jax.experimental import pallas as pl
from jax.experimental.pallas import tpu as pltpu
from jax.sharding import PartitionSpec as P

C = 128
FFH = 512
PLANES = 128
WIN = 8
VIEWS = 4
HV = 16
PIX = HV * HV
TOK = VIEWS * WIN * WIN
HALF = PIX // 2
GAIN_ROWS = 16
MASKED = -1e30
SCALE = C**-0.5
LOG2E = 1.4426950408889634
F32 = jnp.float32
BF16 = jnp.bfloat16
BLOCKS = (3, 1, 3, 1, 4, 4, 9)
MIB = 1024 * 1024


def mm(left, right):
    return lax.dot_general(left, right, (((1,), (0,)), ((), ())), preferred_element_type=F32)


def mm_nt(left, right):
    return lax.dot_general(left, right, (((1,), (1,)), ((), ())), preferred_element_type=F32)


def mm_tn(left, right):
    return lax.dot_general(left, right, (((0,), (0,)), ((), ())), preferred_element_type=F32)


def paired(value):
    half = value.shape[0] // 2
    return jnp.concatenate([value[:half], value[half:]], -1)


def unpaired(value):
    half = value.shape[1] // 2
    return jnp.concatenate([value[:, :half], value[:, half:]], 0)


def norm_forward(value, gain):
    centred = value - jnp.mean(value, -1, keepdims=True)
    spread = jnp.mean(centred * centred, -1, keepdims=True)
    rstd = lax.rsqrt(spread + 1e-05)
    xhat = centred * rstd
    return xhat, jnp.broadcast_to(rstd, value.shape), (xhat * gain).astype(BF16)


def norm_backward(d_normed, xhat, rstd, gain):
    d_xhat = d_normed * gain
    mean_d = jnp.mean(d_xhat, -1, keepdims=True)
    mean_dx = jnp.mean(d_xhat * xhat, -1, keepdims=True)
    d_gain = jnp.sum((d_normed * xhat).reshape(-1, 8, C), 0)
    return rstd * (d_xhat - mean_d - xhat * mean_dx), d_gain


def split_two(value):
    high = value.astype(BF16)
    return jnp.concatenate([high, (value - high.astype(F32)).astype(BF16)], -1)


def iota(shape, axis):
    return lax.broadcasted_iota(jnp.int32, shape, axis)


def bits_of(size):
    return size.bit_length() - 1


def rows_of(parts):
    return -(-(sum(BLOCKS) * (C // parts) + GAIN_ROWS) // 32) * 32


def place_of(parts):
    return lax.axis_index("fsdp").astype(jnp.int32), (lax.axis_index("dp") & 1).astype(jnp.int32)


def gain_lines(parts, gains):
    rows = C // parts
    place = (iota((rows, C), 1) == iota((rows, C), 0) + place_of(parts)[0] * rows).astype(BF16)
    line = iota((GAIN_ROWS, C), 0)
    total = jnp.zeros((GAIN_ROWS, C), F32)
    for which in range(3):
        row = mm(jnp.broadcast_to(gains[which][...], (8, rows)), place)[:1]
        total = jnp.where(line == which, row, total)
    return total


def pack_kernel(parts, *refs):
    gains, weights, out, scratch, sems = refs[:3], refs[3:10], refs[10], refs[11], refs[12]
    rows = C // parts
    copies = []

    def copy(source, target):
        copies.append(pltpu.make_async_copy(source, target, sems.at[len(copies)]))
        copies[-1].start()

    for which in range(3):
        copy(gains[which], scratch.at[which])
    at = 0
    for ref, blocks in zip(weights, BLOCKS):
        if ref.shape[0] == blocks * rows and ref.shape[1] == C:
            copy(ref, out.at[at : at + blocks * rows, :])
        else:
            for block in range(blocks):
                copy(ref.at[:, block * C : (block + 1) * C], out.at[at + block * rows : at + (block + 1) * rows, :])
        at += blocks * rows
    for one in copies[:3]:
        one.wait()
    total = gain_lines(parts, [scratch.at[which] for which in range(3)])
    out[at : at + GAIN_ROWS, :] = total.astype(BF16)
    if at + GAIN_ROWS < out.shape[0]:
        out[at + GAIN_ROWS :, :] = jnp.zeros((out.shape[0] - at - GAIN_ROWS, C), BF16)
    for one in copies[3:]:
        one.wait()


def unpack_kernel(parts, *refs):
    terms = (len(refs) - 11) // 2
    own, other, outs = refs[:terms], refs[terms : 2 * terms], refs[2 * terms :]
    rows = C // parts
    me, side = place_of(parts)
    whole = outs[-1]
    half = own[0].shape[0]
    for first, pieces in ((side, own), (1 - side, other)):
        whole[pl.ds(pl.multiple_of(first * half, 16), half), :] = sum(piece[...].astype(F32) for piece in pieces)
    at = 0
    for out, blocks in zip(outs[3:10], BLOCKS):
        if out.shape[0] == blocks * rows and out.shape[1] == C:
            out[...] = whole[at : at + blocks * rows, :]
        else:
            for block in range(blocks):
                out[:, block * C : (block + 1) * C] = whole[at + block * rows : at + (block + 1) * rows, :]
        at += blocks * rows
    lane = iota((C, rows), 0)
    place = (lane == iota((C, rows), 1) + me * rows).astype(F32)
    picked = lax.dot_general(
        whole[at : at + GAIN_ROWS, :],
        place,
        (((1,), (0,)), ((), ())),
        precision=lax.Precision.HIGHEST,
        preferred_element_type=F32,
    )
    for which in range(3):
        outs[which][...] = picked[which : which + 1]


def merge(*threads, apart=0.0):
    spent = [apart * i for i in range(len(threads))]
    left = set(range(len(threads)))
    while left:
        which = min(left, key=lambda i: (spent[i], i))
        try:
            spent[which] += next(threads[which])
        except StopIteration:
            left.remove(which)


def paced(thread, rate):
    for share in thread:
        yield share * rate


def soft(scores):
    expo = jnp.exp2(scores - jnp.max(scores, -1, keepdims=True))
    return (expo * (1.0 / jnp.sum(expo, -1, keepdims=True))).astype(BF16)


def soft_back(probs, d_probs):
    probs = probs.astype(F32)
    delta = jnp.sum(d_probs * probs, -1, keepdims=True)
    return (probs * ((d_probs - delta) * SCALE)).astype(BF16)


def joined(pieces):
    return jnp.concatenate(pieces, 0)


def main_kernel(
    scenes,
    parts,
    count_ref,
    features_hbm,
    offsets,
    depth_grad,
    *refs,
):
    own_gains, own, packed, refs = refs[:3], refs[3:10], refs[10 : 9 + parts], refs[9 + parts :]
    (
    depth_out,
    grad_hbm,
    keep_out,
    send_out,
    w_sq, w_so, w_cq, w_co, w_fi, w_fo, w_rf,
    t_sq, t_so, t_cq, t_co, t_fi, t_fo, t_rf, b_rf,
    gains,
    bias,
    x0s, x2s,
    xh_a, xh_b, xh_c, rs_a, rs_b, rs_c,
    no_a, no_b, no_c,
    qkv_a, qkv_b, p_a, p_b, o_a, o_b,
    gd, act,
    x3s, d3s,
    low, rev,
    pads, taps, back_taps,
    tables, eye, flip, hots,
    g_sq, g_so, g_cq, g_co, g_fi, g_fo, g_rf, g_gain,
    features, grad_out, sems,
    ) = refs
    rows = C // parts
    me, side_of_rows = place_of(parts)
    bring = pltpu.make_async_copy(features_hbm, features, sems.at[0])
    bring.start()
    sent = []

    total = gain_lines(parts, own_gains)
    for apart in range(parts):
        shard = me ^ apart
        at = 0
        for which, (ref, blocks) in enumerate(zip((w_sq, w_so, w_cq, w_co, w_fi, w_fo, w_rf), BLOCKS)):
            height = blocks * rows if ref is w_fo else rows
            spot = pl.ds(pl.multiple_of(shard * height, 16), height)
            if apart == 0:
                ref[spot, :] = own[which][...]
            elif ref is w_fo:
                ref[spot, :] = packed[apart - 1][at : at + height, :]
            else:
                for block in range(blocks):
                    ref[spot, block * C : (block + 1) * C] = packed[apart - 1][
                        at + block * rows : at + (block + 1) * rows, :
                    ]
            at += blocks * rows
        if apart > 0:
            total = total + packed[apart - 1][at : at + GAIN_ROWS, :].astype(F32)
    gains[...] = total[:8]
    for source, target in ((w_sq, t_sq), (w_so, t_so), (w_cq, t_cq), (w_co, t_co)):
        for block in range(source.shape[1] // C):
            target[block * C : (block + 1) * C, :] = source[:, block * C : (block + 1) * C].T
    for block in range(FFH // C):
        t_fi[block * C : (block + 1) * C, :] = w_fi[:, block * C : (block + 1) * C].T
        t_fo[:, block * C : (block + 1) * C] = w_fo[block * C : (block + 1) * C, :].T
    for tap in range(9):
        block = w_rf[:, tap * C : (tap + 1) * C]
        for ref, piece, at in ((t_rf, block.T, tap), (b_rf, block, 3 * (2 - tap // 3) + tap % 3)):
            ref[at * C : (at + 1) * C, :C] = piece
            ref[(at + 3) * C : (at + 4) * C, C:] = piece
    for ref in (t_rf, b_rf):
        ref[9 * C :, :C] = jnp.zeros((3 * C, C), BF16)
        ref[: 3 * C, C:] = jnp.zeros((3 * C, C), BF16)

    for ref in (g_sq, g_so, g_cq, g_co, g_fi, g_fo, g_rf, g_gain, pads, hots):
        ref[...] = jnp.zeros_like(ref)
    for ref in (taps, back_taps):
        for scene in range(scenes):
            ref[scene, :, :HV, :] = jnp.zeros((VIEWS, HV, 3 * C), BF16)
            ref[scene, :, HV + PIX :, :] = jnp.zeros((VIEWS, HV, 3 * C), BF16)

    row = iota((HV, C), 0)
    lane = iota((HV, C), 1)
    tables[0:HV, :] = jnp.where((lane < HV) & (lane <= row), 0.5 * SCALE, 0.0)
    tables[HV : 2 * HV, :] = jnp.where((lane < HV) & (HV - 1 - lane <= row), 0.5 * SCALE, 0.0)
    tables[2 * HV : 3 * HV, :] = jnp.where(row > 0, 1.0, 0.0)
    tables[3 * HV : 4 * HV, :] = jnp.where(row < HV - 1, 1.0, 0.0)
    eye[...] = jnp.where(iota((HALF, HALF), 0) == iota((HALF, HALF), 1), 1.0, 0.0)
    flip[...] = (iota((HALF, HALF), 0) + iota((HALF, HALF), 1) == HALF - 1).astype(BF16)
    of_key = iota((TOK, TOK), 1) // (WIN * WIN)
    of_query = iota((TOK, TOK), 0) // (WIN * WIN)
    for scene in range(scenes):
        live = count_ref[scene]
        bias[scene] = jnp.where((of_key < live) & (of_key != of_query), 0.0, MASKED)

    gain_a = gains[0:1, :]
    gain_b = gains[1:2, :]
    gain_c = gains[2:3, :]
    depth_values = 1.0 + 3.0 * iota((1, PLANES), 1).astype(F32) / (PLANES - 1)
    upper = [slice(part * HALF, (part + 1) * HALF) for part in range(2)]
    views = range(VIEWS)
    places = [slice(side * TOK, (side + 1) * TOK) for side in range(2)]
    windows = [slice(at * WIN * WIN, (at + 1) * WIN * WIN) for at in range(2 * VIEWS)]

    def attend(scene, half, side):
        step = 2 * scene + half
        spot = places[side]
        if side == 0:
            piece = features[scene, :, half * HALF : (half + 1) * HALF, :]
            x0s[step] = piece.astype(F32).reshape(VIEWS, WIN, 2, WIN, C)
            yield 60
        x0 = x0s[step, :, :, side].reshape(TOK, C)
        xhat, rstd, normed = norm_forward(x0, gain_a)
        xh_a[step, spot, :] = xhat
        rs_a[step, spot, :] = rstd
        no_a[step, spot, :] = normed
        yield 400
        qkv = mm(normed, w_sq[...]).astype(BF16)
        qkv_a[step, spot, :] = qkv
        yield 300
        scores = joined([mm_nt(qkv[at, :C], qkv[at, C : 2 * C]) for at in windows[:VIEWS]])
        yield 200
        probs = soft(scores * (SCALE * LOG2E))
        p_a[step, spot, :] = probs
        yield 400
        mixed = joined([mm(probs[at], qkv[at, 2 * C :]) for at in windows[:VIEWS]]).astype(BF16)
        o_a[step, spot, :] = mixed
        yield 300
        x1 = x0 + mm(mixed, w_so[...])
        yield 200
        xhat, rstd, normed = norm_forward(x1, gain_b)
        xh_b[step, spot, :] = xhat
        rs_b[step, spot, :] = rstd
        no_b[step, spot, :] = normed
        yield 400
        qkv = mm(normed, w_cq[...]).astype(BF16)
        qkv_b[step, spot, :] = qkv
        yield 300
        scores = mm_nt(qkv[:, :C], qkv[:, C : 2 * C]) * (SCALE * LOG2E) + bias[scene]
        yield 300
        probs = soft(scores)
        p_b[step, spot, :] = probs
        yield 500
        mixed = mm(probs, qkv[:, 2 * C :]).astype(BF16)
        o_b[step, spot, :] = mixed
        yield 300
        x2 = x1 + mm(mixed, w_co[...])
        x2s[step, spot, :] = x2
        yield 200
        xhat, rstd, normed = norm_forward(x2, gain_c)
        xh_c[step, spot, :] = xhat
        rs_c[step, spot, :] = rstd
        no_c[step, spot, :] = normed
        yield 400

    def feed(scene, half):
        step = 2 * scene + half
        for block in range(FFH // C):
            cols = slice(block * C, (block + 1) * C)
            for at in places:
                inner = mm(no_c[step, at, :], w_fi[:, cols])
                cdf = 0.5 + 0.5 * lax.erf(inner * 0.5**0.5)
                bell = jnp.exp2(inner * inner * (-0.5 * LOG2E))
                gd[step, at, cols] = cdf + inner * bell * 0.3989422804014327
                act[step, at, cols] = (inner * cdf).astype(BF16)
                yield 100
        x3 = x2s[step] + mm(act[step], w_fo[...])
        for side in range(2):
            x3s[scene, :, half, :, side] = x3[places[side]].reshape(VIEWS, WIN, WIN, C)
        yield 300

    def by_row(value, table):
        return (value.reshape(-1, HV, C) * table).reshape(value.shape)

    def im2col(value, pad, dest, first, last):
        pad[8 : 8 + PIX, :] = value
        dest[HV : HV + PIX, C : 2 * C] = value.astype(BF16)
        before = by_row(pad[7 : 7 + PIX, :], tables[2 * HV : 3 * HV, :])
        after = by_row(pad[9 : 9 + PIX, :], tables[3 * HV : 4 * HV, :])
        dest[HV : HV + PIX, first * C : (first + 1) * C] = before.astype(BF16)
        dest[HV : HV + PIX, last * C : (last + 1) * C] = after.astype(BF16)

    def convolve(padded, kernel):
        rows_two = padded.reshape(HV // 2 + 1, 2, HV, 3 * C)
        columns = jnp.concatenate(
            [rows_two[a // 2 : a // 2 + HV // 2, a % 2].reshape(HALF, 3 * C) for a in range(4)], -1
        )
        both = mm(columns, kernel[...])
        return joined(
            [both[HV * (y // 2) : HV * (y // 2 + 1), C * (y % 2) : C * (y % 2 + 1)] for y in range(HV)]
        )

    def head(scene):
        live = count_ref[scene]
        goes_on = {1: live > 2, 2: live > 3}

        def partner_of(ref, view, at):
            if view in goes_on:
                return jnp.where(goes_on[view], ref[scene, view + 1, at, :], ref[scene, 0, at, :])
            return ref[scene, (view + 1) % VIEWS, at, :]

        for view in views:
            low[scene, view] = x3s[scene, view].reshape(PIX, C).astype(BF16)
            shift = offsets[scene, view : view + 1, :]
            hots[scene, 0, view, 0:HV, :] = (shift == row).astype(BF16)
            hots[scene, 0, view, C : C + HV, :] = (shift == row).astype(BF16)
            hots[scene, 1, view, 0:HV, :] = (shift == HV - 1 - row).astype(BF16)
        yield 300
        for view in views:
            rev[scene, view] = unpaired(mm(flip[...], paired(low[scene, view])).astype(BF16))
        yield 400
        corrs = [[mm_nt(low[scene, view, at, :], partner_of(rev, view, at)) for at in upper] for view in views]
        yield 400
        skewed = [
            [by_row(pltpu.roll(corr, 1, 1, stride=1, stride_axis=0), tables[0:HV, :]) for corr in corrs[view]]
            for view in views
        ]
        yield 500
        cost = [mm(split_two(joined(skewed[view])), hots[scene, 0, view]) for view in views]
        yield 500
        for view in views:
            im2col(cost[view], pads.at[scene, 0, view], taps.at[scene, view], 0, 2)
            yield 80
        refined = []
        for view in views:
            refined.append(cost[view] + convolve(taps[scene, view], t_rf))
            yield 250
        d_refined = []
        for view in views:
            expo = jnp.exp2((refined[view] - jnp.max(refined[view], -1, keepdims=True)) * LOG2E)
            inverse = 1.0 / jnp.sum(expo, -1, keepdims=True)
            depth = jnp.sum(expo * depth_values, -1, keepdims=True) * inverse
            valid = jnp.where(view < live, 1.0, 0.0)
            incoming = []
            for at in upper:
                depth_out[scene, view : view + 1, at] = jnp.sum(eye[...] * depth[at], 0, keepdims=True) * valid
                incoming.append(jnp.sum(eye[...] * depth_grad[scene, view : view + 1, at], 1, keepdims=True))
            weight = joined(incoming) * (inverse * valid)
            d_refined.append(expo * (weight * depth_values - weight * depth))
            yield 250
        for view in views:
            im2col(d_refined[view], pads.at[scene, 1, view], back_taps.at[scene, view], 2, 0)
            yield 80
        d_cost = []
        for view in views:
            d_cost.append(d_refined[view] + convolve(back_taps[scene, view], b_rf))
            yield 250
        for view in views:
            columns = jnp.concatenate([taps[scene, view, HV * a : HV * a + PIX, :] for a in range(3)], -1)
            g_rf[...] += mm_tn(back_taps[scene, view, HV : HV + PIX, C : 2 * C], columns)
            yield 250
        d_skewed = [
            mm_nt(split_two(d_cost[view]), jnp.concatenate([hots[scene, 1, view, :C, :]] * 2, -1)) for view in views
        ]
        yield 300
        d_corr = [
            [
                pltpu.roll(
                    by_row(d_skewed[view][at], tables[HV : 2 * HV, :]), HALF - HV + 1, 1, stride=1, stride_axis=0
                ).astype(BF16)
                for at in upper
            ]
            for view in views
        ]
        yield 250
        for part in range(2):
            at = upper[part]
            total = [mm(d_corr[view][part], partner_of(low, view, at)) for view in views]
            for view in views:
                there = mm_tn(d_corr[view][part], low[scene, view, at, :])
                if view in goes_on:
                    total[view + 1] = total[view + 1] + jnp.where(goes_on[view], there, 0.0)
                    total[0] = total[0] + jnp.where(goes_on[view], 0.0, there)
                else:
                    total[(view + 1) % VIEWS] = total[(view + 1) % VIEWS] + there
            for view in views:
                d3s[scene, view, part] = total[view].reshape(WIN, 2, WIN, C)
            yield 250

    def back(scene, half):
        step = 2 * scene + half
        both = range(2)
        d3 = [d3s[scene, :, half, :, side].reshape(TOK, C) for side in both]
        d_low = [d3[side].astype(BF16) for side in both]
        d_inner = [[], []]
        for block in range(FFH // C):
            cols = slice(block * C, (block + 1) * C)
            for side in both:
                d_inner[side].append((mm(d_low[side], t_fo[:, cols]) * gd[step, places[side], cols]).astype(BF16))
            yield 100
        d_inner = [jnp.concatenate(d_inner[side], -1) for side in both]
        d_normed = []
        for side in both:
            d_normed.append(mm(d_inner[side], t_fi[...]))
            yield 150
        g_fo[...] += mm_tn(joined(d_low), act[step])
        yield 250
        g_fi[...] += mm_tn(no_c[step], joined(d_inner))
        yield 250
        d2 = []
        for side in both:
            spot = places[side]
            d_hidden, d_gain = norm_backward(d_normed[side], xh_c[step, spot, :], rs_c[step, spot, :], gain_c)
            g_gain[2] += d_gain
            d2.append(d3[side] + d_hidden)
            yield 150
        d_low = [d2[side].astype(BF16) for side in both]
        qkv = [qkv_b[step, spot, :] for spot in places]
        d_mixed = []
        for side in both:
            d_mixed.append(mm(d_low[side], t_co[...]).astype(BF16))
            yield 100
        g_co[...] += mm_tn(o_b[step], joined(d_low))
        yield 100
        d_packed = [[], []]
        d_raw = []
        for side in both:
            probs = p_b[step, places[side], :]
            d_values = mm_tn(probs, d_mixed[side])
            d_probs = mm_nt(d_mixed[side], qkv[side][:, 2 * C :])
            yield 150
            d_raw.append(soft_back(probs, d_probs))
            d_packed[side].append(d_values)
            yield 150
        for side in both:
            d_query = mm(d_raw[side], qkv[side][:, C : 2 * C])
            d_keys = mm_tn(d_raw[side], qkv[side][:, :C])
            d_packed[side] = jnp.concatenate([d_query, d_keys] + d_packed[side], -1).astype(BF16)
            yield 200
        d_normed = []
        for side in both:
            d_normed.append(mm(d_packed[side], t_cq[...]))
            yield 100
        g_cq[...] += mm_tn(no_b[step], joined(d_packed))
        yield 200
        d1 = []
        for side in both:
            spot = places[side]
            d_hidden, d_gain = norm_backward(d_normed[side], xh_b[step, spot, :], rs_b[step, spot, :], gain_b)
            g_gain[1] += d_gain
            d1.append(d2[side] + d_hidden)
            yield 150
        d_low = [d1[side].astype(BF16) for side in both]
        qkv = [qkv_a[step, spot, :] for spot in places]
        d_mixed = []
        for side in both:
            d_mixed.append(mm(d_low[side], t_so[...]).astype(BF16))
            yield 100
        g_so[...] += mm_tn(o_a[step], joined(d_low))
        yield 100
        d_packed = [[], []]
        d_raw = []
        for side in both:
            probs = p_a[step, places[side], :]
            d_values = joined([mm_tn(probs[at], d_mixed[side][at]) for at in windows[:VIEWS]])
            d_probs = joined([mm_nt(d_mixed[side][at], qkv[side][at, 2 * C :]) for at in windows[:VIEWS]])
            yield 150
            d_raw.append(soft_back(probs, d_probs))
            d_packed[side].append(d_values)
            yield 100
        for side in both:
            d_query = joined([mm(d_raw[side][at], qkv[side][at, C : 2 * C]) for at in windows[:VIEWS]])
            d_keys = joined([mm_tn(d_raw[side][at], qkv[side][at, :C]) for at in windows[:VIEWS]])
            d_packed[side] = jnp.concatenate([d_query, d_keys] + d_packed[side], -1).astype(BF16)
            yield 150
        d_normed = []
        for side in both:
            d_normed.append(mm(d_packed[side], t_sq[...]))
            yield 100
        g_sq[...] += mm_tn(no_a[step], joined(d_packed))
        yield 200
        for side in both:
            spot = places[side]
            d_hidden, d_gain = norm_backward(d_normed[side], xh_a[step, spot, :], rs_a[step, spot, :], gain_a)
            g_gain[0] += d_gain
            grad_out[scene, :, half, :, side] = (d1[side] + d_hidden).reshape(VIEWS, WIN, WIN, C)
            yield 150
        sent.append(
            pltpu.make_async_copy(grad_out.at[scene, :, half], grad_hbm.at[scene, :, half], sems.at[1 + step])
        )
        sent[-1].start()

    def chain(*threads):
        for thread in threads:
            yield from thread

    def feeds(scene):
        return chain(feed(scene, 0), feed(scene, 1))

    bring.wait()
    def whole_of(thread, total):
        return paced(thread, 1.0 / total)

    def attends(scene):
        return [whole_of(attend(scene, half, side), 4200) for half in range(2) for side in range(2)]

    def feeds(scene):
        return whole_of(chain(feed(scene, 0), feed(scene, 1)), 2200)

    def backs(*which):
        return [whole_of(back(*one), 5400) for one in which]

    merge(*attends(0), *attends(1), apart=0.02)
    merge(feeds(0), feeds(1))
    merge(whole_of(head(0), 7600), whole_of(head(1), 7600), apart=0.05)
    merge(*backs((0, 0), (0, 1), (1, 0), (1, 1)), apart=0.04)

    bits = bits_of(parts)
    line = iota((GAIN_ROWS, C), 0)
    gain_rows = jnp.zeros((GAIN_ROWS, C), F32)
    for which in range(3):
        gain_rows = jnp.where(line == which, jnp.sum(g_gain[which], 0, keepdims=True), gain_rows)
    gain_rows = gain_rows.astype(BF16)
    for block in range(FFH // C):
        w_fo[block * C : (block + 1) * C, :] = g_fo[:, block * C : (block + 1) * C].T.astype(BF16)
    half_rows = rows_of(parts) // 2
    first = side_of_rows
    for apart in range(parts):
        shard = me ^ apart
        slot = sum(((apart >> bit) & 1) << (bits - 1 - bit) for bit in range(bits))
        dest = (keep_out, send_out)[slot // (parts // 2)].at[slot % (parts // 2)]

        def put(at, value):
            height = value.shape[0]
            which, offset = divmod(at, half_rows)
            assert offset + height <= half_rows
            dest[pl.ds(pl.multiple_of((first ^ which) * half_rows + offset, 16), height), :] = value

        at = 0
        for ref, blocks in zip((g_sq, g_so, g_cq, g_co, g_fi, w_fo, g_rf), BLOCKS):
            for block in range(blocks):
                if ref is w_fo:
                    spot = pl.ds(pl.multiple_of(shard * (blocks * rows) + block * rows, 16), rows)
                    put(at, ref[spot, :])
                else:
                    spot = pl.ds(pl.multiple_of(shard * rows, 16), rows)
                    put(at, ref[spot, block * C : (block + 1) * C].astype(BF16))
                at += rows
        put(at, gain_rows)
        if at + GAIN_ROWS < rows_of(parts):
            put(at + GAIN_ROWS, jnp.zeros((rows_of(parts) - at - GAIN_ROWS, C), BF16))
    for one in sent:
        one.wait()


VMEM = pl.BlockSpec(memory_space=pltpu.VMEM)
HBM = pl.BlockSpec(memory_space=pltpu.HBM)
SMEM = pl.BlockSpec(memory_space=pltpu.SMEM)


def exchange(value, fsdp_mask, dp_mask):
    parts = lax.axis_size("fsdp")
    count = parts * lax.axis_size("dp")
    mask = dp_mask * parts + fsdp_mask
    return lax.ppermute(value, ("dp", "fsdp"), [(i, i ^ mask) for i in range(count)])


def local(
    features,
    view_count,
    plane_offsets,
    depth_grad,
    gain_self,
    self_qkv,
    self_out,
    gain_cross,
    cross_qkv,
    cross_out,
    gain_ff,
    ff_in,
    ff_out,
    refine,
):
    parts = lax.axis_size("fsdp")
    copies = lax.axis_size("dp")
    scenes = features.shape[0]
    rows = C // parts
    shard_rows = rows_of(parts)
    small = pltpu.CompilerParams(vmem_limit_bytes=8 * MIB)

    pack = pl.pallas_call(
        functools.partial(pack_kernel, parts),
        out_shape=jax.ShapeDtypeStruct((shard_rows, C), BF16),
        in_specs=[HBM] * 10,
        out_specs=VMEM,
        scratch_shapes=[pltpu.VMEM((3, 1, rows), BF16), pltpu.SemaphoreType.DMA((3 + sum(BLOCKS),))],
        compiler_params=pltpu.CompilerParams(vmem_limit_bytes=60 * MIB),
        name="pack",
    )
    own = [gain.reshape(1, rows) for gain in (gain_self, gain_cross, gain_ff)]
    own += [self_qkv, self_out, cross_qkv, cross_out, ff_in, ff_out, refine]
    shard = pack(*own)
    packed = {0: shard}
    for bit in reversed(range(bits_of(parts))):
        packed |= {apart | (1 << bit): exchange(piece, 1 << bit, 0) for apart, piece in packed.items()}
    packed = [packed[apart] for apart in range(1, parts)]

    steps = scenes * (HV // WIN)
    span = 2 * TOK
    scratch = [
        ((C, 3 * C), BF16), ((C, C), BF16), ((C, 3 * C), BF16), ((C, C), BF16),
        ((C, FFH), BF16), ((FFH, C), BF16), ((C, 9 * PLANES), BF16),
        ((3 * C, C), BF16), ((C, C), BF16), ((3 * C, C), BF16), ((C, C), BF16),
        ((FFH, C), BF16), ((C, FFH), BF16), ((12 * PLANES, 2 * C), BF16), ((12 * PLANES, 2 * C), BF16),
        ((8, C), F32),
        ((scenes, TOK, TOK), F32),
        ((steps, VIEWS, WIN, 2, WIN, C), F32),
        ((steps, span, C), F32),
    ]
    scratch += [((steps, span, C), F32)] * 6
    scratch += [((steps, span, C), BF16)] * 3
    scratch += [
        ((steps, span, 3 * C), BF16), ((steps, span, 3 * C), BF16),
        ((steps, span, WIN * WIN), BF16), ((steps, span, TOK), BF16),
        ((steps, span, C), BF16), ((steps, span, C), BF16),
        ((steps, span, FFH), F32), ((steps, span, FFH), BF16),
        ((scenes, VIEWS, 2, WIN, 2, WIN, C), F32), ((scenes, VIEWS, 2, WIN, 2, WIN, C), F32),
        ((scenes, VIEWS, PIX, C), BF16), ((scenes, VIEWS, PIX, C), BF16),
        ((scenes, 2, VIEWS, PIX + 16, C), F32),
        ((scenes, VIEWS, PIX + 2 * HV, 3 * C), BF16), ((scenes, VIEWS, PIX + 2 * HV, 3 * C), BF16),
        ((4 * HV, C), F32), ((HALF, HALF), F32), ((HALF, HALF), BF16), ((scenes, 2, VIEWS, 2 * C, C), BF16),
        ((C, 3 * C), F32), ((C, C), F32), ((C, 3 * C), F32), ((C, C), F32),
        ((C, FFH), F32), ((C, FFH), F32), ((C, 9 * PLANES), F32), ((3, 8, C), F32),
    ]
    main = pl.pallas_call(
        functools.partial(main_kernel, scenes, parts),
        out_shape=(
            jax.ShapeDtypeStruct((scenes, VIEWS, PIX), F32),
            jax.ShapeDtypeStruct((scenes, VIEWS, 2, WIN, 2, WIN, C), F32),
            jax.ShapeDtypeStruct((parts // 2, shard_rows, C), BF16),
            jax.ShapeDtypeStruct((parts // 2, shard_rows, C), BF16),
        ),
        in_specs=[SMEM, HBM] + [VMEM] * (11 + parts),
        out_specs=(VMEM, HBM, VMEM, VMEM),
        scratch_shapes=[pltpu.VMEM(shape, kind) for shape, kind in scratch]
        + [
            pltpu.VMEM(features.shape, BF16),
            pltpu.VMEM((scenes, VIEWS, 2, WIN, 2, WIN, C), F32),
            pltpu.SemaphoreType.DMA((1 + steps,)),
        ],
        compiler_params=pltpu.CompilerParams(vmem_limit_bytes=52 * MIB),
        name="layer",
    )
    depth, grad_features, keep, send = main(view_count, features, plane_offsets, depth_grad, *own, *packed)

    for bit in range(bits_of(parts)):
        if bit > 0:
            keep, send = keep[: keep.shape[0] // 2], keep[keep.shape[0] // 2 :]
        if bit < bits_of(parts) - 1:
            keep = keep + exchange(send, 1 << bit, 0)
    last = parts // 2
    half = shard_rows // 2
    beside = exchange(send[0, :half], last, 0)
    across = exchange(keep[0, half:], 0, 1)
    corner = exchange(send[0, half:], last, 1)
    grads = (keep[0, :half].astype(F32) + beside) + (across.astype(F32) + corner)
    grads = grads.astype(BF16)
    for bit in reversed(range(2, bits_of(copies))):
        grads = grads + exchange(grads, 0, 1 << bit)
    if bits_of(copies) > 1:
        along = exchange(grads, 0, 2)
        swapped = exchange(grads, 0, 1)
        corner = exchange(grads, 0, 3)
        own, other = (grads, along), (swapped, corner)
    else:
        own, other = (grads,), (exchange(grads, 0, 1),)

    unpack = pl.pallas_call(
        functools.partial(unpack_kernel, parts),
        out_shape=tuple(jax.ShapeDtypeStruct((1, rows), F32) for _ in range(3))
        + tuple(
            jax.ShapeDtypeStruct(piece.shape, F32)
            for piece in (self_qkv, self_out, cross_qkv, cross_out, ff_in, ff_out, refine)
        ),
        in_specs=[VMEM] * (2 * len(own)),
        out_specs=(VMEM,) * 10,
        scratch_shapes=[pltpu.VMEM((shard_rows, C), F32)],
        compiler_params=small,
        name="unpack",
    )
    ga, gb, gc, d_sq, d_so, d_cq, d_co, d_fi, d_fo, d_rf = unpack(*own, *other)
    return (
        depth,
        grad_features.reshape(features.shape),
        ga.reshape(rows),
        d_sq,
        d_so,
        gb.reshape(rows),
        d_cq,
        d_co,
        gc.reshape(rows),
        d_fi,
        d_fo,
        d_rf,
    )


def solution(mesh):
    placed = (
        P(("dp", "fsdp"), None, None, None),
        P(("dp", "fsdp")),
        P(("dp", "fsdp"), None, None),
        P(("dp", "fsdp"), None, None),
        P("fsdp"),
        P("fsdp", None),
        P("fsdp", None),
        P("fsdp"),
        P("fsdp", None),
        P("fsdp", None),
        P("fsdp"),
        P("fsdp", None),
        P("fsdp", None),
        P("fsdp", None),
    )
    return jax.shard_map(
        local,
        mesh=mesh,
        in_specs=placed,
        out_specs=(
            P(("dp", "fsdp"), None, None),
            P(("dp", "fsdp"), None, None, None),
            P("fsdp"),
            P("fsdp", None),
            P("fsdp", None),
            P("fsdp"),
            P("fsdp", None),
            P("fsdp", None),
            P("fsdp"),
            P("fsdp", None),
            P("fsdp", None),
            P("fsdp", None),
        ),
        check_vma=False,
    )
```

```python
import functools

import jax
import jax.numpy as jnp
from jax import lax
from jax.experimental import pallas as pl
from jax.experimental.pallas import tpu as pltpu
from jax.sharding import PartitionSpec as P

C = 128
FFH = 512
PLANES = 128
WIN = 8
VIEWS = 4
HV = 16
PIX = HV * HV
TOK = VIEWS * WIN * WIN
HALF = PIX // 2
GAIN_ROWS = 16
MASKED = -1e30
SCALE = C**-0.5
LOG2E = 1.4426950408889634
F32 = jnp.float32
BF16 = jnp.bfloat16
BLOCKS = (3, 1, 3, 1, 4, 4, 9)
MIB = 1024 * 1024


def mm(left, right):
    return lax.dot_general(left, right, (((1,), (0,)), ((), ())), preferred_element_type=F32)


def mm_nt(left, right):
    return lax.dot_general(left, right, (((1,), (1,)), ((), ())), preferred_element_type=F32)


def mm_tn(left, right):
    return lax.dot_general(left, right, (((0,), (0,)), ((), ())), preferred_element_type=F32)


def paired(value):
    half = value.shape[0] // 2
    return jnp.concatenate([value[:half], value[half:]], -1)


def unpaired(value):
    half = value.shape[1] // 2
    return jnp.concatenate([value[:, :half], value[:, half:]], 0)


def norm_forward(value, gain):
    centred = value - jnp.mean(value, -1, keepdims=True)
    spread = jnp.mean(centred * centred, -1, keepdims=True)
    rstd = lax.rsqrt(spread + 1e-05)
    xhat = centred * rstd
    return xhat, jnp.broadcast_to(rstd, value.shape), (xhat * gain).astype(BF16)


def norm_backward(d_normed, xhat, rstd, gain):
    d_xhat = d_normed * gain
    mean_d = jnp.mean(d_xhat, -1, keepdims=True)
    mean_dx = jnp.mean(d_xhat * xhat, -1, keepdims=True)
    d_gain = jnp.sum((d_normed * xhat).reshape(-1, 8, C), 0)
    return rstd * (d_xhat - mean_d - xhat * mean_dx), d_gain


def split_two(value):
    high = value.astype(BF16)
    return jnp.concatenate([high, (value - high.astype(F32)).astype(BF16)], -1)


def iota(shape, axis):
    return lax.broadcasted_iota(jnp.int32, shape, axis)


def bits_of(size):
    return size.bit_length() - 1


def rows_of(parts):
    return -(-(sum(BLOCKS) * (C // parts) + GAIN_ROWS) // 32) * 32


def place_of(parts):
    return lax.axis_index("fsdp").astype(jnp.int32), (lax.axis_index("dp") & 1).astype(jnp.int32)


def gain_lines(parts, gains):
    rows = C // parts
    place = (iota((rows, C), 1) == iota((rows, C), 0) + place_of(parts)[0] * rows).astype(BF16)
    line = iota((GAIN_ROWS, C), 0)
    total = jnp.zeros((GAIN_ROWS, C), F32)
    for which in range(3):
        row = mm(jnp.broadcast_to(gains[which][...], (8, rows)), place)[:1]
        total = jnp.where(line == which, row, total)
    return total


def pack_kernel(parts, *refs):
    gains, weights, out, scratch, sems = refs[:3], refs[3:10], refs[10], refs[11], refs[12]
    rows = C // parts
    copies = []

    def copy(source, target):
        copies.append(pltpu.make_async_copy(source, target, sems.at[len(copies)]))
        copies[-1].start()

    for which in range(3):
        copy(gains[which], scratch.at[which])
    at = 0
    for ref, blocks in zip(weights, BLOCKS):
        if ref.shape[0] == blocks * rows and ref.shape[1] == C:
            copy(ref, out.at[at : at + blocks * rows, :])
        else:
            for block in range(blocks):
                copy(ref.at[:, block * C : (block + 1) * C], out.at[at + block * rows : at + (block + 1) * rows, :])
        at += blocks * rows
    for one in copies[:3]:
        one.wait()
    total = gain_lines(parts, [scratch.at[which] for which in range(3)])
    out[at : at + GAIN_ROWS, :] = total.astype(BF16)
    if at + GAIN_ROWS < out.shape[0]:
        out[at + GAIN_ROWS :, :] = jnp.zeros((out.shape[0] - at - GAIN_ROWS, C), BF16)
    for one in copies[3:]:
        one.wait()


def unpack_kernel(parts, *refs):
    terms = (len(refs) - 11) // 2
    own, other, outs = refs[:terms], refs[terms : 2 * terms], refs[2 * terms :]
    rows = C // parts
    me, side = place_of(parts)
    whole = outs[-1]
    half = own[0].shape[0]
    for first, pieces in ((side, own), (1 - side, other)):
        whole[pl.ds(pl.multiple_of(first * half, 16), half), :] = sum(piece[...].astype(F32) for piece in pieces)
    at = 0
    for out, blocks in zip(outs[3:10], BLOCKS):
        if out.shape[0] == blocks * rows and out.shape[1] == C:
            out[...] = whole[at : at + blocks * rows, :]
        else:
            for block in range(blocks):
                out[:, block * C : (block + 1) * C] = whole[at + block * rows : at + (block + 1) * rows, :]
        at += blocks * rows
    lane = iota((C, rows), 0)
    place = (lane == iota((C, rows), 1) + me * rows).astype(F32)
    picked = lax.dot_general(
        whole[at : at + GAIN_ROWS, :],
        place,
        (((1,), (0,)), ((), ())),
        precision=lax.Precision.HIGHEST,
        preferred_element_type=F32,
    )
    for which in range(3):
        outs[which][...] = picked[which : which + 1]


def merge(*threads, apart=0.0):
    spent = [apart * i for i in range(len(threads))]
    left = set(range(len(threads)))
    while left:
        which = min(left, key=lambda i: (spent[i], i))
        try:
            spent[which] += next(threads[which])
        except StopIteration:
            left.remove(which)


def paced(thread, rate):
    for share in thread:
        yield share * rate


def soft(scores):
    expo = jnp.exp2(scores - jnp.max(scores, -1, keepdims=True))
    return (expo * (1.0 / jnp.sum(expo, -1, keepdims=True))).astype(BF16)


def soft_back(probs, d_probs):
    probs = probs.astype(F32)
    delta = jnp.sum(d_probs * probs, -1, keepdims=True)
    return (probs * ((d_probs - delta) * SCALE)).astype(BF16)


def joined(pieces):
    return jnp.concatenate(pieces, 0)


def start_kernel(scenes, features, x0s, xhats, rstds):
    for scene in range(scenes):
        for half in range(2):
            step = 2 * scene + half
            piece = features[scene, :, half * HALF : (half + 1) * HALF, :]
            piece = piece.astype(F32).reshape(VIEWS, WIN, 2, WIN, C)
            for side in range(2):
                spot = slice(side * TOK, (side + 1) * TOK)
                x0 = piece[:, :, side].reshape(TOK, C)
                centred = x0 - jnp.mean(x0, -1, keepdims=True)
                spread = jnp.mean(centred * centred, -1, keepdims=True)
                rstd = lax.rsqrt(spread + 1e-05)
                x0s[step, spot, :] = x0
                xhats[step, spot, :] = centred * rstd
                rstds[step, spot, :] = jnp.broadcast_to(rstd, x0.shape)


def main_kernel(
    scenes,
    parts,
    count_ref,
    x0s,
    xh_a,
    rs_a,
    offsets,
    depth_grad,
    *refs,
):
    own_gains, own, packed, refs = refs[:3], refs[3:10], refs[10 : 9 + parts], refs[9 + parts :]
    (
    depth_out,
    grad_out,
    keep_out,
    send_out,
    w_sq, w_so, w_cq, w_co, w_fi, w_fo, w_rf,
    t_sq, t_so, t_cq, t_co, t_fi, t_fo, t_rf, b_rf,
    gains,
    bias,
    x2s,
    xh_b, xh_c, rs_b, rs_c,
    no_a, no_b, no_c,
    qkv_a, qkv_b, p_a, p_b, o_a, o_b,
    gd, act,
    x3s, d3s,
    low, rev,
    pads, taps, back_taps,
    tables, eye, flip, hots,
    g_sq, g_so, g_cq, g_co, g_fi, g_fo, g_rf, g_gain,
    ) = refs
    rows = C // parts
    me, side_of_rows = place_of(parts)

    total = gain_lines(parts, own_gains)
    for apart in range(parts):
        shard = me ^ apart
        at = 0
        for which, (ref, blocks) in enumerate(zip((w_sq, w_so, w_cq, w_co, w_fi, w_fo, w_rf), BLOCKS)):
            height = blocks * rows if ref is w_fo else rows
            spot = pl.ds(pl.multiple_of(shard * height, 16), height)
            if apart == 0:
                ref[spot, :] = own[which][...]
            elif ref is w_fo:
                ref[spot, :] = packed[apart - 1][at : at + height, :]
            else:
                for block in range(blocks):
                    ref[spot, block * C : (block + 1) * C] = packed[apart - 1][
                        at + block * rows : at + (block + 1) * rows, :
                    ]
            at += blocks * rows
        if apart > 0:
            total = total + packed[apart - 1][at : at + GAIN_ROWS, :].astype(F32)
    gains[...] = total[:8]
    for source, target in ((w_sq, t_sq), (w_so, t_so), (w_cq, t_cq), (w_co, t_co)):
        for block in range(source.shape[1] // C):
            target[block * C : (block + 1) * C, :] = source[:, block * C : (block + 1) * C].T
    for block in range(FFH // C):
        t_fi[block * C : (block + 1) * C, :] = w_fi[:, block * C : (block + 1) * C].T
        t_fo[:, block * C : (block + 1) * C] = w_fo[block * C : (block + 1) * C, :].T
    for tap in range(9):
        block = w_rf[:, tap * C : (tap + 1) * C]
        for ref, piece, at in ((t_rf, block.T, tap), (b_rf, block, 3 * (2 - tap // 3) + tap % 3)):
            ref[at * C : (at + 1) * C, :C] = piece
            ref[(at + 3) * C : (at + 4) * C, C:] = piece
    for ref in (t_rf, b_rf):
        ref[9 * C :, :C] = jnp.zeros((3 * C, C), BF16)
        ref[: 3 * C, C:] = jnp.zeros((3 * C, C), BF16)

    for ref in (g_sq, g_so, g_cq, g_co, g_fi, g_fo, g_rf, g_gain, pads, hots):
        ref[...] = jnp.zeros_like(ref)
    for ref in (taps, back_taps):
        for scene in range(scenes):
            ref[scene, :, :HV, :] = jnp.zeros((VIEWS, HV, 3 * C), BF16)
            ref[scene, :, HV + PIX :, :] = jnp.zeros((VIEWS, HV, 3 * C), BF16)

    row = iota((HV, C), 0)
    lane = iota((HV, C), 1)
    tables[0:HV, :] = jnp.where((lane < HV) & (lane <= row), 0.5 * SCALE, 0.0)
    tables[HV : 2 * HV, :] = jnp.where((lane < HV) & (HV - 1 - lane <= row), 0.5 * SCALE, 0.0)
    tables[2 * HV : 3 * HV, :] = jnp.where(row > 0, 1.0, 0.0)
    tables[3 * HV : 4 * HV, :] = jnp.where(row < HV - 1, 1.0, 0.0)
    eye[...] = jnp.where(iota((HALF, HALF), 0) == iota((HALF, HALF), 1), 1.0, 0.0)
    flip[...] = (iota((HALF, HALF), 0) + iota((HALF, HALF), 1) == HALF - 1).astype(BF16)
    of_key = iota((TOK, TOK), 1) // (WIN * WIN)
    of_query = iota((TOK, TOK), 0) // (WIN * WIN)
    for scene in range(scenes):
        live = count_ref[scene]
        bias[scene] = jnp.where((of_key < live) & (of_key != of_query), 0.0, MASKED)

    gain_a = gains[0:1, :]
    gain_b = gains[1:2, :]
    gain_c = gains[2:3, :]
    depth_values = 1.0 + 3.0 * iota((1, PLANES), 1).astype(F32) / (PLANES - 1)
    upper = [slice(part * HALF, (part + 1) * HALF) for part in range(2)]
    views = range(VIEWS)
    places = [slice(side * TOK, (side + 1) * TOK) for side in range(2)]
    windows = [slice(at * WIN * WIN, (at + 1) * WIN * WIN) for at in range(2 * VIEWS)]

    def attend(scene, half, side):
        step = 2 * scene + half
        spot = places[side]
        x0 = x0s[step, spot, :]
        normed = (xh_a[step, spot, :] * gain_a).astype(BF16)
        no_a[step, spot, :] = normed
        yield 100
        qkv = mm(normed, w_sq[...]).astype(BF16)
        qkv_a[step, spot, :] = qkv
        yield 300
        scores = joined([mm_nt(qkv[at, :C], qkv[at, C : 2 * C]) for at in windows[:VIEWS]])
        yield 200
        probs = soft(scores * (SCALE * LOG2E))
        p_a[step, spot, :] = probs
        yield 400
        mixed = joined([mm(probs[at], qkv[at, 2 * C :]) for at in windows[:VIEWS]]).astype(BF16)
        o_a[step, spot, :] = mixed
        yield 300
        x1 = x0 + mm(mixed, w_so[...])
        yield 200
        xhat, rstd, normed = norm_forward(x1, gain_b)
        xh_b[step, spot, :] = xhat
        rs_b[step, spot, :] = rstd
        no_b[step, spot, :] = normed
        yield 400
        qkv = mm(normed, w_cq[...]).astype(BF16)
        qkv_b[step, spot, :] = qkv
        yield 300
        scores = mm_nt(qkv[:, :C], qkv[:, C : 2 * C]) * (SCALE * LOG2E) + bias[scene]
        yield 300
        probs = soft(scores)
        p_b[step, spot, :] = probs
        yield 500
        mixed = mm(probs, qkv[:, 2 * C :]).astype(BF16)
        o_b[step, spot, :] = mixed
        yield 300
        x2 = x1 + mm(mixed, w_co[...])
        x2s[step, spot, :] = x2
        yield 200
        xhat, rstd, normed = norm_forward(x2, gain_c)
        xh_c[step, spot, :] = xhat
        rs_c[step, spot, :] = rstd
        no_c[step, spot, :] = normed
        yield 400

    def feed(scene, half):
        step = 2 * scene + half
        for block in range(FFH // C):
            cols = slice(block * C, (block + 1) * C)
            for at in places:
                inner = mm(no_c[step, at, :], w_fi[:, cols])
                cdf = 0.5 + 0.5 * lax.erf(inner * 0.5**0.5)
                bell = jnp.exp2(inner * inner * (-0.5 * LOG2E))
                gd[step, at, cols] = cdf + inner * bell * 0.3989422804014327
                act[step, at, cols] = (inner * cdf).astype(BF16)
                yield 100
        x3 = x2s[step] + mm(act[step], w_fo[...])
        for side in range(2):
            x3s[scene, :, half, :, side] = x3[places[side]].reshape(VIEWS, WIN, WIN, C)
        yield 300

    def by_row(value, table):
        return (value.reshape(-1, HV, C) * table).reshape(value.shape)

    def im2col(value, pad, dest, first, last):
        pad[8 : 8 + PIX, :] = value
        dest[HV : HV + PIX, C : 2 * C] = value.astype(BF16)
        before = by_row(pad[7 : 7 + PIX, :], tables[2 * HV : 3 * HV, :])
        after = by_row(pad[9 : 9 + PIX, :], tables[3 * HV : 4 * HV, :])
        dest[HV : HV + PIX, first * C : (first + 1) * C] = before.astype(BF16)
        dest[HV : HV + PIX, last * C : (last + 1) * C] = after.astype(BF16)

    def convolve(padded, kernel):
        rows_two = padded.reshape(HV // 2 + 1, 2, HV, 3 * C)
        columns = jnp.concatenate(
            [rows_two[a // 2 : a // 2 + HV // 2, a % 2].reshape(HALF, 3 * C) for a in range(4)], -1
        )
        both = mm(columns, kernel[...])
        return joined(
            [both[HV * (y // 2) : HV * (y // 2 + 1), C * (y % 2) : C * (y % 2 + 1)] for y in range(HV)]
        )

    def head(scene):
        live = count_ref[scene]
        goes_on = {1: live > 2, 2: live > 3}

        def partner_of(ref, view, at):
            if view in goes_on:
                return jnp.where(goes_on[view], ref[scene, view + 1, at, :], ref[scene, 0, at, :])
            return ref[scene, (view + 1) % VIEWS, at, :]

        for view in views:
            low[scene, view] = x3s[scene, view].reshape(PIX, C).astype(BF16)
            shift = offsets[scene, view : view + 1, :]
            hots[scene, 0, view, 0:HV, :] = (shift == row).astype(BF16)
            hots[scene, 0, view, C : C + HV, :] = (shift == row).astype(BF16)
            hots[scene, 1, view, 0:HV, :] = (shift == HV - 1 - row).astype(BF16)
        yield 300
        for view in views:
            rev[scene, view] = unpaired(mm(flip[...], paired(low[scene, view])).astype(BF16))
        yield 400
        corrs = [[mm_nt(low[scene, view, at, :], partner_of(rev, view, at)) for at in upper] for view in views]
        yield 400
        skewed = [
            [by_row(pltpu.roll(corr, 1, 1, stride=1, stride_axis=0), tables[0:HV, :]) for corr in corrs[view]]
            for view in views
        ]
        yield 500
        cost = [mm(split_two(joined(skewed[view])), hots[scene, 0, view]) for view in views]
        yield 500
        for view in views:
            im2col(cost[view], pads.at[scene, 0, view], taps.at[scene, view], 0, 2)
            yield 80
        refined = []
        for view in views:
            refined.append(cost[view] + convolve(taps[scene, view], t_rf))
            yield 250
        d_refined = []
        for view in views:
            expo = jnp.exp2((refined[view] - jnp.max(refined[view], -1, keepdims=True)) * LOG2E)
            inverse = 1.0 / jnp.sum(expo, -1, keepdims=True)
            depth = jnp.sum(expo * depth_values, -1, keepdims=True) * inverse
            valid = jnp.where(view < live, 1.0, 0.0)
            incoming = []
            for at in upper:
                depth_out[scene, view : view + 1, at] = jnp.sum(eye[...] * depth[at], 0, keepdims=True)
                incoming.append(jnp.sum(eye[...] * depth_grad[scene, view : view + 1, at], 1, keepdims=True))
            weight = joined(incoming) * (inverse * valid)
            d_refined.append(expo * (weight * depth_values - weight * depth))
            yield 250
        for view in views:
            im2col(d_refined[view], pads.at[scene, 1, view], back_taps.at[scene, view], 2, 0)
            yield 80
        d_cost = []
        for view in views:
            d_cost.append(d_refined[view] + convolve(back_taps[scene, view], b_rf))
            yield 250
        for view in views:
            columns = jnp.concatenate([taps[scene, view, HV * a : HV * a + PIX, :] for a in range(3)], -1)
            g_rf[...] += mm_tn(back_taps[scene, view, HV : HV + PIX, C : 2 * C], columns)
            yield 250
        d_skewed = [
            mm_nt(split_two(d_cost[view]), jnp.concatenate([hots[scene, 1, view, :C, :]] * 2, -1)) for view in views
        ]
        yield 300
        d_corr = [
            [
                pltpu.roll(
                    by_row(d_skewed[view][at], tables[HV : 2 * HV, :]), HALF - HV + 1, 1, stride=1, stride_axis=0
                ).astype(BF16)
                for at in upper
            ]
            for view in views
        ]
        yield 250
        for part in range(2):
            at = upper[part]
            total = [mm(d_corr[view][part], partner_of(low, view, at)) for view in views]
            for view in views:
                there = mm_tn(d_corr[view][part], low[scene, view, at, :])
                if view in goes_on:
                    total[view + 1] = total[view + 1] + jnp.where(goes_on[view], there, 0.0)
                    total[0] = total[0] + jnp.where(goes_on[view], 0.0, there)
                else:
                    total[(view + 1) % VIEWS] = total[(view + 1) % VIEWS] + there
            for view in views:
                d3s[scene, view, part] = total[view].reshape(WIN, 2, WIN, C)
            yield 250

    def back(scene, half):
        step = 2 * scene + half
        both = range(2)
        d3 = [d3s[scene, :, half, :, side].reshape(TOK, C) for side in both]
        d_low = [d3[side].astype(BF16) for side in both]
        d_inner = [[], []]
        for block in range(FFH // C):
            cols = slice(block * C, (block + 1) * C)
            for side in both:
                d_inner[side].append((mm(d_low[side], t_fo[:, cols]) * gd[step, places[side], cols]).astype(BF16))
            yield 100
        d_inner = [jnp.concatenate(d_inner[side], -1) for side in both]
        d_normed = []
        for side in both:
            d_normed.append(mm(d_inner[side], t_fi[...]))
            yield 150
        g_fo[...] += mm_tn(joined(d_low), act[step])
        yield 250
        g_fi[...] += mm_tn(no_c[step], joined(d_inner))
        yield 250
        d2 = []
        for side in both:
            spot = places[side]
            d_hidden, d_gain = norm_backward(d_normed[side], xh_c[step, spot, :], rs_c[step, spot, :], gain_c)
            g_gain[2] += d_gain
            d2.append(d3[side] + d_hidden)
            yield 150
        d_low = [d2[side].astype(BF16) for side in both]
        qkv = [qkv_b[step, spot, :] for spot in places]
        d_mixed = []
        for side in both:
            d_mixed.append(mm(d_low[side], t_co[...]).astype(BF16))
            yield 100
        g_co[...] += mm_tn(o_b[step], joined(d_low))
        yield 100
        d_packed = [[], []]
        d_raw = []
        for side in both:
            probs = p_b[step, places[side], :]
            d_values = mm_tn(probs, d_mixed[side])
            d_probs = mm_nt(d_mixed[side], qkv[side][:, 2 * C :])
            yield 150
            d_raw.append(soft_back(probs, d_probs))
            d_packed[side].append(d_values)
            yield 150
        for side in both:
            d_query = mm(d_raw[side], qkv[side][:, C : 2 * C])
            d_keys = mm_tn(d_raw[side], qkv[side][:, :C])
            d_packed[side] = jnp.concatenate([d_query, d_keys] + d_packed[side], -1).astype(BF16)
            yield 200
        d_normed = []
        for side in both:
            d_normed.append(mm(d_packed[side], t_cq[...]))
            yield 100
        g_cq[...] += mm_tn(no_b[step], joined(d_packed))
        yield 200
        d1 = []
        for side in both:
            spot = places[side]
            d_hidden, d_gain = norm_backward(d_normed[side], xh_b[step, spot, :], rs_b[step, spot, :], gain_b)
            g_gain[1] += d_gain
            d1.append(d2[side] + d_hidden)
            yield 150
        d_low = [d1[side].astype(BF16) for side in both]
        qkv = [qkv_a[step, spot, :] for spot in places]
        d_mixed = []
        for side in both:
            d_mixed.append(mm(d_low[side], t_so[...]).astype(BF16))
            yield 100
        g_so[...] += mm_tn(o_a[step], joined(d_low))
        yield 100
        d_packed = [[], []]
        d_raw = []
        for side in both:
            probs = p_a[step, places[side], :]
            d_values = joined([mm_tn(probs[at], d_mixed[side][at]) for at in windows[:VIEWS]])
            d_probs = joined([mm_nt(d_mixed[side][at], qkv[side][at, 2 * C :]) for at in windows[:VIEWS]])
            yield 150
            d_raw.append(soft_back(probs, d_probs))
            d_packed[side].append(d_values)
            yield 100
        for side in both:
            d_query = joined([mm(d_raw[side][at], qkv[side][at, C : 2 * C]) for at in windows[:VIEWS]])
            d_keys = joined([mm_tn(d_raw[side][at], qkv[side][at, :C]) for at in windows[:VIEWS]])
            d_packed[side] = jnp.concatenate([d_query, d_keys] + d_packed[side], -1).astype(BF16)
            yield 150
        d_normed = []
        for side in both:
            d_normed.append(mm(d_packed[side], t_sq[...]))
            yield 100
        g_sq[...] += mm_tn(no_a[step], joined(d_packed))
        yield 200
        for side in both:
            spot = places[side]
            d_hidden, d_gain = norm_backward(d_normed[side], xh_a[step, spot, :], rs_a[step, spot, :], gain_a)
            g_gain[0] += d_gain
            grad_out[step, spot, :] = d1[side] + d_hidden
            yield 150

    def chain(*threads):
        for thread in threads:
            yield from thread

    def feeds(scene):
        return chain(feed(scene, 0), feed(scene, 1))

    def whole_of(thread, total):
        return paced(thread, 1.0 / total)

    def attends(scene):
        return [whole_of(attend(scene, half, side), 4200) for half in range(2) for side in range(2)]

    def feeds(scene):
        return whole_of(chain(feed(scene, 0), feed(scene, 1)), 2200)

    def backs(*which):
        return [whole_of(back(*one), 5400) for one in which]

    merge(*attends(0), *attends(1), apart=0.02)
    merge(feeds(0), feeds(1))
    merge(whole_of(head(0), 7600), whole_of(head(1), 7600), apart=0.05)
    merge(*backs((0, 0), (0, 1), (1, 0), (1, 1)), apart=0.04)

    bits = bits_of(parts)
    line = iota((GAIN_ROWS, C), 0)
    gain_rows = jnp.zeros((GAIN_ROWS, C), F32)
    for which in range(3):
        gain_rows = jnp.where(line == which, jnp.sum(g_gain[which], 0, keepdims=True), gain_rows)
    gain_rows = gain_rows.astype(BF16)
    for block in range(FFH // C):
        w_fo[block * C : (block + 1) * C, :] = g_fo[:, block * C : (block + 1) * C].T.astype(BF16)
    half_rows = rows_of(parts) // 2
    first = side_of_rows
    for apart in range(parts):
        shard = me ^ apart
        slot = sum(((apart >> bit) & 1) << (bits - 1 - bit) for bit in range(bits))
        dest = (keep_out, send_out)[slot // (parts // 2)].at[slot % (parts // 2)]

        def put(at, value):
            height = value.shape[0]
            which, offset = divmod(at, half_rows)
            assert offset + height <= half_rows
            dest[pl.ds(pl.multiple_of((first ^ which) * half_rows + offset, 16), height), :] = value

        at = 0
        for ref, blocks in zip((g_sq, g_so, g_cq, g_co, g_fi, w_fo, g_rf), BLOCKS):
            for block in range(blocks):
                if ref is w_fo:
                    spot = pl.ds(pl.multiple_of(shard * (blocks * rows) + block * rows, 16), rows)
                    put(at, ref[spot, :])
                else:
                    spot = pl.ds(pl.multiple_of(shard * rows, 16), rows)
                    put(at, ref[spot, block * C : (block + 1) * C].astype(BF16))
                at += rows
        put(at, gain_rows)
        if at + GAIN_ROWS < rows_of(parts):
            put(at + GAIN_ROWS, jnp.zeros((rows_of(parts) - at - GAIN_ROWS, C), BF16))


VMEM = pl.BlockSpec(memory_space=pltpu.VMEM)
HBM = pl.BlockSpec(memory_space=pltpu.HBM)
SMEM = pl.BlockSpec(memory_space=pltpu.SMEM)


def exchange(value, fsdp_mask, dp_mask):
    parts = lax.axis_size("fsdp")
    count = parts * lax.axis_size("dp")
    mask = dp_mask * parts + fsdp_mask
    return lax.ppermute(value, ("dp", "fsdp"), [(i, i ^ mask) for i in range(count)])


def local(
    features,
    view_count,
    plane_offsets,
    depth_grad,
    gain_self,
    self_qkv,
    self_out,
    gain_cross,
    cross_qkv,
    cross_out,
    gain_ff,
    ff_in,
    ff_out,
    refine,
):
    parts = lax.axis_size("fsdp")
    copies = lax.axis_size("dp")
    scenes = features.shape[0]
    rows = C // parts
    shard_rows = rows_of(parts)
    small = pltpu.CompilerParams(vmem_limit_bytes=8 * MIB)

    pack = pl.pallas_call(
        functools.partial(pack_kernel, parts),
        out_shape=jax.ShapeDtypeStruct((shard_rows, C), BF16),
        in_specs=[HBM] * 10,
        out_specs=VMEM,
        scratch_shapes=[pltpu.VMEM((3, 1, rows), BF16), pltpu.SemaphoreType.DMA((3 + sum(BLOCKS),))],
        compiler_params=pltpu.CompilerParams(vmem_limit_bytes=60 * MIB),
        name="pack",
    )
    own = [gain.reshape(1, rows) for gain in (gain_self, gain_cross, gain_ff)]
    own += [self_qkv, self_out, cross_qkv, cross_out, ff_in, ff_out, refine]
    shard = pack(*own)
    steps = scenes * (HV // WIN)
    span = 2 * TOK
    start = pl.pallas_call(
        functools.partial(start_kernel, scenes),
        out_shape=(jax.ShapeDtypeStruct((steps, span, C), F32),) * 3,
        in_specs=[VMEM],
        out_specs=(VMEM,) * 3,
        compiler_params=small,
        cost_estimate=pl.CostEstimate(flops=10 * features.size, bytes_accessed=14 * features.size, transcendentals=0),
        name="start",
    )
    began = start(features)

    packed = {0: shard}
    for bit in reversed(range(bits_of(parts))):
        came = {apart | (1 << bit): exchange(piece, 1 << bit, 0) for apart, piece in packed.items()}
        if len(packed) == 1:
            came, began = lax.optimization_barrier((came, began))
        packed |= came
    packed = [packed[apart] for apart in range(1, parts)]

    scratch = [
        ((C, 3 * C), BF16), ((C, C), BF16), ((C, 3 * C), BF16), ((C, C), BF16),
        ((C, FFH), BF16), ((FFH, C), BF16), ((C, 9 * PLANES), BF16),
        ((3 * C, C), BF16), ((C, C), BF16), ((3 * C, C), BF16), ((C, C), BF16),
        ((FFH, C), BF16), ((C, FFH), BF16), ((12 * PLANES, 2 * C), BF16), ((12 * PLANES, 2 * C), BF16),
        ((8, C), F32),
        ((scenes, TOK, TOK), F32),
        ((steps, span, C), F32),
    ]
    scratch += [((steps, span, C), F32)] * 4
    scratch += [((steps, span, C), BF16)] * 3
    scratch += [
        ((steps, span, 3 * C), BF16), ((steps, span, 3 * C), BF16),
        ((steps, span, WIN * WIN), BF16), ((steps, span, TOK), BF16),
        ((steps, span, C), BF16), ((steps, span, C), BF16),
        ((steps, span, FFH), F32), ((steps, span, FFH), BF16),
        ((scenes, VIEWS, 2, WIN, 2, WIN, C), F32), ((scenes, VIEWS, 2, WIN, 2, WIN, C), F32),
        ((scenes, VIEWS, PIX, C), BF16), ((scenes, VIEWS, PIX, C), BF16),
        ((scenes, 2, VIEWS, PIX + 16, C), F32),
        ((scenes, VIEWS, PIX + 2 * HV, 3 * C), BF16), ((scenes, VIEWS, PIX + 2 * HV, 3 * C), BF16),
        ((4 * HV, C), F32), ((HALF, HALF), F32), ((HALF, HALF), BF16), ((scenes, 2, VIEWS, 2 * C, C), BF16),
        ((C, 3 * C), F32), ((C, C), F32), ((C, 3 * C), F32), ((C, C), F32),
        ((C, FFH), F32), ((C, FFH), F32), ((C, 9 * PLANES), F32), ((3, 8, C), F32),
    ]
    main = pl.pallas_call(
        functools.partial(main_kernel, scenes, parts),
        out_shape=(
            jax.ShapeDtypeStruct((scenes, VIEWS, PIX), F32),
            jax.ShapeDtypeStruct((steps, span, C), F32),
            jax.ShapeDtypeStruct((parts // 2, shard_rows, C), BF16),
            jax.ShapeDtypeStruct((parts // 2, shard_rows, C), BF16),
        ),
        in_specs=[SMEM] + [VMEM] * (14 + parts),
        out_specs=(VMEM,) * 4,
        scratch_shapes=[pltpu.VMEM(shape, kind) for shape, kind in scratch]
,
        compiler_params=pltpu.CompilerParams(vmem_limit_bytes=46 * MIB),
        name="layer",
    )
    depth, grad_features, keep, send = main(view_count, *began, plane_offsets, depth_grad, *own, *packed)

    grad_features = grad_features.reshape(scenes, 2, 2, VIEWS, WIN, WIN, C).transpose(0, 3, 1, 4, 2, 5, 6)
    grad_features = grad_features.reshape(features.shape)

    for bit in range(bits_of(parts)):
        if bit > 0:
            keep, send = keep[: keep.shape[0] // 2], keep[keep.shape[0] // 2 :]
        if bit < bits_of(parts) - 1:
            keep = keep + exchange(send, 1 << bit, 0)
    last = parts // 2
    half = shard_rows // 2
    beside = exchange(send[0, :half], last, 0)
    across = exchange(keep[0, half:], 0, 1)
    corner = exchange(send[0, half:], last, 1)
    grads = (keep[0, :half].astype(F32) + beside) + (across.astype(F32) + corner)
    grads = grads.astype(BF16)
    for bit in reversed(range(2, bits_of(copies))):
        grads = grads + exchange(grads, 0, 1 << bit)
    if bits_of(copies) > 1:
        along = exchange(grads, 0, 2)
        swapped = exchange(grads, 0, 1)
        corner = exchange(grads, 0, 3)
        own, other = (grads, along), (swapped, corner)
    else:
        own, other = (grads,), (exchange(grads, 0, 1),)

    unpack = pl.pallas_call(
        functools.partial(unpack_kernel, parts),
        out_shape=tuple(jax.ShapeDtypeStruct((1, rows), F32) for _ in range(3))
        + tuple(
            jax.ShapeDtypeStruct(piece.shape, F32)
            for piece in (self_qkv, self_out, cross_qkv, cross_out, ff_in, ff_out, refine)
        ),
        in_specs=[VMEM] * (2 * len(own)),
        out_specs=(VMEM,) * 10,
        scratch_shapes=[pltpu.VMEM((shard_rows, C), F32)],
        compiler_params=small,
        name="unpack",
    )
    ga, gb, gc, d_sq, d_so, d_cq, d_co, d_fi, d_fo, d_rf = unpack(*own, *other)
    return (
        depth * (jnp.arange(VIEWS) < view_count[:, None])[:, :, None],
        grad_features,
        ga.reshape(rows),
        d_sq,
        d_so,
        gb.reshape(rows),
        d_cq,
        d_co,
        gc.reshape(rows),
        d_fi,
        d_fo,
        d_rf,
    )


def solution(mesh):
    placed = (
        P(("dp", "fsdp"), None, None, None),
        P(("dp", "fsdp")),
        P(("dp", "fsdp"), None, None),
        P(("dp", "fsdp"), None, None),
        P("fsdp"),
        P("fsdp", None),
        P("fsdp", None),
        P("fsdp"),
        P("fsdp", None),
        P("fsdp", None),
        P("fsdp"),
        P("fsdp", None),
        P("fsdp", None),
        P("fsdp", None),
    )
    return jax.shard_map(
        local,
        mesh=mesh,
        in_specs=placed,
        out_specs=(
            P(("dp", "fsdp"), None, None),
            P(("dp", "fsdp"), None, None, None),
            P("fsdp"),
            P("fsdp", None),
            P("fsdp", None),
            P("fsdp"),
            P("fsdp", None),
            P("fsdp", None),
            P("fsdp"),
            P("fsdp", None),
            P("fsdp", None),
            P("fsdp", None),
        ),
        check_vma=False,
    )
```

```python
import functools

import jax
import jax.numpy as jnp
from jax import lax
from jax.experimental import pallas as pl
from jax.experimental.pallas import tpu as pltpu
from jax.sharding import PartitionSpec as P

C = 128
FFH = 512
PLANES = 128
WIN = 8
VIEWS = 4
HV = 16
PIX = HV * HV
TOK = VIEWS * WIN * WIN
HALF = PIX // 2
GAIN_ROWS = 16
MASKED = -1e30
SCALE = C**-0.5
LOG2E = 1.4426950408889634
F32 = jnp.float32
BF16 = jnp.bfloat16
BLOCKS = (3, 1, 3, 1, 4, 4, 9)
MIB = 1024 * 1024


def mm(left, right):
    return lax.dot_general(left, right, (((1,), (0,)), ((), ())), preferred_element_type=F32)


def mm_nt(left, right):
    return lax.dot_general(left, right, (((1,), (1,)), ((), ())), preferred_element_type=F32)


def mm_tn(left, right):
    return lax.dot_general(left, right, (((0,), (0,)), ((), ())), preferred_element_type=F32)


def paired(value):
    half = value.shape[0] // 2
    return jnp.concatenate([value[:half], value[half:]], -1)


def unpaired(value):
    half = value.shape[1] // 2
    return jnp.concatenate([value[:, :half], value[:, half:]], 0)


def norm_forward(value, gain):
    centred = value - jnp.mean(value, -1, keepdims=True)
    spread = jnp.mean(centred * centred, -1, keepdims=True)
    rstd = lax.rsqrt(spread + 1e-05)
    xhat = centred * rstd
    return xhat, jnp.broadcast_to(rstd, value.shape), (xhat * gain).astype(BF16)


def norm_backward(d_normed, xhat, rstd, gain):
    d_xhat = d_normed * gain
    mean_d = jnp.mean(d_xhat, -1, keepdims=True)
    mean_dx = jnp.mean(d_xhat * xhat, -1, keepdims=True)
    return rstd * (d_xhat - mean_d - xhat * mean_dx)


def split_two(value):
    high = value.astype(BF16)
    return jnp.concatenate([high, (value - high.astype(F32)).astype(BF16)], -1)


def iota(shape, axis):
    return lax.broadcasted_iota(jnp.int32, shape, axis)


def bits_of(size):
    return size.bit_length() - 1


def rows_of(parts):
    return -(-sum(BLOCKS) * (C // parts) // 32) * 32


def place_of(parts):
    return lax.axis_index("fsdp").astype(jnp.int32), (lax.axis_index("dp") & 1).astype(jnp.int32)


def gain_lines(parts, gains):
    rows = C // parts
    place = (iota((rows, C), 1) == iota((rows, C), 0) + place_of(parts)[0] * rows).astype(BF16)
    line = iota((GAIN_ROWS, C), 0)
    total = jnp.zeros((GAIN_ROWS, C), F32)
    for which in range(3):
        row = mm(jnp.broadcast_to(gains[which][...], (8, rows)), place)[:1]
        total = jnp.where(line == which, row, total)
    return total


def pack_kernel(parts, *refs):
    gains, weights, out, scratch, sems = refs[:3], refs[3:10], refs[10], refs[11], refs[12]
    rows = C // parts
    copies = []

    def copy(source, target):
        copies.append(pltpu.make_async_copy(source, target, sems.at[len(copies)]))
        copies[-1].start()

    for which in range(3):
        copy(gains[which], scratch.at[which])
    at = 0
    for ref, blocks in zip(weights, BLOCKS):
        if ref.shape[0] == blocks * rows and ref.shape[1] == C:
            copy(ref, out.at[at : at + blocks * rows, :])
        else:
            for block in range(blocks):
                copy(ref.at[:, block * C : (block + 1) * C], out.at[at + block * rows : at + (block + 1) * rows, :])
        at += blocks * rows
    for one in copies[:3]:
        one.wait()
    total = gain_lines(parts, [scratch.at[which] for which in range(3)])
    out[at : at + GAIN_ROWS, :] = total.astype(BF16)
    for one in copies[3:]:
        one.wait()


def unpack_kernel(parts, *refs):
    gains, weights, refs = refs[0], refs[1], refs[2:]
    terms = (len(refs) - 11) // 2
    own, other, outs = refs[:terms], refs[terms : 2 * terms], refs[2 * terms :]
    rows = C // parts
    me, side = place_of(parts)
    whole = outs[-1]
    half = own[0].shape[0]
    for first, pieces in ((side, own), (1 - side, other)):
        whole[pl.ds(pl.multiple_of(first * half, 8), half), :] = sum(piece[...].astype(F32) for piece in pieces)
    at = 0
    for out, blocks in zip(outs[3:10], BLOCKS):
        if out.shape[0] == blocks * rows and out.shape[1] == C:
            out[...] = whole[at : at + blocks * rows, :]
        else:
            for block in range(blocks):
                out[:, block * C : (block + 1) * C] = whole[at + block * rows : at + (block + 1) * rows, :]
        at += blocks * rows
    eye = (iota((rows, rows), 0) == iota((rows, rows), 1)).astype(F32)
    place = (iota((rows, C), 1) == iota((rows, C), 0) + me * rows).astype(BF16)
    gain_rows = mm_nt(gains[...].astype(BF16), place)
    for which in range(3):
        grad = outs[3 + 2 * which]
        at = sum(BLOCKS[: 2 * which]) * rows
        column = jnp.zeros((rows, C), F32)
        for block in range(grad.shape[1] // C):
            weight = weights[at + block * rows : at + (block + 1) * rows, :].astype(F32)
            column = column + weight * grad[:, block * C : (block + 1) * C]
        column = jnp.sum(column, -1, keepdims=True)
        outs[which][...] = jnp.sum(eye * column, 0, keepdims=True) / gain_rows[which : which + 1]


def finish_kernel(scenes, d_packed, d_first, xhats, rstds, turned, gains, out):
    for scene in range(scenes):
        for half in range(2):
            step = 2 * scene + half
            for side in range(2):
                spot = slice(side * TOK, (side + 1) * TOK)
                d_normed = mm(d_packed[step, spot, :], turned[...])
                d_hidden = norm_backward(d_normed, xhats[step, spot, :], rstds[step, spot, :], gains[0:1, :])
                out[scene, :, half, :, side] = (d_first[step, spot, :] + d_hidden).reshape(VIEWS, WIN, WIN, C)


def merge(*threads, apart=0.0):
    spent = [apart * i for i in range(len(threads))]
    left = set(range(len(threads)))
    while left:
        which = min(left, key=lambda i: (spent[i], i))
        try:
            spent[which] += next(threads[which])
        except StopIteration:
            left.remove(which)


def paced(thread, rate):
    for share in thread:
        yield share * rate


def soft(scores):
    expo = jnp.exp2(scores - jnp.max(scores, -1, keepdims=True))
    return (expo * (1.0 / jnp.sum(expo, -1, keepdims=True))).astype(BF16)


def soft_back(probs, d_probs):
    probs = probs.astype(F32)
    delta = jnp.sum(d_probs * probs, -1, keepdims=True)
    return (probs * ((d_probs - delta) * SCALE)).astype(BF16)


def joined(pieces):
    return jnp.concatenate(pieces, 0)


def start_kernel(
    scenes, count, features, shard, offsets, depth_grad,
    lives, bias, x0s, xhats, rstds, shard_out, offsets_out, grad_out,
):
    of_key = iota((TOK, TOK), 1) // (WIN * WIN)
    of_query = iota((TOK, TOK), 0) // (WIN * WIN)
    for scene in range(scenes):
        live = count[scene]
        lives[scene] = jnp.broadcast_to(live, (8, C))
        bias[scene] = jnp.where((of_key < live) & (of_key != of_query), 0.0, MASKED)
    shard_out[...] = shard[...]
    offsets_out[...] = offsets[...]
    grad_out[...] = depth_grad[...]
    for scene in range(scenes):
        for half in range(2):
            step = 2 * scene + half
            piece = features[scene, :, half * HALF : (half + 1) * HALF, :]
            piece = piece.astype(F32).reshape(VIEWS, WIN, 2, WIN, C)
            for side in range(2):
                spot = slice(side * TOK, (side + 1) * TOK)
                x0 = piece[:, :, side].reshape(TOK, C)
                centred = x0 - jnp.mean(x0, -1, keepdims=True)
                spread = jnp.mean(centred * centred, -1, keepdims=True)
                rstd = lax.rsqrt(spread + 1e-05)
                x0s[step, spot, :] = x0
                xhats[step, spot, :] = centred * rstd
                rstds[step, spot, :] = jnp.broadcast_to(rstd, x0.shape)


def main_kernel(
    scenes,
    parts,
    lives,
    bias,
    x0s,
    xh_a,
    rs_a,
    offsets,
    depth_grad,
    *refs,
):
    packed, refs = refs[:parts], refs[parts:]
    (
    depth_out,
    d_packs,
    d_firsts,
    t_sq,
    gains,
    keep_out,
    send_out,
    w_sq, w_so, w_cq, w_co, w_fi, w_fo, w_rf,
    t_so, t_cq, t_co, t_fi, t_fo, t_rf, b_rf,
    x2s,
    xh_b, xh_c, rs_b, rs_c,
    no_a, no_b, no_c,
    qkv_a, qkv_b, p_a, p_b, o_a, o_b,
    gd, act,
    x3s, d3s,
    low, rev,
    pads, taps, back_taps,
    tables, eye, flip, hots,
    g_sq, g_so, g_cq, g_co, g_fi, g_fo, g_rf,
    ) = refs
    rows = C // parts
    me, side_of_rows = place_of(parts)

    total = jnp.zeros((GAIN_ROWS, C), F32)
    for apart, piece in enumerate(packed):
        shard = me ^ apart
        at = 0
        for ref, blocks in zip((w_sq, w_so, w_cq, w_co, w_fi, w_fo, w_rf), BLOCKS):
            height = blocks * rows if ref is w_fo else rows
            spot = pl.ds(pl.multiple_of(shard * height, 16), height)
            if ref is w_fo:
                ref[spot, :] = piece[at : at + height, :]
            else:
                for block in range(blocks):
                    ref[spot, block * C : (block + 1) * C] = piece[at + block * rows : at + (block + 1) * rows, :]
            at += blocks * rows
        total = total + piece[at : at + GAIN_ROWS, :].astype(F32)
    gains[...] = total[:8]
    for source, target in ((w_sq, t_sq), (w_so, t_so), (w_cq, t_cq), (w_co, t_co)):
        for block in range(source.shape[1] // C):
            target[block * C : (block + 1) * C, :] = source[:, block * C : (block + 1) * C].T
    for block in range(FFH // C):
        t_fi[block * C : (block + 1) * C, :] = w_fi[:, block * C : (block + 1) * C].T
        t_fo[:, block * C : (block + 1) * C] = w_fo[block * C : (block + 1) * C, :].T
    for tap in range(9):
        block = w_rf[:, tap * C : (tap + 1) * C]
        for ref, piece, at in ((t_rf, block.T, tap), (b_rf, block, 3 * (2 - tap // 3) + tap % 3)):
            ref[at * C : (at + 1) * C, :C] = piece
            ref[(at + 3) * C : (at + 4) * C, C:] = piece
    for ref in (t_rf, b_rf):
        ref[9 * C :, :C] = jnp.zeros((3 * C, C), BF16)
        ref[: 3 * C, C:] = jnp.zeros((3 * C, C), BF16)

    for ref in (g_sq, g_so, g_cq, g_co, g_fi, g_fo, g_rf, pads, hots):
        ref[...] = jnp.zeros_like(ref)
    empty = rows_of(parts) - sum(BLOCKS) * rows
    if empty:
        for ref in (keep_out, send_out):
            ref[...] = jnp.zeros_like(ref)
    for ref in (taps, back_taps):
        for scene in range(scenes):
            ref[scene, :, :HV, :] = jnp.zeros((VIEWS, HV, 3 * C), BF16)
            ref[scene, :, HV + PIX :, :] = jnp.zeros((VIEWS, HV, 3 * C), BF16)

    row = iota((HV, C), 0)
    lane = iota((HV, C), 1)
    tables[0:HV, :] = jnp.where((lane < HV) & (lane <= row), 0.5 * SCALE, 0.0)
    tables[HV : 2 * HV, :] = jnp.where((lane < HV) & (HV - 1 - lane <= row), 0.5 * SCALE, 0.0)
    tables[2 * HV : 3 * HV, :] = jnp.where(row > 0, 1.0, 0.0)
    tables[3 * HV : 4 * HV, :] = jnp.where(row < HV - 1, 1.0, 0.0)
    eye[...] = jnp.where(iota((HALF, HALF), 0) == iota((HALF, HALF), 1), 1.0, 0.0)
    flip[...] = (iota((HALF, HALF), 0) + iota((HALF, HALF), 1) == HALF - 1).astype(BF16)
    gain_a = gains[0:1, :]
    gain_b = gains[1:2, :]
    gain_c = gains[2:3, :]
    depth_values = 1.0 + 3.0 * iota((1, PLANES), 1).astype(F32) / (PLANES - 1)
    upper = [slice(part * HALF, (part + 1) * HALF) for part in range(2)]
    views = range(VIEWS)
    places = [slice(side * TOK, (side + 1) * TOK) for side in range(2)]
    windows = [slice(at * WIN * WIN, (at + 1) * WIN * WIN) for at in range(2 * VIEWS)]

    def attend(scene, half, side):
        step = 2 * scene + half
        spot = places[side]
        x0 = x0s[step, spot, :]
        normed = (xh_a[step, spot, :] * gain_a).astype(BF16)
        no_a[step, spot, :] = normed
        yield 100
        qkv = mm(normed, w_sq[...]).astype(BF16)
        qkv_a[step, spot, :] = qkv
        yield 300
        scores = joined([mm_nt(qkv[at, :C], qkv[at, C : 2 * C]) for at in windows[:VIEWS]])
        yield 200
        probs = soft(scores * (SCALE * LOG2E))
        p_a[step, spot, :] = probs
        yield 400
        mixed = joined([mm(probs[at], qkv[at, 2 * C :]) for at in windows[:VIEWS]]).astype(BF16)
        o_a[step, spot, :] = mixed
        yield 300
        x1 = x0 + mm(mixed, w_so[...])
        yield 200
        xhat, rstd, normed = norm_forward(x1, gain_b)
        xh_b[step, spot, :] = xhat
        rs_b[step, spot, :] = rstd
        no_b[step, spot, :] = normed
        yield 400
        qkv = mm(normed, w_cq[...]).astype(BF16)
        qkv_b[step, spot, :] = qkv
        yield 300
        scores = mm_nt(qkv[:, :C], qkv[:, C : 2 * C]) * (SCALE * LOG2E) + bias[scene]
        yield 300
        probs = soft(scores)
        p_b[step, spot, :] = probs
        yield 500
        mixed = mm(probs, qkv[:, 2 * C :]).astype(BF16)
        o_b[step, spot, :] = mixed
        yield 300
        x2 = x1 + mm(mixed, w_co[...])
        x2s[step, spot, :] = x2
        yield 200
        xhat, rstd, normed = norm_forward(x2, gain_c)
        xh_c[step, spot, :] = xhat
        rs_c[step, spot, :] = rstd
        no_c[step, spot, :] = normed
        yield 400

    def feed(scene, half):
        step = 2 * scene + half
        for block in range(FFH // C):
            cols = slice(block * C, (block + 1) * C)
            for at in places:
                inner = mm(no_c[step, at, :], w_fi[:, cols])
                cdf = 0.5 + 0.5 * lax.erf(inner * 0.5**0.5)
                bell = jnp.exp2(inner * inner * (-0.5 * LOG2E))
                gd[step, at, cols] = cdf + inner * bell * 0.3989422804014327
                act[step, at, cols] = (inner * cdf).astype(BF16)
                yield 100
        x3 = x2s[step] + mm(act[step], w_fo[...])
        for side in range(2):
            x3s[scene, :, half, :, side] = x3[places[side]].reshape(VIEWS, WIN, WIN, C)
        yield 300

    def by_row(value, table):
        return (value.reshape(-1, HV, C) * table).reshape(value.shape)

    def im2col(value, pad, dest, first, last):
        pad[8 : 8 + PIX, :] = value
        dest[HV : HV + PIX, C : 2 * C] = value.astype(BF16)
        before = by_row(pad[7 : 7 + PIX, :], tables[2 * HV : 3 * HV, :])
        after = by_row(pad[9 : 9 + PIX, :], tables[3 * HV : 4 * HV, :])
        dest[HV : HV + PIX, first * C : (first + 1) * C] = before.astype(BF16)
        dest[HV : HV + PIX, last * C : (last + 1) * C] = after.astype(BF16)

    def convolve(padded, kernel):
        rows_two = padded.reshape(HV // 2 + 1, 2, HV, 3 * C)
        columns = jnp.concatenate(
            [rows_two[a // 2 : a // 2 + HV // 2, a % 2].reshape(HALF, 3 * C) for a in range(4)], -1
        )
        both = mm(columns, kernel[...])
        return joined(
            [both[HV * (y // 2) : HV * (y // 2 + 1), C * (y % 2) : C * (y % 2 + 1)] for y in range(HV)]
        )

    def head(scene):
        live = lives[scene, 0:1, :]
        goes_on = {1: live > 2, 2: live > 3}

        def partner_of(ref, view, at):
            if view in goes_on:
                after, first = ref[scene, view + 1, at, :], ref[scene, 0, at, :]
                return jnp.where(goes_on[view], after.astype(F32), first.astype(F32)).astype(BF16)
            return ref[scene, (view + 1) % VIEWS, at, :]

        for view in views:
            low[scene, view] = x3s[scene, view].reshape(PIX, C).astype(BF16)
            shift = offsets[scene, view : view + 1, :]
            hots[scene, 0, view, 0:HV, :] = (shift == row).astype(BF16)
            hots[scene, 0, view, C : C + HV, :] = (shift == row).astype(BF16)
            hots[scene, 1, view, 0:HV, :] = (shift == HV - 1 - row).astype(BF16)
        yield 300
        for view in views:
            rev[scene, view] = unpaired(mm(flip[...], paired(low[scene, view])).astype(BF16))
        yield 400
        corrs = [[mm_nt(low[scene, view, at, :], partner_of(rev, view, at)) for at in upper] for view in views]
        yield 400
        skewed = [
            [by_row(pltpu.roll(corr, 1, 1, stride=1, stride_axis=0), tables[0:HV, :]) for corr in corrs[view]]
            for view in views
        ]
        yield 500
        cost = [mm(split_two(joined(skewed[view])), hots[scene, 0, view]) for view in views]
        yield 500
        for view in views:
            im2col(cost[view], pads.at[scene, 0, view], taps.at[scene, view], 0, 2)
            yield 80
        refined = []
        for view in views:
            refined.append(cost[view] + convolve(taps[scene, view], t_rf))
            yield 250
        d_refined = []
        for view in views:
            expo = jnp.exp2((refined[view] - jnp.max(refined[view], -1, keepdims=True)) * LOG2E)
            inverse = 1.0 / jnp.sum(expo, -1, keepdims=True)
            depth = jnp.sum(expo * depth_values, -1, keepdims=True) * inverse
            valid = jnp.where(view < live, 1.0, 0.0)
            incoming = []
            for at in upper:
                depth_out[scene, view : view + 1, at] = jnp.sum(eye[...] * depth[at], 0, keepdims=True)
                incoming.append(jnp.sum(eye[...] * depth_grad[scene, view : view + 1, at], 1, keepdims=True))
            weight = joined(incoming) * (inverse * valid)
            d_refined.append(expo * (weight * depth_values - weight * depth))
            yield 250
        for view in views:
            im2col(d_refined[view], pads.at[scene, 1, view], back_taps.at[scene, view], 2, 0)
            yield 80
        d_cost = []
        for view in views:
            d_cost.append(d_refined[view] + convolve(back_taps[scene, view], b_rf))
            yield 250
        for view in views:
            columns = jnp.concatenate([taps[scene, view, HV * a : HV * a + PIX, :] for a in range(3)], -1)
            g_rf[...] += mm_tn(back_taps[scene, view, HV : HV + PIX, C : 2 * C], columns)
            yield 250
        d_skewed = [
            mm_nt(split_two(d_cost[view]), jnp.concatenate([hots[scene, 1, view, :C, :]] * 2, -1)) for view in views
        ]
        yield 300
        d_corr = [
            [
                pltpu.roll(
                    by_row(d_skewed[view][at], tables[HV : 2 * HV, :]), HALF - HV + 1, 1, stride=1, stride_axis=0
                ).astype(BF16)
                for at in upper
            ]
            for view in views
        ]
        yield 250
        for part in range(2):
            at = upper[part]
            total = [mm(d_corr[view][part], partner_of(low, view, at)) for view in views]
            for view in views:
                there = mm_tn(d_corr[view][part], low[scene, view, at, :])
                if view in goes_on:
                    total[view + 1] = total[view + 1] + jnp.where(goes_on[view], there, 0.0)
                    total[0] = total[0] + jnp.where(goes_on[view], 0.0, there)
                else:
                    total[(view + 1) % VIEWS] = total[(view + 1) % VIEWS] + there
            for view in views:
                d3s[scene, view, part] = total[view].reshape(WIN, 2, WIN, C)
            yield 250

    def back(scene, half):
        step = 2 * scene + half
        both = range(2)
        d3 = [d3s[scene, :, half, :, side].reshape(TOK, C) for side in both]
        d_low = [d3[side].astype(BF16) for side in both]
        d_inner = [[], []]
        for block in range(FFH // C):
            cols = slice(block * C, (block + 1) * C)
            for side in both:
                d_inner[side].append((mm(d_low[side], t_fo[:, cols]) * gd[step, places[side], cols]).astype(BF16))
            yield 100
        d_inner = [jnp.concatenate(d_inner[side], -1) for side in both]
        d_normed = []
        for side in both:
            d_normed.append(mm(d_inner[side], t_fi[...]))
            yield 150
        g_fo[...] += mm_tn(joined(d_low), act[step])
        yield 250
        g_fi[...] += mm_tn(no_c[step], joined(d_inner))
        yield 250
        d2 = []
        for side in both:
            spot = places[side]
            d_hidden = norm_backward(d_normed[side], xh_c[step, spot, :], rs_c[step, spot, :], gain_c)
            d2.append(d3[side] + d_hidden)
            yield 150
        d_low = [d2[side].astype(BF16) for side in both]
        qkv = [qkv_b[step, spot, :] for spot in places]
        d_mixed = []
        for side in both:
            d_mixed.append(mm(d_low[side], t_co[...]).astype(BF16))
            yield 100
        g_co[...] += mm_tn(o_b[step], joined(d_low))
        yield 100
        d_packed = [[], []]
        d_raw = []
        for side in both:
            probs = p_b[step, places[side], :]
            d_values = mm_tn(probs, d_mixed[side])
            d_probs = mm_nt(d_mixed[side], qkv[side][:, 2 * C :])
            yield 150
            d_raw.append(soft_back(probs, d_probs))
            d_packed[side].append(d_values)
            yield 150
        for side in both:
            d_query = mm(d_raw[side], qkv[side][:, C : 2 * C])
            d_keys = mm_tn(d_raw[side], qkv[side][:, :C])
            d_packed[side] = jnp.concatenate([d_query, d_keys] + d_packed[side], -1).astype(BF16)
            yield 200
        d_normed = []
        for side in both:
            d_normed.append(mm(d_packed[side], t_cq[...]))
            yield 100
        g_cq[...] += mm_tn(no_b[step], joined(d_packed))
        yield 200
        d1 = []
        for side in both:
            spot = places[side]
            d_hidden = norm_backward(d_normed[side], xh_b[step, spot, :], rs_b[step, spot, :], gain_b)
            d1.append(d2[side] + d_hidden)
            yield 150
        d_low = [d1[side].astype(BF16) for side in both]
        qkv = [qkv_a[step, spot, :] for spot in places]
        d_mixed = []
        for side in both:
            d_mixed.append(mm(d_low[side], t_so[...]).astype(BF16))
            yield 100
        g_so[...] += mm_tn(o_a[step], joined(d_low))
        yield 100
        d_packed = [[], []]
        d_raw = []
        for side in both:
            probs = p_a[step, places[side], :]
            d_values = joined([mm_tn(probs[at], d_mixed[side][at]) for at in windows[:VIEWS]])
            d_probs = joined([mm_nt(d_mixed[side][at], qkv[side][at, 2 * C :]) for at in windows[:VIEWS]])
            yield 150
            d_raw.append(soft_back(probs, d_probs))
            d_packed[side].append(d_values)
            yield 100
        for side in both:
            d_query = joined([mm(d_raw[side][at], qkv[side][at, C : 2 * C]) for at in windows[:VIEWS]])
            d_keys = joined([mm_tn(d_raw[side][at], qkv[side][at, :C]) for at in windows[:VIEWS]])
            d_packed[side] = jnp.concatenate([d_query, d_keys] + d_packed[side], -1).astype(BF16)
            yield 150
        for side in both:
            d_packs[step, places[side], :] = d_packed[side]
            d_firsts[step, places[side], :] = d1[side]
            yield 50
        g_sq[...] += mm_tn(no_a[step], joined(d_packed))
        yield 200

    def chain(*threads):
        for thread in threads:
            yield from thread

    grads = (g_sq, g_so, g_cq, g_co, g_fi, w_fo, g_rf)

    def ship(*chosen):
        bits = bits_of(parts)
        half_rows = rows_of(parts) // 2
        for ref, blocks, before in zip(grads, BLOCKS, (sum(BLOCKS[:i]) for i in range(len(BLOCKS)))):
            if not any(ref is one for one in chosen):
                continue
            for apart in range(parts):
                shard = me ^ apart
                slot = sum(((apart >> bit) & 1) << (bits - 1 - bit) for bit in range(bits))
                dest = (keep_out, send_out)[slot // (parts // 2)].at[slot % (parts // 2)]
                for block in range(blocks):
                    if ref is w_fo:
                        spot = pl.ds(pl.multiple_of(shard * (blocks * rows) + block * rows, 16), rows)
                        value = ref[spot, :]
                    else:
                        spot = pl.ds(pl.multiple_of(shard * rows, 16), rows)
                        value = ref[spot, block * C : (block + 1) * C].astype(BF16)
                    for start in range(0, rows, 16):
                        which, offset = divmod((before + block) * rows + start, half_rows)
                        spot = pl.ds(pl.multiple_of((side_of_rows ^ which) * half_rows + offset, 16), 16)
                        dest[spot, :] = value[start : start + 16]
                yield 40

    def turn_back():
        for block in range(FFH // C):
            w_fo[block * C : (block + 1) * C, :] = g_fo[:, block * C : (block + 1) * C].T.astype(BF16)
            yield 30

    def whole_of(thread, total):
        return paced(thread, 1.0 / total)

    def attends(scene):
        return [whole_of(attend(scene, half, side), 4200) for half in range(2) for side in range(2)]

    def feeds(scene):
        return whole_of(chain(feed(scene, 0), feed(scene, 1)), 2200)

    def backs(*which):
        return [whole_of(back(*one), 5400) for one in which]

    merge(*attends(0), *attends(1), apart=0.02)
    merge(feeds(0), feeds(1))
    merge(whole_of(head(0), 7600), whole_of(head(1), 7600), apart=0.05)
    merge(*backs((0, 0), (0, 1), (1, 0), (1, 1)), whole_of(ship(g_rf), 160), apart=0.02)
    merge(chain(turn_back(), ship(w_fo)), ship(g_sq, g_so, g_cq, g_co, g_fi))


VMEM = pl.BlockSpec(memory_space=pltpu.VMEM)
HBM = pl.BlockSpec(memory_space=pltpu.HBM)
SMEM = pl.BlockSpec(memory_space=pltpu.SMEM)


def exchange(value, fsdp_mask, dp_mask):
    parts = lax.axis_size("fsdp")
    count = parts * lax.axis_size("dp")
    mask = dp_mask * parts + fsdp_mask
    return lax.ppermute(value, ("dp", "fsdp"), [(i, i ^ mask) for i in range(count)])


def local(
    features,
    view_count,
    plane_offsets,
    depth_grad,
    gain_self,
    self_qkv,
    self_out,
    gain_cross,
    cross_qkv,
    cross_out,
    gain_ff,
    ff_in,
    ff_out,
    refine,
):
    parts = lax.axis_size("fsdp")
    copies = lax.axis_size("dp")
    scenes = features.shape[0]
    rows = C // parts
    shard_rows = rows_of(parts)
    small = pltpu.CompilerParams(vmem_limit_bytes=8 * MIB)

    pack = pl.pallas_call(
        functools.partial(pack_kernel, parts),
        out_shape=jax.ShapeDtypeStruct((sum(BLOCKS) * rows + GAIN_ROWS, C), BF16),
        in_specs=[HBM] * 10,
        out_specs=VMEM,
        scratch_shapes=[pltpu.VMEM((3, 1, rows), BF16), pltpu.SemaphoreType.DMA((3 + sum(BLOCKS),))],
        compiler_params=pltpu.CompilerParams(vmem_limit_bytes=60 * MIB),
        name="pack",
    )
    own = [gain.reshape(1, rows) for gain in (gain_self, gain_cross, gain_ff)]
    own += [self_qkv, self_out, cross_qkv, cross_out, ff_in, ff_out, refine]
    shard = pack(*own)
    steps = scenes * (HV // WIN)
    span = 2 * TOK
    start = pl.pallas_call(
        functools.partial(start_kernel, scenes),
        out_shape=(
            jax.ShapeDtypeStruct((scenes, 8, C), jnp.int32),
            jax.ShapeDtypeStruct((scenes, TOK, TOK), F32),
        )
        + (jax.ShapeDtypeStruct((steps, span, C), F32),) * 3
        + tuple(jax.ShapeDtypeStruct(piece.shape, piece.dtype) for piece in (shard, plane_offsets, depth_grad)),
        in_specs=[SMEM] + [VMEM] * 4,
        out_specs=(VMEM,) * 8,
        compiler_params=small,
        cost_estimate=pl.CostEstimate(flops=10 * features.size, bytes_accessed=14 * features.size, transcendentals=0),
        name="start",
    )
    began = start(view_count, features, shard, plane_offsets, depth_grad)

    packed = {0: shard}
    for bit in reversed(range(bits_of(parts))):
        came = {apart | (1 << bit): exchange(piece, 1 << bit, 0) for apart, piece in packed.items()}
        if len(packed) == 1:
            came, began = lax.optimization_barrier((came, began))
        packed |= came
    packed = [packed[apart] for apart in range(parts)]

    scratch = [
        ((C, 3 * C), BF16), ((C, C), BF16), ((C, 3 * C), BF16), ((C, C), BF16),
        ((C, FFH), BF16), ((FFH, C), BF16), ((C, 9 * PLANES), BF16),
        ((C, C), BF16), ((3 * C, C), BF16), ((C, C), BF16),
        ((FFH, C), BF16), ((C, FFH), BF16), ((12 * PLANES, 2 * C), BF16), ((12 * PLANES, 2 * C), BF16),
        ((steps, span, C), F32),
    ]
    scratch += [((steps, span, C), F32)] * 4
    scratch += [((steps, span, C), BF16)] * 3
    scratch += [
        ((steps, span, 3 * C), BF16), ((steps, span, 3 * C), BF16),
        ((steps, span, WIN * WIN), BF16), ((steps, span, TOK), BF16),
        ((steps, span, C), BF16), ((steps, span, C), BF16),
        ((steps, span, FFH), F32), ((steps, span, FFH), BF16),
        ((scenes, VIEWS, 2, WIN, 2, WIN, C), F32), ((scenes, VIEWS, 2, WIN, 2, WIN, C), F32),
        ((scenes, VIEWS, PIX, C), BF16), ((scenes, VIEWS, PIX, C), BF16),
        ((scenes, 2, VIEWS, PIX + 16, C), F32),
        ((scenes, VIEWS, PIX + 2 * HV, 3 * C), BF16), ((scenes, VIEWS, PIX + 2 * HV, 3 * C), BF16),
        ((4 * HV, C), F32), ((HALF, HALF), F32), ((HALF, HALF), BF16), ((scenes, 2, VIEWS, 2 * C, C), BF16),
        ((C, 3 * C), F32), ((C, C), F32), ((C, 3 * C), F32), ((C, C), F32),
        ((C, FFH), F32), ((C, FFH), F32), ((C, 9 * PLANES), F32),
    ]
    main = pl.pallas_call(
        functools.partial(main_kernel, scenes, parts),
        out_shape=(
            jax.ShapeDtypeStruct((scenes, VIEWS, PIX), F32),
            jax.ShapeDtypeStruct((steps, span, 3 * C), BF16),
            jax.ShapeDtypeStruct((steps, span, C), F32),
            jax.ShapeDtypeStruct((3 * C, C), BF16),
            jax.ShapeDtypeStruct((8, C), F32),
            jax.ShapeDtypeStruct((parts // 2, shard_rows, C), BF16),
            jax.ShapeDtypeStruct((parts // 2, shard_rows, C), BF16),
        ),
        in_specs=[VMEM] * (7 + parts),
        out_specs=(VMEM,) * 7,
        scratch_shapes=[pltpu.VMEM(shape, kind) for shape, kind in scratch],
        compiler_params=pltpu.CompilerParams(vmem_limit_bytes=46 * MIB),
        name="layer",
    )
    lives, bias, x0s, xhats, rstds, packed[0], plane_offsets, depth_grad = began
    depth, d_packs, d_firsts, turned, gains, keep, send = main(
        lives, bias, x0s, xhats, rstds, plane_offsets, depth_grad, *packed
    )

    finish = pl.pallas_call(
        functools.partial(finish_kernel, scenes),
        out_shape=jax.ShapeDtypeStruct((scenes, VIEWS, 2, WIN, 2, WIN, C), F32),
        in_specs=[VMEM] * 6,
        out_specs=VMEM,
        compiler_params=small,
        cost_estimate=pl.CostEstimate(flops=6 * C * features.size, bytes_accessed=16 * features.size, transcendentals=0),
        name="finish",
    )
    grad_features = finish(d_packs, d_firsts, xhats, rstds, turned, gains).reshape(features.shape)

    for bit in range(bits_of(parts)):
        if bit > 0:
            keep, send = keep[: keep.shape[0] // 2], keep[keep.shape[0] // 2 :]
        if bit < bits_of(parts) - 1:
            keep = keep + exchange(send, 1 << bit, 0)
    last = parts // 2
    half = shard_rows // 2
    beside = exchange(send[0, :half], last, 0)
    across = exchange(keep[0, half:], 0, 1)
    corner = exchange(send[0, half:], last, 1)
    grads = (keep[0, :half].astype(F32) + beside) + (across.astype(F32) + corner)
    grads = grads.astype(BF16)
    for bit in reversed(range(2, bits_of(copies))):
        grads = grads + exchange(grads, 0, 1 << bit)
    if bits_of(copies) > 1:
        along = exchange(grads, 0, 2)
        swapped = exchange(grads, 0, 1)
        corner = exchange(grads, 0, 3)
        mine, other = (grads, along), (swapped, corner)
    else:
        mine, other = (grads,), (exchange(grads, 0, 1),)

    unpack = pl.pallas_call(
        functools.partial(unpack_kernel, parts),
        out_shape=tuple(jax.ShapeDtypeStruct((1, rows), F32) for _ in range(3))
        + tuple(
            jax.ShapeDtypeStruct(piece.shape, F32)
            for piece in (self_qkv, self_out, cross_qkv, cross_out, ff_in, ff_out, refine)
        ),
        in_specs=[VMEM] * (2 + 2 * len(mine)),
        out_specs=(VMEM,) * 10,
        scratch_shapes=[pltpu.VMEM((shard_rows, C), F32)],
        compiler_params=small,
        name="unpack",
    )
    ga, gb, gc, d_sq, d_so, d_cq, d_co, d_fi, d_fo, d_rf = unpack(
        gains, packed[0], *mine, *other
    )
    return (
        depth * (jnp.arange(VIEWS) < view_count[:, None])[:, :, None],
        grad_features,
        ga.reshape(rows),
        d_sq,
        d_so,
        gb.reshape(rows),
        d_cq,
        d_co,
        gc.reshape(rows),
        d_fi,
        d_fo,
        d_rf,
    )


def solution(mesh):
    placed = (
        P(("dp", "fsdp"), None, None, None),
        P(("dp", "fsdp")),
        P(("dp", "fsdp"), None, None),
        P(("dp", "fsdp"), None, None),
        P("fsdp"),
        P("fsdp", None),
        P("fsdp", None),
        P("fsdp"),
        P("fsdp", None),
        P("fsdp", None),
        P("fsdp"),
        P("fsdp", None),
        P("fsdp", None),
        P("fsdp", None),
    )
    return jax.shard_map(
        local,
        mesh=mesh,
        in_specs=placed,
        out_specs=(
            P(("dp", "fsdp"), None, None),
            P(("dp", "fsdp"), None, None, None),
            P("fsdp"),
            P("fsdp", None),
            P("fsdp", None),
            P("fsdp"),
            P("fsdp", None),
            P("fsdp", None),
            P("fsdp"),
            P("fsdp", None),
            P("fsdp", None),
            P("fsdp", None),
        ),
        check_vma=False,
    )
```

```python
import functools

import jax
import jax.numpy as jnp
from jax import lax
from jax.experimental import pallas as pl
from jax.experimental.pallas import tpu as pltpu
from jax.sharding import PartitionSpec as P

C = 128
FFH = 512
PLANES = 128
WIN = 8
VIEWS = 4
HV = 16
PIX = HV * HV
TOK = VIEWS * WIN * WIN
HALF = PIX // 2
GAIN_ROWS = 16
MASKED = -1e30
SCALE = C**-0.5
LOG2E = 1.4426950408889634
F32 = jnp.float32
BF16 = jnp.bfloat16
BLOCKS = (3, 1, 3, 1, 4, 4, 9)
MIB = 1024 * 1024


def mm(left, right):
    return lax.dot_general(left, right, (((1,), (0,)), ((), ())), preferred_element_type=F32)


def mm_nt(left, right):
    return lax.dot_general(left, right, (((1,), (1,)), ((), ())), preferred_element_type=F32)


def mm_tn(left, right):
    return lax.dot_general(left, right, (((0,), (0,)), ((), ())), preferred_element_type=F32)


def paired(value):
    half = value.shape[0] // 2
    return jnp.concatenate([value[:half], value[half:]], -1)


def unpaired(value):
    half = value.shape[1] // 2
    return jnp.concatenate([value[:, :half], value[:, half:]], 0)


def norm_forward(value, gain):
    centred = value - jnp.mean(value, -1, keepdims=True)
    spread = jnp.mean(centred * centred, -1, keepdims=True)
    rstd = lax.rsqrt(spread + 1e-05)
    xhat = centred * rstd
    return xhat, jnp.broadcast_to(rstd, value.shape), (xhat * gain).astype(BF16)


def norm_backward(d_normed, xhat, rstd, gain):
    d_xhat = d_normed * gain
    mean_d = jnp.mean(d_xhat, -1, keepdims=True)
    mean_dx = jnp.mean(d_xhat * xhat, -1, keepdims=True)
    return rstd * (d_xhat - mean_d - xhat * mean_dx)


def split_two(value):
    high = value.astype(BF16)
    return jnp.concatenate([high, (value - high.astype(F32)).astype(BF16)], -1)


def iota(shape, axis):
    return lax.broadcasted_iota(jnp.int32, shape, axis)


def bits_of(size):
    return size.bit_length() - 1


def rows_of(parts):
    return -(-sum(BLOCKS) * (C // parts) // 32) * 32


def place_of(parts):
    return lax.axis_index("fsdp").astype(jnp.int32), (lax.axis_index("dp") & 1).astype(jnp.int32)


def gain_lines(parts, gains):
    rows = C // parts
    place = (iota((rows, C), 1) == iota((rows, C), 0) + place_of(parts)[0] * rows).astype(BF16)
    line = iota((GAIN_ROWS, C), 0)
    total = jnp.zeros((GAIN_ROWS, C), F32)
    for which in range(3):
        row = mm(jnp.broadcast_to(gains[which][...], (8, rows)), place)[:1]
        total = jnp.where(line == which, row, total)
    return total


def pack_kernel(parts, *refs):
    gains, weights, out, scratch, sems = refs[:3], refs[3:10], refs[10], refs[11], refs[12]
    rows = C // parts
    copies = []

    def copy(source, target):
        copies.append(pltpu.make_async_copy(source, target, sems.at[len(copies)]))
        copies[-1].start()

    for which in range(3):
        copy(gains[which], scratch.at[which])
    at = 0
    for ref, blocks in zip(weights, BLOCKS):
        if ref.shape[0] == blocks * rows and ref.shape[1] == C:
            copy(ref, out.at[at : at + blocks * rows, :])
        else:
            for block in range(blocks):
                copy(ref.at[:, block * C : (block + 1) * C], out.at[at + block * rows : at + (block + 1) * rows, :])
        at += blocks * rows
    for one in copies[:3]:
        one.wait()
    total = gain_lines(parts, [scratch.at[which] for which in range(3)])
    out[at : at + GAIN_ROWS, :] = total.astype(BF16)
    for one in copies[3:]:
        one.wait()


def unpack_kernel(parts, *refs):
    gains, weights, refs = refs[0], refs[1], refs[2:]
    terms = (len(refs) - 11) // 2
    own, other, outs = refs[:terms], refs[terms : 2 * terms], refs[2 * terms :]
    rows = C // parts
    me, side = place_of(parts)
    whole = outs[-1]
    half = own[0].shape[0]
    for first, pieces in ((side, own), (1 - side, other)):
        whole[pl.ds(pl.multiple_of(first * half, 8), half), :] = sum(piece[...].astype(F32) for piece in pieces)
    at = 0
    for out, blocks in zip(outs[3:10], BLOCKS):
        if out.shape[0] == blocks * rows and out.shape[1] == C:
            out[...] = whole[at : at + blocks * rows, :]
        else:
            for block in range(blocks):
                out[:, block * C : (block + 1) * C] = whole[at + block * rows : at + (block + 1) * rows, :]
        at += blocks * rows
    eye = (iota((rows, rows), 0) == iota((rows, rows), 1)).astype(F32)
    place = (iota((rows, C), 1) == iota((rows, C), 0) + me * rows).astype(BF16)
    gain_rows = mm_nt(gains[...].astype(BF16), place)
    for which in range(3):
        grad = outs[3 + 2 * which]
        at = sum(BLOCKS[: 2 * which]) * rows
        column = jnp.zeros((rows, C), F32)
        for block in range(grad.shape[1] // C):
            weight = weights[at + block * rows : at + (block + 1) * rows, :].astype(F32)
            column = column + weight * grad[:, block * C : (block + 1) * C]
        column = jnp.sum(column, -1, keepdims=True)
        outs[which][...] = jnp.sum(eye * column, 0, keepdims=True) / gain_rows[which : which + 1]


def finish_kernel(scenes, d_packed, d_first, xhats, rstds, turned, gains, out):
    for scene in range(scenes):
        for half in range(2):
            step = 2 * scene + half
            for side in range(2):
                spot = slice(side * TOK, (side + 1) * TOK)
                d_normed = mm(d_packed[step, spot, :], turned[...])
                d_hidden = norm_backward(d_normed, xhats[step, spot, :], rstds[step, spot, :], gains[0:1, :])
                out[scene, :, half, :, side] = (d_first[step, spot, :] + d_hidden).reshape(VIEWS, WIN, WIN, C)


def merge(*threads, apart=0.0):
    spent = [apart * i for i in range(len(threads))]
    left = set(range(len(threads)))
    while left:
        which = min(left, key=lambda i: (spent[i], i))
        try:
            spent[which] += next(threads[which])
        except StopIteration:
            left.remove(which)


def paced(thread, rate):
    for share in thread:
        yield share * rate


def soft(scores):
    expo = jnp.exp2(scores - jnp.max(scores, -1, keepdims=True))
    return (expo * (1.0 / jnp.sum(expo, -1, keepdims=True))).astype(BF16)


def soft_back(probs, d_probs):
    probs = probs.astype(F32)
    delta = jnp.sum(d_probs * probs, -1, keepdims=True)
    return (probs * ((d_probs - delta) * SCALE)).astype(BF16)


def joined(pieces):
    return jnp.concatenate(pieces, 0)


def start_kernel(
    scenes, count, features, shard, offsets, depth_grad,
    lives, bias, x0s, xhats, rstds, shard_out, offsets_out, grad_out,
):
    of_key = iota((TOK, TOK), 1) // (WIN * WIN)
    of_query = iota((TOK, TOK), 0) // (WIN * WIN)
    for scene in range(scenes):
        live = count[scene]
        lives[scene] = jnp.broadcast_to(live, (8, C))
        bias[scene] = jnp.where((of_key < live) & (of_key != of_query), 0.0, MASKED)
    shard_out[...] = shard[...]
    offsets_out[...] = offsets[...]
    grad_out[...] = depth_grad[...]
    for scene in range(scenes):
        for half in range(2):
            step = 2 * scene + half
            piece = features[scene, :, half * HALF : (half + 1) * HALF, :]
            piece = piece.astype(F32).reshape(VIEWS, WIN, 2, WIN, C)
            for side in range(2):
                spot = slice(side * TOK, (side + 1) * TOK)
                x0 = piece[:, :, side].reshape(TOK, C)
                centred = x0 - jnp.mean(x0, -1, keepdims=True)
                spread = jnp.mean(centred * centred, -1, keepdims=True)
                rstd = lax.rsqrt(spread + 1e-05)
                x0s[step, spot, :] = x0
                xhats[step, spot, :] = centred * rstd
                rstds[step, spot, :] = jnp.broadcast_to(rstd, x0.shape)


def main_kernel(
    scenes,
    parts,
    lives,
    bias,
    x0s,
    xh_a,
    rs_a,
    offsets,
    depth_grad,
    *refs,
):
    packed, refs = refs[:parts], refs[parts:]
    (
    depth_out,
    d_packs,
    d_firsts,
    t_sq,
    gains,
    keep_out,
    send_out,
    w_sq, w_so, w_cq, w_co, w_fi, w_fo, w_rf,
    t_so, t_cq, t_co, t_fi, t_fo, t_rf, b_rf,
    x2s,
    xh_b, xh_c, rs_b, rs_c,
    no_a, no_b, no_c,
    qkv_a, qkv_b, p_a, p_b, o_a, o_b,
    gd, act,
    x3s, d3s,
    low, rev,
    pads, taps, back_taps,
    tables, eye, flip, hots,
    g_sq, g_so, g_cq, g_co, g_fi, g_fo, g_rf,
    ) = refs
    rows = C // parts
    me, side_of_rows = place_of(parts)

    total = jnp.zeros((GAIN_ROWS, C), F32)
    for apart, piece in enumerate(packed):
        shard = me ^ apart
        at = 0
        for ref, blocks in zip((w_sq, w_so, w_cq, w_co, w_fi, w_fo, w_rf), BLOCKS):
            height = blocks * rows if ref is w_fo else rows
            spot = pl.ds(pl.multiple_of(shard * height, 16), height)
            if ref is w_fo:
                ref[spot, :] = piece[at : at + height, :]
            else:
                for block in range(blocks):
                    ref[spot, block * C : (block + 1) * C] = piece[at + block * rows : at + (block + 1) * rows, :]
            at += blocks * rows
        total = total + piece[at : at + GAIN_ROWS, :].astype(F32)
    gains[...] = total[:8]
    for source, target in ((w_sq, t_sq), (w_so, t_so), (w_cq, t_cq), (w_co, t_co)):
        for block in range(source.shape[1] // C):
            target[block * C : (block + 1) * C, :] = source[:, block * C : (block + 1) * C].T
    for block in range(FFH // C):
        t_fi[block * C : (block + 1) * C, :] = w_fi[:, block * C : (block + 1) * C].T
        t_fo[:, block * C : (block + 1) * C] = w_fo[block * C : (block + 1) * C, :].T
    for tap in range(9):
        block = w_rf[:, tap * C : (tap + 1) * C]
        for ref, piece, at in ((t_rf, block.T, tap), (b_rf, block, 3 * (2 - tap // 3) + tap % 3)):
            ref[at * C : (at + 1) * C, :C] = piece
            ref[(at + 3) * C : (at + 4) * C, C:] = piece
    for ref in (t_rf, b_rf):
        ref[9 * C :, :C] = jnp.zeros((3 * C, C), BF16)
        ref[: 3 * C, C:] = jnp.zeros((3 * C, C), BF16)

    for ref in (g_sq, g_so, g_cq, g_co, g_fi, g_fo, g_rf, pads, hots):
        ref[...] = jnp.zeros_like(ref)
    empty = rows_of(parts) - sum(BLOCKS) * rows
    if empty:
        for ref in (keep_out, send_out):
            ref[...] = jnp.zeros_like(ref)
    for ref in (taps, back_taps):
        for scene in range(scenes):
            ref[scene, :, :HV, :] = jnp.zeros((VIEWS, HV, 3 * C), BF16)
            ref[scene, :, HV + PIX :, :] = jnp.zeros((VIEWS, HV, 3 * C), BF16)

    row = iota((HV, C), 0)
    lane = iota((HV, C), 1)
    tables[0:HV, :] = jnp.where((lane < HV) & (lane <= row), 0.5 * SCALE, 0.0)
    tables[HV : 2 * HV, :] = jnp.where((lane < HV) & (HV - 1 - lane <= row), 0.5 * SCALE, 0.0)
    tables[2 * HV : 3 * HV, :] = jnp.where(row > 0, 1.0, 0.0)
    tables[3 * HV : 4 * HV, :] = jnp.where(row < HV - 1, 1.0, 0.0)
    eye[...] = jnp.where(iota((HALF, HALF), 0) == iota((HALF, HALF), 1), 1.0, 0.0)
    flip[...] = (iota((HALF, HALF), 0) + iota((HALF, HALF), 1) == HALF - 1).astype(BF16)
    gain_a = gains[0:1, :]
    gain_b = gains[1:2, :]
    gain_c = gains[2:3, :]
    depth_values = 1.0 + 3.0 * iota((1, PLANES), 1).astype(F32) / (PLANES - 1)
    upper = [slice(part * HALF, (part + 1) * HALF) for part in range(2)]
    views = range(VIEWS)
    places = [slice(side * TOK, (side + 1) * TOK) for side in range(2)]
    windows = [slice(at * WIN * WIN, (at + 1) * WIN * WIN) for at in range(2 * VIEWS)]

    def attend(scene, half, side):
        step = 2 * scene + half
        spot = places[side]
        x0 = x0s[step, spot, :]
        normed = (xh_a[step, spot, :] * gain_a).astype(BF16)
        no_a[step, spot, :] = normed
        yield 100
        qkv = mm(normed, w_sq[...]).astype(BF16)
        qkv_a[step, spot, :] = qkv
        yield 300
        scores = joined([mm_nt(qkv[at, :C], qkv[at, C : 2 * C]) for at in windows[:VIEWS]])
        yield 200
        probs = soft(scores * (SCALE * LOG2E))
        p_a[step, spot, :] = probs
        yield 400
        mixed = joined([mm(probs[at], qkv[at, 2 * C :]) for at in windows[:VIEWS]]).astype(BF16)
        o_a[step, spot, :] = mixed
        yield 300
        x1 = x0 + mm(mixed, w_so[...])
        yield 200
        xhat, rstd, normed = norm_forward(x1, gain_b)
        xh_b[step, spot, :] = xhat
        rs_b[step, spot, :] = rstd
        no_b[step, spot, :] = normed
        yield 400
        qkv = mm(normed, w_cq[...]).astype(BF16)
        qkv_b[step, spot, :] = qkv
        yield 300
        scores = mm_nt(qkv[:, :C], qkv[:, C : 2 * C]) * (SCALE * LOG2E) + bias[scene]
        yield 300
        probs = soft(scores)
        p_b[step, spot, :] = probs
        yield 500
        mixed = mm(probs, qkv[:, 2 * C :]).astype(BF16)
        o_b[step, spot, :] = mixed
        yield 300
        x2 = x1 + mm(mixed, w_co[...])
        x2s[step, spot, :] = x2
        yield 200
        xhat, rstd, normed = norm_forward(x2, gain_c)
        xh_c[step, spot, :] = xhat
        rs_c[step, spot, :] = rstd
        no_c[step, spot, :] = normed
        yield 400

    def feed(scene, half):
        step = 2 * scene + half
        for block in range(FFH // C):
            cols = slice(block * C, (block + 1) * C)
            for at in places:
                inner = mm(no_c[step, at, :], w_fi[:, cols])
                cdf = 0.5 + 0.5 * lax.erf(inner * 0.5**0.5)
                bell = jnp.exp2(inner * inner * (-0.5 * LOG2E))
                gd[step, at, cols] = cdf + inner * bell * 0.3989422804014327
                act[step, at, cols] = (inner * cdf).astype(BF16)
                yield 100
        x3 = x2s[step] + mm(act[step], w_fo[...])
        for side in range(2):
            x3s[scene, :, half, :, side] = x3[places[side]].reshape(VIEWS, WIN, WIN, C)
        yield 300

    def by_row(value, table):
        return (value.reshape(-1, HV, C) * table).reshape(value.shape)

    def im2col(value, pad, dest, first, last):
        pad[8 : 8 + PIX, :] = value
        dest[HV : HV + PIX, C : 2 * C] = value.astype(BF16)
        before = by_row(pad[7 : 7 + PIX, :], tables[2 * HV : 3 * HV, :])
        after = by_row(pad[9 : 9 + PIX, :], tables[3 * HV : 4 * HV, :])
        dest[HV : HV + PIX, first * C : (first + 1) * C] = before.astype(BF16)
        dest[HV : HV + PIX, last * C : (last + 1) * C] = after.astype(BF16)

    def convolve(padded, kernel):
        rows_two = padded.reshape(HV // 2 + 1, 2, HV, 3 * C)
        columns = jnp.concatenate(
            [rows_two[a // 2 : a // 2 + HV // 2, a % 2].reshape(HALF, 3 * C) for a in range(4)], -1
        )
        both = mm(columns, kernel[...])
        return joined(
            [both[HV * (y // 2) : HV * (y // 2 + 1), C * (y % 2) : C * (y % 2 + 1)] for y in range(HV)]
        )

    def head(scene):
        live = lives[scene, 0:1, :]
        goes_on = {1: live > 2, 2: live > 3}

        def partner_of(ref, view, at):
            if view in goes_on:
                after, first = ref[scene, view + 1, at, :], ref[scene, 0, at, :]
                return jnp.where(goes_on[view], after.astype(F32), first.astype(F32)).astype(BF16)
            return ref[scene, (view + 1) % VIEWS, at, :]

        for view in views:
            low[scene, view] = x3s[scene, view].reshape(PIX, C).astype(BF16)
            shift = offsets[scene, view : view + 1, :]
            hots[scene, 0, view, 0:HV, :] = (shift == row).astype(BF16)
            hots[scene, 0, view, C : C + HV, :] = (shift == row).astype(BF16)
            hots[scene, 1, view, 0:HV, :] = (shift == HV - 1 - row).astype(BF16)
        yield 300
        for view in views:
            rev[scene, view] = unpaired(mm(flip[...], paired(low[scene, view])).astype(BF16))
        yield 400
        corrs = [[mm_nt(low[scene, view, at, :], partner_of(rev, view, at)) for at in upper] for view in views]
        yield 400
        skewed = [
            [by_row(pltpu.roll(corr, 1, 1, stride=1, stride_axis=0), tables[0:HV, :]) for corr in corrs[view]]
            for view in views
        ]
        yield 500
        cost = [mm(split_two(joined(skewed[view])), hots[scene, 0, view]) for view in views]
        yield 500
        for view in views:
            im2col(cost[view], pads.at[scene, 0, view], taps.at[scene, view], 0, 2)
            yield 80
        refined = []
        for view in views:
            refined.append(cost[view] + convolve(taps[scene, view], t_rf))
            yield 250
        d_refined = []
        for view in views:
            expo = jnp.exp2((refined[view] - jnp.max(refined[view], -1, keepdims=True)) * LOG2E)
            inverse = 1.0 / jnp.sum(expo, -1, keepdims=True)
            depth = jnp.sum(expo * depth_values, -1, keepdims=True) * inverse
            valid = jnp.where(view < live, 1.0, 0.0)
            incoming = []
            for at in upper:
                depth_out[scene, view : view + 1, at] = jnp.sum(eye[...] * depth[at], 0, keepdims=True)
                incoming.append(jnp.sum(eye[...] * depth_grad[scene, view : view + 1, at], 1, keepdims=True))
            weight = joined(incoming) * (inverse * valid)
            d_refined.append(expo * (weight * depth_values - weight * depth))
            yield 250
        for view in views:
            im2col(d_refined[view], pads.at[scene, 1, view], back_taps.at[scene, view], 2, 0)
            yield 80
        d_cost = []
        for view in views:
            d_cost.append(d_refined[view] + convolve(back_taps[scene, view], b_rf))
            yield 250
        for view in views:
            columns = jnp.concatenate([taps[scene, view, HV * a : HV * a + PIX, :] for a in range(3)], -1)
            g_rf[...] += mm_tn(back_taps[scene, view, HV : HV + PIX, C : 2 * C], columns)
            yield 250
        d_skewed = [
            mm_nt(split_two(d_cost[view]), jnp.concatenate([hots[scene, 1, view, :C, :]] * 2, -1)) for view in views
        ]
        yield 300
        d_corr = [
            [
                pltpu.roll(
                    by_row(d_skewed[view][at], tables[HV : 2 * HV, :]), HALF - HV + 1, 1, stride=1, stride_axis=0
                ).astype(BF16)
                for at in upper
            ]
            for view in views
        ]
        yield 250
        for part in range(2):
            at = upper[part]
            total = [mm(d_corr[view][part], partner_of(low, view, at)) for view in views]
            for view in views:
                there = mm_tn(d_corr[view][part], low[scene, view, at, :])
                if view in goes_on:
                    total[view + 1] = total[view + 1] + jnp.where(goes_on[view], there, 0.0)
                    total[0] = total[0] + jnp.where(goes_on[view], 0.0, there)
                else:
                    total[(view + 1) % VIEWS] = total[(view + 1) % VIEWS] + there
            for view in views:
                d3s[scene, view, part] = total[view].reshape(WIN, 2, WIN, C)
            yield 250

    def back(scene, half):
        step = 2 * scene + half
        both = range(2)
        d3 = [d3s[scene, :, half, :, side].reshape(TOK, C) for side in both]
        d_low = [d3[side].astype(BF16) for side in both]
        d_inner = [[], []]
        for block in range(FFH // C):
            cols = slice(block * C, (block + 1) * C)
            for side in both:
                d_inner[side].append((mm(d_low[side], t_fo[:, cols]) * gd[step, places[side], cols]).astype(BF16))
            yield 100
        d_inner = [jnp.concatenate(d_inner[side], -1) for side in both]
        d_normed = []
        for side in both:
            d_normed.append(mm(d_inner[side], t_fi[...]))
            yield 150
        g_fo[...] += mm_tn(joined(d_low), act[step])
        yield 250
        g_fi[...] += mm_tn(no_c[step], joined(d_inner))
        yield 250
        d2 = []
        for side in both:
            spot = places[side]
            d_hidden = norm_backward(d_normed[side], xh_c[step, spot, :], rs_c[step, spot, :], gain_c)
            d2.append(d3[side] + d_hidden)
            yield 150
        d_low = [d2[side].astype(BF16) for side in both]
        qkv = [qkv_b[step, spot, :] for spot in places]
        d_mixed = []
        for side in both:
            d_mixed.append(mm(d_low[side], t_co[...]).astype(BF16))
            yield 100
        g_co[...] += mm_tn(o_b[step], joined(d_low))
        yield 100
        d_packed = [[], []]
        d_raw = []
        for side in both:
            probs = p_b[step, places[side], :]
            d_values = mm_tn(probs, d_mixed[side])
            d_probs = mm_nt(d_mixed[side], qkv[side][:, 2 * C :])
            yield 150
            d_raw.append(soft_back(probs, d_probs))
            d_packed[side].append(d_values)
            yield 150
        for side in both:
            d_query = mm(d_raw[side], qkv[side][:, C : 2 * C])
            d_keys = mm_tn(d_raw[side], qkv[side][:, :C])
            d_packed[side] = jnp.concatenate([d_query, d_keys] + d_packed[side], -1).astype(BF16)
            yield 200
        d_normed = []
        for side in both:
            d_normed.append(mm(d_packed[side], t_cq[...]))
            yield 100
        g_cq[...] += mm_tn(no_b[step], joined(d_packed))
        yield 200
        d1 = []
        for side in both:
            spot = places[side]
            d_hidden = norm_backward(d_normed[side], xh_b[step, spot, :], rs_b[step, spot, :], gain_b)
            d1.append(d2[side] + d_hidden)
            yield 150
        d_low = [d1[side].astype(BF16) for side in both]
        qkv = [qkv_a[step, spot, :] for spot in places]
        d_mixed = []
        for side in both:
            d_mixed.append(mm(d_low[side], t_so[...]).astype(BF16))
            yield 100
        g_so[...] += mm_tn(o_a[step], joined(d_low))
        yield 100
        d_packed = [[], []]
        d_raw = []
        for side in both:
            probs = p_a[step, places[side], :]
            d_values = joined([mm_tn(probs[at], d_mixed[side][at]) for at in windows[:VIEWS]])
            d_probs = joined([mm_nt(d_mixed[side][at], qkv[side][at, 2 * C :]) for at in windows[:VIEWS]])
            yield 150
            d_raw.append(soft_back(probs, d_probs))
            d_packed[side].append(d_values)
            yield 100
        for side in both:
            d_query = joined([mm(d_raw[side][at], qkv[side][at, C : 2 * C]) for at in windows[:VIEWS]])
            d_keys = joined([mm_tn(d_raw[side][at], qkv[side][at, :C]) for at in windows[:VIEWS]])
            d_packed[side] = jnp.concatenate([d_query, d_keys] + d_packed[side], -1).astype(BF16)
            yield 150
        for side in both:
            d_packs[step, places[side], :] = d_packed[side]
            d_firsts[step, places[side], :] = d1[side]
            yield 50
        g_sq[...] += mm_tn(no_a[step], joined(d_packed))
        yield 200

    def chain(*threads):
        for thread in threads:
            yield from thread

    grads = (g_sq, g_so, g_cq, g_co, g_fi, w_fo, g_rf)

    def ship(*chosen):
        bits = bits_of(parts)
        half_rows = rows_of(parts) // 2
        for ref, blocks, before in zip(grads, BLOCKS, (sum(BLOCKS[:i]) for i in range(len(BLOCKS)))):
            if not any(ref is one for one in chosen):
                continue
            for apart in range(parts):
                shard = me ^ apart
                slot = sum(((apart >> bit) & 1) << (bits - 1 - bit) for bit in range(bits))
                dest = (keep_out, send_out)[slot // (parts // 2)].at[slot % (parts // 2)]
                for block in range(blocks):
                    if ref is w_fo:
                        spot = pl.ds(pl.multiple_of(shard * (blocks * rows) + block * rows, 16), rows)
                        value = ref[spot, :]
                    else:
                        spot = pl.ds(pl.multiple_of(shard * rows, 16), rows)
                        value = ref[spot, block * C : (block + 1) * C].astype(BF16)
                    for start in range(0, rows, 16):
                        which, offset = divmod((before + block) * rows + start, half_rows)
                        spot = pl.ds(pl.multiple_of((side_of_rows ^ which) * half_rows + offset, 16), 16)
                        dest[spot, :] = value[start : start + 16]
                yield 40

    def turn_back():
        for block in range(FFH // C):
            w_fo[block * C : (block + 1) * C, :] = g_fo[:, block * C : (block + 1) * C].T.astype(BF16)
            yield 30

    def whole_of(thread, total):
        return paced(thread, 1.0 / total)

    def attends(scene):
        return [whole_of(attend(scene, half, side), 4200) for half in range(2) for side in range(2)]

    def feeds(scene):
        return whole_of(chain(feed(scene, 0), feed(scene, 1)), 2200)

    def backs(*which):
        return [whole_of(back(*one), 5400) for one in which]

    merge(*attends(0), *attends(1), apart=0.02)
    merge(feeds(0), feeds(1))
    merge(whole_of(head(0), 7600), whole_of(head(1), 7600), apart=0.05)
    merge(*backs((0, 0), (0, 1), (1, 0), (1, 1)), whole_of(ship(g_rf), 160), apart=0.02)
    merge(chain(turn_back(), ship(w_fo)), ship(g_sq, g_so, g_cq, g_co, g_fi))


VMEM = pl.BlockSpec(memory_space=pltpu.VMEM)
HBM = pl.BlockSpec(memory_space=pltpu.HBM)
SMEM = pl.BlockSpec(memory_space=pltpu.SMEM)


def exchange(value, fsdp_mask, dp_mask):
    parts = lax.axis_size("fsdp")
    count = parts * lax.axis_size("dp")
    mask = dp_mask * parts + fsdp_mask
    return lax.ppermute(value, ("dp", "fsdp"), [(i, i ^ mask) for i in range(count)])


def local(
    features,
    view_count,
    plane_offsets,
    depth_grad,
    gain_self,
    self_qkv,
    self_out,
    gain_cross,
    cross_qkv,
    cross_out,
    gain_ff,
    ff_in,
    ff_out,
    refine,
):
    parts = lax.axis_size("fsdp")
    copies = lax.axis_size("dp")
    scenes = features.shape[0]
    rows = C // parts
    shard_rows = rows_of(parts)
    small = pltpu.CompilerParams(vmem_limit_bytes=8 * MIB)

    pack = pl.pallas_call(
        functools.partial(pack_kernel, parts),
        out_shape=jax.ShapeDtypeStruct((sum(BLOCKS) * rows + GAIN_ROWS, C), BF16),
        in_specs=[HBM] * 10,
        out_specs=VMEM,
        scratch_shapes=[pltpu.VMEM((3, 1, rows), BF16), pltpu.SemaphoreType.DMA((3 + sum(BLOCKS),))],
        compiler_params=pltpu.CompilerParams(vmem_limit_bytes=8 * MIB),
        name="pack",
    )
    own = [gain.reshape(1, rows) for gain in (gain_self, gain_cross, gain_ff)]
    own += [self_qkv, self_out, cross_qkv, cross_out, ff_in, ff_out, refine]
    shard = pack(*[pltpu.with_memory_space_constraint(one, pltpu.HBM) for one in own])
    steps = scenes * (HV // WIN)
    span = 2 * TOK
    start = pl.pallas_call(
        functools.partial(start_kernel, scenes),
        out_shape=(
            jax.ShapeDtypeStruct((scenes, 8, C), jnp.int32),
            jax.ShapeDtypeStruct((scenes, TOK, TOK), F32),
        )
        + (jax.ShapeDtypeStruct((steps, span, C), F32),) * 3
        + tuple(jax.ShapeDtypeStruct(piece.shape, piece.dtype) for piece in (shard, plane_offsets, depth_grad)),
        in_specs=[SMEM] + [VMEM] * 4,
        out_specs=(VMEM,) * 8,
        compiler_params=small,
        cost_estimate=pl.CostEstimate(flops=10 * features.size, bytes_accessed=14 * features.size, transcendentals=0),
        name="start",
    )
    began = start(view_count, features, shard, plane_offsets, depth_grad)

    packed = {0: shard}
    for bit in reversed(range(bits_of(parts))):
        came = {apart | (1 << bit): exchange(piece, 1 << bit, 0) for apart, piece in packed.items()}
        if len(packed) == 1:
            came, began = lax.optimization_barrier((came, began))
        packed |= came
    packed = [packed[apart] for apart in range(parts)]

    scratch = [
        ((C, 3 * C), BF16), ((C, C), BF16), ((C, 3 * C), BF16), ((C, C), BF16),
        ((C, FFH), BF16), ((FFH, C), BF16), ((C, 9 * PLANES), BF16),
        ((C, C), BF16), ((3 * C, C), BF16), ((C, C), BF16),
        ((FFH, C), BF16), ((C, FFH), BF16), ((12 * PLANES, 2 * C), BF16), ((12 * PLANES, 2 * C), BF16),
        ((steps, span, C), F32),
    ]
    scratch += [((steps, span, C), F32)] * 4
    scratch += [((steps, span, C), BF16)] * 3
    scratch += [
        ((steps, span, 3 * C), BF16), ((steps, span, 3 * C), BF16),
        ((steps, span, WIN * WIN), BF16), ((steps, span, TOK), BF16),
        ((steps, span, C), BF16), ((steps, span, C), BF16),
        ((steps, span, FFH), F32), ((steps, span, FFH), BF16),
        ((scenes, VIEWS, 2, WIN, 2, WIN, C), F32), ((scenes, VIEWS, 2, WIN, 2, WIN, C), F32),
        ((scenes, VIEWS, PIX, C), BF16), ((scenes, VIEWS, PIX, C), BF16),
        ((scenes, 2, VIEWS, PIX + 16, C), F32),
        ((scenes, VIEWS, PIX + 2 * HV, 3 * C), BF16), ((scenes, VIEWS, PIX + 2 * HV, 3 * C), BF16),
        ((4 * HV, C), F32), ((HALF, HALF), F32), ((HALF, HALF), BF16), ((scenes, 2, VIEWS, 2 * C, C), BF16),
        ((C, 3 * C), F32), ((C, C), F32), ((C, 3 * C), F32), ((C, C), F32),
        ((C, FFH), F32), ((C, FFH), F32), ((C, 9 * PLANES), F32),
    ]
    main = pl.pallas_call(
        functools.partial(main_kernel, scenes, parts),
        out_shape=(
            jax.ShapeDtypeStruct((scenes, VIEWS, PIX), F32),
            jax.ShapeDtypeStruct((steps, span, 3 * C), BF16),
            jax.ShapeDtypeStruct((steps, span, C), F32),
            jax.ShapeDtypeStruct((3 * C, C), BF16),
            jax.ShapeDtypeStruct((8, C), F32),
            jax.ShapeDtypeStruct((parts // 2, shard_rows, C), BF16),
            jax.ShapeDtypeStruct((parts // 2, shard_rows, C), BF16),
        ),
        in_specs=[VMEM] * (7 + parts),
        out_specs=(VMEM,) * 7,
        scratch_shapes=[pltpu.VMEM(shape, kind) for shape, kind in scratch],
        compiler_params=pltpu.CompilerParams(vmem_limit_bytes=46 * MIB),
        name="layer",
    )
    lives, bias, x0s, xhats, rstds, packed[0], plane_offsets, depth_grad = began
    depth, d_packs, d_firsts, turned, gains, keep, send = main(
        lives, bias, x0s, xhats, rstds, plane_offsets, depth_grad, *packed
    )

    finish = pl.pallas_call(
        functools.partial(finish_kernel, scenes),
        out_shape=jax.ShapeDtypeStruct((scenes, VIEWS, 2, WIN, 2, WIN, C), F32),
        in_specs=[VMEM] * 6,
        out_specs=VMEM,
        compiler_params=small,
        cost_estimate=pl.CostEstimate(flops=6 * C * features.size, bytes_accessed=16 * features.size, transcendentals=0),
        name="finish",
    )
    grad_features = finish(d_packs, d_firsts, xhats, rstds, turned, gains).reshape(features.shape)

    for bit in range(bits_of(parts) - 1):
        middle = keep.shape[0] // 2
        onward = keep[middle:] + exchange(send[middle:], 1 << bit, 0)
        keep, send = keep[:middle] + exchange(send[:middle], 1 << bit, 0), onward
    last = parts // 2
    half = shard_rows // 2
    beside = exchange(send[0, :half], last, 0)
    across = exchange(keep[0, half:], 0, 1)
    corner = exchange(send[0, half:], last, 1)
    grads = (keep[0, :half].astype(F32) + beside) + (across.astype(F32) + corner)
    grads = grads.astype(BF16)
    for bit in reversed(range(2, bits_of(copies))):
        grads = grads + exchange(grads, 0, 1 << bit)
    if bits_of(copies) > 1:
        along = exchange(grads, 0, 2)
        swapped = exchange(grads, 0, 1)
        corner = exchange(grads, 0, 3)
        mine, other = (grads, along), (swapped, corner)
    else:
        mine, other = (grads,), (exchange(grads, 0, 1),)

    unpack = pl.pallas_call(
        functools.partial(unpack_kernel, parts),
        out_shape=tuple(jax.ShapeDtypeStruct((1, rows), F32) for _ in range(3))
        + tuple(
            jax.ShapeDtypeStruct(piece.shape, F32)
            for piece in (self_qkv, self_out, cross_qkv, cross_out, ff_in, ff_out, refine)
        ),
        in_specs=[VMEM] * (2 + 2 * len(mine)),
        out_specs=(VMEM,) * 10,
        scratch_shapes=[pltpu.VMEM((shard_rows, C), F32)],
        compiler_params=small,
        name="unpack",
    )
    ga, gb, gc, d_sq, d_so, d_cq, d_co, d_fi, d_fo, d_rf = unpack(
        gains, packed[0], *mine, *other
    )
    return (
        depth * (jnp.arange(VIEWS) < view_count[:, None])[:, :, None],
        grad_features,
        ga.reshape(rows),
        d_sq,
        d_so,
        gb.reshape(rows),
        d_cq,
        d_co,
        gc.reshape(rows),
        d_fi,
        d_fo,
        d_rf,
    )


def solution(mesh):
    placed = (
        P(("dp", "fsdp"), None, None, None),
        P(("dp", "fsdp")),
        P(("dp", "fsdp"), None, None),
        P(("dp", "fsdp"), None, None),
        P("fsdp"),
        P("fsdp", None),
        P("fsdp", None),
        P("fsdp"),
        P("fsdp", None),
        P("fsdp", None),
        P("fsdp"),
        P("fsdp", None),
        P("fsdp", None),
        P("fsdp", None),
    )
    return jax.shard_map(
        local,
        mesh=mesh,
        in_specs=placed,
        out_specs=(
            P(("dp", "fsdp"), None, None),
            P(("dp", "fsdp"), None, None, None),
            P("fsdp"),
            P("fsdp", None),
            P("fsdp", None),
            P("fsdp"),
            P("fsdp", None),
            P("fsdp", None),
            P("fsdp"),
            P("fsdp", None),
            P("fsdp", None),
            P("fsdp", None),
        ),
        check_vma=False,
    )
```

```python
import functools

import jax
import jax.numpy as jnp
from jax import lax
from jax.experimental import pallas as pl
from jax.experimental.pallas import tpu as pltpu
from jax.sharding import PartitionSpec as P

C = 128
FFH = 512
PLANES = 128
WIN = 8
VIEWS = 4
HV = 16
PIX = HV * HV
TOK = VIEWS * WIN * WIN
HALF = PIX // 2
GAIN_ROWS = 16
MASKED = -1e30
SCALE = C**-0.5
LOG2E = 1.4426950408889634
F32 = jnp.float32
BF16 = jnp.bfloat16
BLOCKS = (3, 1, 3, 1, 4, 4, 9)
MIB = 1024 * 1024


def mm(left, right):
    return lax.dot_general(left, right, (((1,), (0,)), ((), ())), preferred_element_type=F32)


def mm_nt(left, right):
    return lax.dot_general(left, right, (((1,), (1,)), ((), ())), preferred_element_type=F32)


def mm_tn(left, right):
    return lax.dot_general(left, right, (((0,), (0,)), ((), ())), preferred_element_type=F32)


def paired(value):
    half = value.shape[0] // 2
    return jnp.concatenate([value[:half], value[half:]], -1)


def unpaired(value):
    half = value.shape[1] // 2
    return jnp.concatenate([value[:, :half], value[:, half:]], 0)


def norm_forward(value, gain):
    centred = value - jnp.mean(value, -1, keepdims=True)
    spread = jnp.mean(centred * centred, -1, keepdims=True)
    rstd = lax.rsqrt(spread + 1e-05)
    xhat = centred * rstd
    return xhat, jnp.broadcast_to(rstd, value.shape), (xhat * gain).astype(BF16)


def norm_backward(d_normed, xhat, rstd, gain):
    d_xhat = d_normed * gain
    mean_d = jnp.mean(d_xhat, -1, keepdims=True)
    mean_dx = jnp.mean(d_xhat * xhat, -1, keepdims=True)
    return rstd * (d_xhat - mean_d - xhat * mean_dx)


def split_two(value):
    high = value.astype(BF16)
    return jnp.concatenate([high, (value - high.astype(F32)).astype(BF16)], -1)


def iota(shape, axis):
    return lax.broadcasted_iota(jnp.int32, shape, axis)


def bits_of(size):
    return size.bit_length() - 1


def rows_of(parts):
    return -(-sum(BLOCKS) * (C // parts) // 32) * 32


def place_of(parts):
    return lax.axis_index("fsdp").astype(jnp.int32), (lax.axis_index("dp") & 1).astype(jnp.int32)


def gain_lines(parts, gains):
    rows = C // parts
    place = (iota((rows, C), 1) == iota((rows, C), 0) + place_of(parts)[0] * rows).astype(BF16)
    line = iota((GAIN_ROWS, C), 0)
    total = jnp.zeros((GAIN_ROWS, C), F32)
    for which in range(3):
        row = mm(jnp.broadcast_to(gains[which][...], (8, rows)), place)[:1]
        total = jnp.where(line == which, row, total)
    return total


def pack_kernel(parts, *refs):
    gains, weights, out, scratch, sems = refs[:3], refs[3:10], refs[10], refs[11], refs[12]
    rows = C // parts
    copies = []

    def copy(source, target):
        copies.append(pltpu.make_async_copy(source, target, sems.at[len(copies)]))
        copies[-1].start()

    for which in range(3):
        copy(gains[which], scratch.at[which])
    at = 0
    for ref, blocks in zip(weights, BLOCKS):
        if ref.shape[0] == blocks * rows and ref.shape[1] == C:
            copy(ref, out.at[at : at + blocks * rows, :])
        else:
            for block in range(blocks):
                copy(ref.at[:, block * C : (block + 1) * C], out.at[at + block * rows : at + (block + 1) * rows, :])
        at += blocks * rows
    for one in copies[:3]:
        one.wait()
    total = gain_lines(parts, [scratch.at[which] for which in range(3)])
    out[at : at + GAIN_ROWS, :] = total.astype(BF16)
    for one in copies[3:]:
        one.wait()


def unpack_kernel(parts, *refs):
    gains, weights, refs = refs[0], refs[1], refs[2:]
    terms = (len(refs) - 11) // 2
    own, other, outs = refs[:terms], refs[terms : 2 * terms], refs[2 * terms :]
    rows = C // parts
    me, side = place_of(parts)
    whole = outs[-1]
    half = own[0].shape[0]
    for first, pieces in ((side, own), (1 - side, other)):
        whole[pl.ds(pl.multiple_of(first * half, 8), half), :] = sum(piece[...].astype(F32) for piece in pieces)
    at = 0
    for out, blocks in zip(outs[3:10], BLOCKS):
        if out.shape[0] == blocks * rows and out.shape[1] == C:
            out[...] = whole[at : at + blocks * rows, :]
        else:
            for block in range(blocks):
                out[:, block * C : (block + 1) * C] = whole[at + block * rows : at + (block + 1) * rows, :]
        at += blocks * rows
    eye = (iota((rows, rows), 0) == iota((rows, rows), 1)).astype(F32)
    place = (iota((rows, C), 1) == iota((rows, C), 0) + me * rows).astype(BF16)
    gain_rows = mm_nt(gains[...].astype(BF16), place)
    for which in range(3):
        grad = outs[3 + 2 * which]
        at = sum(BLOCKS[: 2 * which]) * rows
        column = jnp.zeros((rows, C), F32)
        for block in range(grad.shape[1] // C):
            weight = weights[at + block * rows : at + (block + 1) * rows, :].astype(F32)
            column = column + weight * grad[:, block * C : (block + 1) * C]
        column = jnp.sum(column, -1, keepdims=True)
        outs[which][...] = jnp.sum(eye * column, 0, keepdims=True) / gain_rows[which : which + 1]


def finish_kernel(scenes, d_packed, d_first, xhats, rstds, turned, gains, out):
    for scene in range(scenes):
        for half in range(2):
            step = 2 * scene + half
            for side in range(2):
                spot = slice(side * TOK, (side + 1) * TOK)
                d_normed = mm(d_packed[step, spot, :], turned[...])
                d_hidden = norm_backward(d_normed, xhats[step, spot, :], rstds[step, spot, :], gains[0:1, :])
                out[scene, :, half, :, side] = (d_first[step, spot, :] + d_hidden).reshape(VIEWS, WIN, WIN, C)


def merge(*threads, apart=0.0):
    spent = [apart * i for i in range(len(threads))]
    left = set(range(len(threads)))
    while left:
        which = min(left, key=lambda i: (spent[i], i))
        try:
            spent[which] += next(threads[which])
        except StopIteration:
            left.remove(which)


def paced(thread, rate):
    for share in thread:
        yield share * rate


def soft(scores):
    expo = jnp.exp2(scores - jnp.max(scores, -1, keepdims=True))
    return (expo * (1.0 / jnp.sum(expo, -1, keepdims=True))).astype(BF16)


def soft_back(probs, d_probs):
    probs = probs.astype(F32)
    delta = jnp.sum(d_probs * probs, -1, keepdims=True)
    return (probs * ((d_probs - delta) * SCALE)).astype(BF16)


def joined(pieces):
    return jnp.concatenate(pieces, 0)


def start_kernel(
    scenes, count, features, shard, offsets, depth_grad,
    lives, bias, x0s, xhats, rstds, shard_out, hots, incoming,
):
    of_key = iota((TOK, TOK), 1) // (WIN * WIN)
    of_query = iota((TOK, TOK), 0) // (WIN * WIN)
    for scene in range(scenes):
        live = count[scene]
        lives[scene] = jnp.broadcast_to(live, (8, C))
        bias[scene] = jnp.where((of_key < live) & (of_key != of_query), 0.0, MASKED)
    shard_out[...] = shard[...]
    row = iota((HV, C), 0)
    eye = jnp.where(iota((HALF, HALF), 0) == iota((HALF, HALF), 1), 1.0, 0.0)
    hots[...] = jnp.zeros_like(hots)
    for scene in range(scenes):
        for view in range(VIEWS):
            shift = offsets[scene, view : view + 1, :]
            hot = (shift == row).astype(BF16)
            hots[scene, 0, view, 0:HV, :] = hot
            hots[scene, 0, view, C : C + HV, :] = hot
            hots[scene, 1, view, 0:HV, :] = (shift == HV - 1 - row).astype(BF16)
            for part in range(2):
                at = slice(part * HALF, (part + 1) * HALF)
                column = jnp.sum(eye * depth_grad[scene, view : view + 1, at], 1, keepdims=True)
                incoming[scene, view, at, :] = jnp.broadcast_to(column, (HALF, C))
    for scene in range(scenes):
        for half in range(2):
            step = 2 * scene + half
            piece = features[scene, :, half * HALF : (half + 1) * HALF, :]
            piece = piece.astype(F32).reshape(VIEWS, WIN, 2, WIN, C)
            for side in range(2):
                spot = slice(side * TOK, (side + 1) * TOK)
                x0 = piece[:, :, side].reshape(TOK, C)
                centred = x0 - jnp.mean(x0, -1, keepdims=True)
                spread = jnp.mean(centred * centred, -1, keepdims=True)
                rstd = lax.rsqrt(spread + 1e-05)
                x0s[step, spot, :] = x0
                xhats[step, spot, :] = centred * rstd
                rstds[step, spot, :] = jnp.broadcast_to(rstd, x0.shape)


def main_kernel(
    scenes,
    parts,
    lives,
    bias,
    x0s,
    xh_a,
    rs_a,
    hots,
    incoming,
    *refs,
):
    packed, refs = refs[:parts], refs[parts:]
    (
    depth_out,
    d_packs,
    d_firsts,
    t_sq,
    gains,
    keep_out,
    send_out,
    w_sq, w_so, w_cq, w_co, w_fi, w_fo, w_rf,
    t_so, t_cq, t_co, t_fi, t_fo, t_rf, b_rf,
    x2s,
    xh_b, xh_c, rs_b, rs_c,
    no_a, no_b, no_c,
    qkv_a, qkv_b, p_a, p_b, o_a, o_b,
    gd, act,
    x3s, d3s,
    low, rev,
    pads, taps, back_taps,
    tables, eye, flip,
    g_sq, g_so, g_cq, g_co, g_fi, g_fo, g_rf,
    ) = refs
    rows = C // parts
    me, side_of_rows = place_of(parts)

    total = jnp.zeros((GAIN_ROWS, C), F32)
    for apart, piece in enumerate(packed):
        shard = me ^ apart
        at = 0
        for ref, blocks in zip((w_sq, w_so, w_cq, w_co, w_fi, w_fo, w_rf), BLOCKS):
            height = blocks * rows if ref is w_fo else rows
            spot = pl.ds(pl.multiple_of(shard * height, 16), height)
            if ref is w_fo:
                ref[spot, :] = piece[at : at + height, :]
            else:
                for block in range(blocks):
                    ref[spot, block * C : (block + 1) * C] = piece[at + block * rows : at + (block + 1) * rows, :]
            at += blocks * rows
        total = total + piece[at : at + GAIN_ROWS, :].astype(F32)
    gains[...] = total[:8]
    for source, target in ((w_sq, t_sq), (w_so, t_so), (w_cq, t_cq), (w_co, t_co)):
        for block in range(source.shape[1] // C):
            target[block * C : (block + 1) * C, :] = source[:, block * C : (block + 1) * C].T
    for block in range(FFH // C):
        t_fi[block * C : (block + 1) * C, :] = w_fi[:, block * C : (block + 1) * C].T
        t_fo[:, block * C : (block + 1) * C] = w_fo[block * C : (block + 1) * C, :].T
    for tap in range(9):
        block = w_rf[:, tap * C : (tap + 1) * C]
        for ref, piece, at in ((t_rf, block.T, tap), (b_rf, block, 3 * (2 - tap // 3) + tap % 3)):
            ref[at * C : (at + 1) * C, :C] = piece
            ref[(at + 3) * C : (at + 4) * C, C:] = piece
    for ref in (t_rf, b_rf):
        ref[9 * C :, :C] = jnp.zeros((3 * C, C), BF16)
        ref[: 3 * C, C:] = jnp.zeros((3 * C, C), BF16)

    for ref in (g_sq, g_so, g_cq, g_co, g_fi, g_fo, g_rf, pads):
        ref[...] = jnp.zeros_like(ref)
    empty = rows_of(parts) - sum(BLOCKS) * rows
    if empty:
        for ref in (keep_out, send_out):
            ref[...] = jnp.zeros_like(ref)
    for ref in (taps, back_taps):
        for scene in range(scenes):
            ref[scene, :, :HV, :] = jnp.zeros((VIEWS, HV, 3 * C), BF16)
            ref[scene, :, HV + PIX :, :] = jnp.zeros((VIEWS, HV, 3 * C), BF16)

    row = iota((HV, C), 0)
    lane = iota((HV, C), 1)
    tables[0:HV, :] = jnp.where((lane < HV) & (lane <= row), 0.5 * SCALE, 0.0)
    tables[HV : 2 * HV, :] = jnp.where((lane < HV) & (HV - 1 - lane <= row), 0.5 * SCALE, 0.0)
    tables[2 * HV : 3 * HV, :] = jnp.where(row > 0, 1.0, 0.0)
    tables[3 * HV : 4 * HV, :] = jnp.where(row < HV - 1, 1.0, 0.0)
    eye[...] = jnp.where(iota((HALF, HALF), 0) == iota((HALF, HALF), 1), 1.0, 0.0)
    flip[...] = (iota((HALF, HALF), 0) + iota((HALF, HALF), 1) == HALF - 1).astype(BF16)
    gain_a = gains[0:1, :]
    gain_b = gains[1:2, :]
    gain_c = gains[2:3, :]
    depth_values = 1.0 + 3.0 * iota((1, PLANES), 1).astype(F32) / (PLANES - 1)
    upper = [slice(part * HALF, (part + 1) * HALF) for part in range(2)]
    views = range(VIEWS)
    places = [slice(side * TOK, (side + 1) * TOK) for side in range(2)]
    windows = [slice(at * WIN * WIN, (at + 1) * WIN * WIN) for at in range(2 * VIEWS)]

    def attend(scene, half, side):
        step = 2 * scene + half
        spot = places[side]
        x0 = x0s[step, spot, :]
        normed = (xh_a[step, spot, :] * gain_a).astype(BF16)
        no_a[step, spot, :] = normed
        yield 100
        qkv = mm(normed, w_sq[...]).astype(BF16)
        qkv_a[step, spot, :] = qkv
        yield 300
        scores = joined([mm_nt(qkv[at, :C], qkv[at, C : 2 * C]) for at in windows[:VIEWS]])
        yield 200
        probs = soft(scores * (SCALE * LOG2E))
        p_a[step, spot, :] = probs
        yield 400
        mixed = joined([mm(probs[at], qkv[at, 2 * C :]) for at in windows[:VIEWS]]).astype(BF16)
        o_a[step, spot, :] = mixed
        yield 300
        x1 = x0 + mm(mixed, w_so[...])
        yield 200
        xhat, rstd, normed = norm_forward(x1, gain_b)
        xh_b[step, spot, :] = xhat
        rs_b[step, spot, :] = rstd
        no_b[step, spot, :] = normed
        yield 400
        qkv = mm(normed, w_cq[...]).astype(BF16)
        qkv_b[step, spot, :] = qkv
        yield 300
        scores = mm_nt(qkv[:, :C], qkv[:, C : 2 * C]) * (SCALE * LOG2E) + bias[scene]
        yield 300
        probs = soft(scores)
        p_b[step, spot, :] = probs
        yield 500
        mixed = mm(probs, qkv[:, 2 * C :]).astype(BF16)
        o_b[step, spot, :] = mixed
        yield 300
        x2 = x1 + mm(mixed, w_co[...])
        x2s[step, spot, :] = x2
        yield 200
        xhat, rstd, normed = norm_forward(x2, gain_c)
        xh_c[step, spot, :] = xhat
        rs_c[step, spot, :] = rstd
        no_c[step, spot, :] = normed
        yield 400

    def feed(scene, half):
        step = 2 * scene + half
        for block in range(FFH // C):
            cols = slice(block * C, (block + 1) * C)
            for at in places:
                inner = mm(no_c[step, at, :], w_fi[:, cols])
                cdf = 0.5 + 0.5 * lax.erf(inner * 0.5**0.5)
                bell = jnp.exp2(inner * inner * (-0.5 * LOG2E))
                gd[step, at, cols] = cdf + inner * bell * 0.3989422804014327
                act[step, at, cols] = (inner * cdf).astype(BF16)
                yield 100
        x3 = x2s[step] + mm(act[step], w_fo[...])
        for side in range(2):
            x3s[scene, :, half, :, side] = x3[places[side]].reshape(VIEWS, WIN, WIN, C)
        yield 300

    def by_row(value, table):
        return (value.reshape(-1, HV, C) * table).reshape(value.shape)

    def im2col(value, pad, dest, first, last):
        pad[8 : 8 + PIX, :] = value
        dest[HV : HV + PIX, C : 2 * C] = value.astype(BF16)
        before = by_row(pad[7 : 7 + PIX, :], tables[2 * HV : 3 * HV, :])
        after = by_row(pad[9 : 9 + PIX, :], tables[3 * HV : 4 * HV, :])
        dest[HV : HV + PIX, first * C : (first + 1) * C] = before.astype(BF16)
        dest[HV : HV + PIX, last * C : (last + 1) * C] = after.astype(BF16)

    def convolve(padded, kernel):
        rows_two = padded.reshape(HV // 2 + 1, 2, HV, 3 * C)
        columns = jnp.concatenate(
            [rows_two[a // 2 : a // 2 + HV // 2, a % 2].reshape(HALF, 3 * C) for a in range(4)], -1
        )
        both = mm(columns, kernel[...])
        return joined(
            [both[HV * (y // 2) : HV * (y // 2 + 1), C * (y % 2) : C * (y % 2 + 1)] for y in range(HV)]
        )

    def head(scene):
        live = lives[scene, 0:1, :]
        goes_on = {1: live > 2, 2: live > 3}

        def partner_of(ref, view, at):
            if view in goes_on:
                after, first = ref[scene, view + 1, at, :], ref[scene, 0, at, :]
                return jnp.where(goes_on[view], after.astype(F32), first.astype(F32)).astype(BF16)
            return ref[scene, (view + 1) % VIEWS, at, :]

        for view in views:
            low[scene, view] = x3s[scene, view].reshape(PIX, C).astype(BF16)
        yield 300
        for view in views:
            rev[scene, view] = unpaired(mm(flip[...], paired(low[scene, view])).astype(BF16))
        yield 400
        corrs = [[mm_nt(low[scene, view, at, :], partner_of(rev, view, at)) for at in upper] for view in views]
        yield 400
        skewed = [
            [by_row(pltpu.roll(corr, 1, 1, stride=1, stride_axis=0), tables[0:HV, :]) for corr in corrs[view]]
            for view in views
        ]
        yield 500
        cost = [mm(split_two(joined(skewed[view])), hots[scene, 0, view]) for view in views]
        yield 500
        for view in views:
            im2col(cost[view], pads.at[scene, 0, view], taps.at[scene, view], 0, 2)
            yield 80
        refined = []
        for view in views:
            refined.append(cost[view] + convolve(taps[scene, view], t_rf))
            yield 250
        d_refined = []
        for view in views:
            expo = jnp.exp2((refined[view] - jnp.max(refined[view], -1, keepdims=True)) * LOG2E)
            inverse = 1.0 / jnp.sum(expo, -1, keepdims=True)
            depth = jnp.sum(expo * depth_values, -1, keepdims=True) * inverse
            valid = jnp.where(view < live, 1.0, 0.0)
            for at in upper:
                depth_out[scene, view : view + 1, at] = jnp.sum(eye[...] * depth[at], 0, keepdims=True)
            weight = incoming[scene, view] * (inverse * valid)
            d_refined.append(expo * (weight * depth_values - weight * depth))
            yield 250
        for view in views:
            im2col(d_refined[view], pads.at[scene, 1, view], back_taps.at[scene, view], 2, 0)
            yield 80
        d_cost = []
        for view in views:
            d_cost.append(d_refined[view] + convolve(back_taps[scene, view], b_rf))
            yield 250
        for view in views:
            columns = jnp.concatenate([taps[scene, view, HV * a : HV * a + PIX, :] for a in range(3)], -1)
            g_rf[...] += mm_tn(back_taps[scene, view, HV : HV + PIX, C : 2 * C], columns)
            yield 250
        d_skewed = [
            mm_nt(split_two(d_cost[view]), jnp.concatenate([hots[scene, 1, view, :C, :]] * 2, -1)) for view in views
        ]
        yield 300
        d_corr = [
            [
                pltpu.roll(
                    by_row(d_skewed[view][at], tables[HV : 2 * HV, :]), HALF - HV + 1, 1, stride=1, stride_axis=0
                ).astype(BF16)
                for at in upper
            ]
            for view in views
        ]
        yield 250
        for part in range(2):
            at = upper[part]
            total = [mm(d_corr[view][part], partner_of(low, view, at)) for view in views]
            for view in views:
                there = mm_tn(d_corr[view][part], low[scene, view, at, :])
                if view in goes_on:
                    total[view + 1] = total[view + 1] + jnp.where(goes_on[view], there, 0.0)
                    total[0] = total[0] + jnp.where(goes_on[view], 0.0, there)
                else:
                    total[(view + 1) % VIEWS] = total[(view + 1) % VIEWS] + there
            for view in views:
                d3s[scene, view, part] = total[view].reshape(WIN, 2, WIN, C)
            yield 250

    def back(scene, half):
        step = 2 * scene + half
        both = range(2)
        d3 = [d3s[scene, :, half, :, side].reshape(TOK, C) for side in both]
        d_low = [d3[side].astype(BF16) for side in both]
        d_inner = [[], []]
        for block in range(FFH // C):
            cols = slice(block * C, (block + 1) * C)
            for side in both:
                d_inner[side].append((mm(d_low[side], t_fo[:, cols]) * gd[step, places[side], cols]).astype(BF16))
            yield 100
        d_inner = [jnp.concatenate(d_inner[side], -1) for side in both]
        d_normed = []
        for side in both:
            d_normed.append(mm(d_inner[side], t_fi[...]))
            yield 150
        g_fo[...] += mm_tn(joined(d_low), act[step])
        yield 250
        g_fi[...] += mm_tn(no_c[step], joined(d_inner))
        yield 250
        d2 = []
        for side in both:
            spot = places[side]
            d_hidden = norm_backward(d_normed[side], xh_c[step, spot, :], rs_c[step, spot, :], gain_c)
            d2.append(d3[side] + d_hidden)
            yield 150
        d_low = [d2[side].astype(BF16) for side in both]
        qkv = [qkv_b[step, spot, :] for spot in places]
        d_mixed = []
        for side in both:
            d_mixed.append(mm(d_low[side], t_co[...]).astype(BF16))
            yield 100
        g_co[...] += mm_tn(o_b[step], joined(d_low))
        yield 100
        d_packed = [[], []]
        d_raw = []
        for side in both:
            probs = p_b[step, places[side], :]
            d_values = mm_tn(probs, d_mixed[side])
            d_probs = mm_nt(d_mixed[side], qkv[side][:, 2 * C :])
            yield 150
            d_raw.append(soft_back(probs, d_probs))
            d_packed[side].append(d_values)
            yield 150
        for side in both:
            d_query = mm(d_raw[side], qkv[side][:, C : 2 * C])
            d_keys = mm_tn(d_raw[side], qkv[side][:, :C])
            d_packed[side] = jnp.concatenate([d_query, d_keys] + d_packed[side], -1).astype(BF16)
            yield 200
        d_normed = []
        for side in both:
            d_normed.append(mm(d_packed[side], t_cq[...]))
            yield 100
        g_cq[...] += mm_tn(no_b[step], joined(d_packed))
        yield 200
        d1 = []
        for side in both:
            spot = places[side]
            d_hidden = norm_backward(d_normed[side], xh_b[step, spot, :], rs_b[step, spot, :], gain_b)
            d1.append(d2[side] + d_hidden)
            yield 150
        d_low = [d1[side].astype(BF16) for side in both]
        qkv = [qkv_a[step, spot, :] for spot in places]
        d_mixed = []
        for side in both:
            d_mixed.append(mm(d_low[side], t_so[...]).astype(BF16))
            yield 100
        g_so[...] += mm_tn(o_a[step], joined(d_low))
        yield 100
        d_packed = [[], []]
        d_raw = []
        for side in both:
            probs = p_a[step, places[side], :]
            d_values = joined([mm_tn(probs[at], d_mixed[side][at]) for at in windows[:VIEWS]])
            d_probs = joined([mm_nt(d_mixed[side][at], qkv[side][at, 2 * C :]) for at in windows[:VIEWS]])
            yield 150
            d_raw.append(soft_back(probs, d_probs))
            d_packed[side].append(d_values)
            yield 100
        for side in both:
            d_query = joined([mm(d_raw[side][at], qkv[side][at, C : 2 * C]) for at in windows[:VIEWS]])
            d_keys = joined([mm_tn(d_raw[side][at], qkv[side][at, :C]) for at in windows[:VIEWS]])
            d_packed[side] = jnp.concatenate([d_query, d_keys] + d_packed[side], -1).astype(BF16)
            yield 150
        for side in both:
            d_packs[step, places[side], :] = d_packed[side]
            d_firsts[step, places[side], :] = d1[side]
            yield 50
        g_sq[...] += mm_tn(no_a[step], joined(d_packed))
        yield 200

    def chain(*threads):
        for thread in threads:
            yield from thread

    grads = (g_sq, g_so, g_cq, g_co, g_fi, w_fo, g_rf)

    def ship(*chosen):
        bits = bits_of(parts)
        half_rows = rows_of(parts) // 2
        for ref, blocks, before in zip(grads, BLOCKS, (sum(BLOCKS[:i]) for i in range(len(BLOCKS)))):
            if not any(ref is one for one in chosen):
                continue
            for apart in range(parts):
                shard = me ^ apart
                slot = sum(((apart >> bit) & 1) << (bits - 1 - bit) for bit in range(bits))
                dest = (keep_out, send_out)[slot // (parts // 2)].at[slot % (parts // 2)]
                for block in range(blocks):
                    if ref is w_fo:
                        spot = pl.ds(pl.multiple_of(shard * (blocks * rows) + block * rows, 16), rows)
                        value = ref[spot, :]
                    else:
                        spot = pl.ds(pl.multiple_of(shard * rows, 16), rows)
                        value = ref[spot, block * C : (block + 1) * C].astype(BF16)
                    for start in range(0, rows, 16):
                        which, offset = divmod((before + block) * rows + start, half_rows)
                        spot = pl.ds(pl.multiple_of((side_of_rows ^ which) * half_rows + offset, 16), 16)
                        dest[spot, :] = value[start : start + 16]
                yield 40

    def turn_back():
        for block in range(FFH // C):
            w_fo[block * C : (block + 1) * C, :] = g_fo[:, block * C : (block + 1) * C].T.astype(BF16)
            yield 30

    def whole_of(thread, total):
        return paced(thread, 1.0 / total)

    def attends(scene):
        return [whole_of(attend(scene, half, side), 4200) for half in range(2) for side in range(2)]

    def feeds(scene):
        return whole_of(chain(feed(scene, 0), feed(scene, 1)), 2200)

    def backs(*which):
        return [whole_of(back(*one), 5400) for one in which]

    merge(*attends(0), *attends(1), apart=0.02)
    merge(feeds(0), feeds(1))
    merge(whole_of(head(0), 7600), whole_of(head(1), 7600), apart=0.05)
    merge(*backs((0, 0), (0, 1), (1, 0), (1, 1)), whole_of(ship(g_rf), 160), apart=0.02)
    merge(chain(turn_back(), ship(w_fo)), ship(g_sq, g_so, g_cq, g_co, g_fi))


VMEM = pl.BlockSpec(memory_space=pltpu.VMEM)
HBM = pl.BlockSpec(memory_space=pltpu.HBM)
SMEM = pl.BlockSpec(memory_space=pltpu.SMEM)


def exchange(value, fsdp_mask, dp_mask):
    parts = lax.axis_size("fsdp")
    count = parts * lax.axis_size("dp")
    mask = dp_mask * parts + fsdp_mask
    return lax.ppermute(value, ("dp", "fsdp"), [(i, i ^ mask) for i in range(count)])


def local(
    features,
    view_count,
    plane_offsets,
    depth_grad,
    gain_self,
    self_qkv,
    self_out,
    gain_cross,
    cross_qkv,
    cross_out,
    gain_ff,
    ff_in,
    ff_out,
    refine,
):
    parts = lax.axis_size("fsdp")
    copies = lax.axis_size("dp")
    scenes = features.shape[0]
    rows = C // parts
    shard_rows = rows_of(parts)
    small = pltpu.CompilerParams(vmem_limit_bytes=8 * MIB)

    pack = pl.pallas_call(
        functools.partial(pack_kernel, parts),
        out_shape=jax.ShapeDtypeStruct((sum(BLOCKS) * rows + GAIN_ROWS, C), BF16),
        in_specs=[HBM] * 10,
        out_specs=VMEM,
        scratch_shapes=[pltpu.VMEM((3, 1, rows), BF16), pltpu.SemaphoreType.DMA((3 + sum(BLOCKS),))],
        compiler_params=pltpu.CompilerParams(vmem_limit_bytes=8 * MIB),
        name="pack",
    )
    own = [gain.reshape(1, rows) for gain in (gain_self, gain_cross, gain_ff)]
    own += [self_qkv, self_out, cross_qkv, cross_out, ff_in, ff_out, refine]
    shard = pack(*[pltpu.with_memory_space_constraint(one, pltpu.HBM) for one in own])
    steps = scenes * (HV // WIN)
    span = 2 * TOK
    start = pl.pallas_call(
        functools.partial(start_kernel, scenes),
        out_shape=(
            jax.ShapeDtypeStruct((scenes, 8, C), jnp.int32),
            jax.ShapeDtypeStruct((scenes, TOK, TOK), F32),
        )
        + (jax.ShapeDtypeStruct((steps, span, C), F32),) * 3
        + (
            jax.ShapeDtypeStruct(shard.shape, BF16),
            jax.ShapeDtypeStruct((scenes, 2, VIEWS, 2 * C, C), BF16),
            jax.ShapeDtypeStruct((scenes, VIEWS, PIX, C), F32),
        ),
        in_specs=[SMEM] + [VMEM] * 4,
        out_specs=(VMEM,) * 8,
        compiler_params=small,
        cost_estimate=pl.CostEstimate(flops=10 * features.size, bytes_accessed=14 * features.size, transcendentals=0),
        name="start",
    )
    hbm = [pltpu.with_memory_space_constraint(one, pltpu.HBM) for one in (features, plane_offsets, depth_grad)]
    began = start(view_count, hbm[0], shard, hbm[1], hbm[2])

    packed = {0: shard}
    for bit in reversed(range(bits_of(parts))):
        came = {apart | (1 << bit): exchange(piece, 1 << bit, 0) for apart, piece in packed.items()}
        if len(packed) == 1:
            came, began = lax.optimization_barrier((came, began))
        packed |= came
    packed = [packed[apart] for apart in range(parts)]

    scratch = [
        ((C, 3 * C), BF16), ((C, C), BF16), ((C, 3 * C), BF16), ((C, C), BF16),
        ((C, FFH), BF16), ((FFH, C), BF16), ((C, 9 * PLANES), BF16),
        ((C, C), BF16), ((3 * C, C), BF16), ((C, C), BF16),
        ((FFH, C), BF16), ((C, FFH), BF16), ((12 * PLANES, 2 * C), BF16), ((12 * PLANES, 2 * C), BF16),
        ((steps, span, C), F32),
    ]
    scratch += [((steps, span, C), F32)] * 4
    scratch += [((steps, span, C), BF16)] * 3
    scratch += [
        ((steps, span, 3 * C), BF16), ((steps, span, 3 * C), BF16),
        ((steps, span, WIN * WIN), BF16), ((steps, span, TOK), BF16),
        ((steps, span, C), BF16), ((steps, span, C), BF16),
        ((steps, span, FFH), F32), ((steps, span, FFH), BF16),
        ((scenes, VIEWS, 2, WIN, 2, WIN, C), F32), ((scenes, VIEWS, 2, WIN, 2, WIN, C), F32),
        ((scenes, VIEWS, PIX, C), BF16), ((scenes, VIEWS, PIX, C), BF16),
        ((scenes, 2, VIEWS, PIX + 16, C), F32),
        ((scenes, VIEWS, PIX + 2 * HV, 3 * C), BF16), ((scenes, VIEWS, PIX + 2 * HV, 3 * C), BF16),
        ((4 * HV, C), F32), ((HALF, HALF), F32), ((HALF, HALF), BF16),
        ((C, 3 * C), F32), ((C, C), F32), ((C, 3 * C), F32), ((C, C), F32),
        ((C, FFH), F32), ((C, FFH), F32), ((C, 9 * PLANES), F32),
    ]
    main = pl.pallas_call(
        functools.partial(main_kernel, scenes, parts),
        out_shape=(
            jax.ShapeDtypeStruct((scenes, VIEWS, PIX), F32),
            jax.ShapeDtypeStruct((steps, span, 3 * C), BF16),
            jax.ShapeDtypeStruct((steps, span, C), F32),
            jax.ShapeDtypeStruct((3 * C, C), BF16),
            jax.ShapeDtypeStruct((8, C), F32),
            jax.ShapeDtypeStruct((parts // 2, shard_rows, C), BF16),
            jax.ShapeDtypeStruct((parts // 2, shard_rows, C), BF16),
        ),
        in_specs=[VMEM] * (7 + parts),
        out_specs=(VMEM,) * 7,
        scratch_shapes=[pltpu.VMEM(shape, kind) for shape, kind in scratch],
        compiler_params=pltpu.CompilerParams(vmem_limit_bytes=43 * MIB),
        name="layer",
    )
    lives, bias, x0s, xhats, rstds, packed[0], hots, incoming = began
    depth, d_packs, d_firsts, turned, gains, keep, send = main(
        lives, bias, x0s, xhats, rstds, hots, incoming, *packed
    )

    finish = pl.pallas_call(
        functools.partial(finish_kernel, scenes),
        out_shape=jax.ShapeDtypeStruct((scenes, VIEWS, 2, WIN, 2, WIN, C), F32),
        in_specs=[VMEM] * 6,
        out_specs=VMEM,
        compiler_params=small,
        cost_estimate=pl.CostEstimate(flops=6 * C * features.size, bytes_accessed=16 * features.size, transcendentals=0),
        name="finish",
    )
    grad_features = finish(d_packs, d_firsts, xhats, rstds, turned, gains).reshape(features.shape)

    for bit in range(bits_of(parts) - 1):
        middle = keep.shape[0] // 2
        onward = keep[middle:] + exchange(send[middle:], 1 << bit, 0)
        keep, send = keep[:middle] + exchange(send[:middle], 1 << bit, 0), onward
    last = parts // 2
    half = shard_rows // 2
    beside = exchange(send[0, :half], last, 0)
    across = exchange(keep[0, half:], 0, 1)
    corner = exchange(send[0, half:], last, 1)
    grads = (keep[0, :half].astype(F32) + beside) + (across.astype(F32) + corner)
    grads = grads.astype(BF16)
    for bit in reversed(range(2, bits_of(copies))):
        grads = grads + exchange(grads, 0, 1 << bit)
    if bits_of(copies) > 1:
        along = exchange(grads, 0, 2)
        swapped = exchange(grads, 0, 1)
        corner = exchange(grads, 0, 3)
        mine, other = (grads, along), (swapped, corner)
    else:
        mine, other = (grads,), (exchange(grads, 0, 1),)

    unpack = pl.pallas_call(
        functools.partial(unpack_kernel, parts),
        out_shape=tuple(jax.ShapeDtypeStruct((1, rows), F32) for _ in range(3))
        + tuple(
            jax.ShapeDtypeStruct(piece.shape, F32)
            for piece in (self_qkv, self_out, cross_qkv, cross_out, ff_in, ff_out, refine)
        ),
        in_specs=[VMEM] * (2 + 2 * len(mine)),
        out_specs=(VMEM,) * 10,
        scratch_shapes=[pltpu.VMEM((shard_rows, C), F32)],
        compiler_params=small,
        name="unpack",
    )
    ga, gb, gc, d_sq, d_so, d_cq, d_co, d_fi, d_fo, d_rf = unpack(
        gains, packed[0], *mine, *other
    )
    return (
        depth * (jnp.arange(VIEWS) < view_count[:, None])[:, :, None],
        grad_features,
        ga.reshape(rows),
        d_sq,
        d_so,
        gb.reshape(rows),
        d_cq,
        d_co,
        gc.reshape(rows),
        d_fi,
        d_fo,
        d_rf,
    )


def solution(mesh):
    placed = (
        P(("dp", "fsdp"), None, None, None),
        P(("dp", "fsdp")),
        P(("dp", "fsdp"), None, None),
        P(("dp", "fsdp"), None, None),
        P("fsdp"),
        P("fsdp", None),
        P("fsdp", None),
        P("fsdp"),
        P("fsdp", None),
        P("fsdp", None),
        P("fsdp"),
        P("fsdp", None),
        P("fsdp", None),
        P("fsdp", None),
    )
    return jax.shard_map(
        local,
        mesh=mesh,
        in_specs=placed,
        out_specs=(
            P(("dp", "fsdp"), None, None),
            P(("dp", "fsdp"), None, None, None),
            P("fsdp"),
            P("fsdp", None),
            P("fsdp", None),
            P("fsdp"),
            P("fsdp", None),
            P("fsdp", None),
            P("fsdp"),
            P("fsdp", None),
            P("fsdp", None),
            P("fsdp", None),
        ),
        check_vma=False,
    )
```
